32 devices in a mesh: seq: 4 (over y, x), exp: 8 (over z, core).
Axes of the slice: x: 2, y: 2, z: 4, core: 2. Of those that a mesh axis runs over, the one named last changes fastest.
Arguments:
- tokens: bfloat16 [16, 1024, 768], P('exp', 'seq'), may hold values from -6 to 6
- lengths: int32 [16], P('exp'), may hold values from 128 to 1024, as said below
- routes: int32 [16, 1024, 1], P('exp', 'seq'), may hold values from 0 to 7
- bucket_table: int32 [2047], replicated, may hold values from 0 to 31
- gain_one: float32 [768], replicated, may hold values from 0.5 to 1.5
- w_query: bfloat16 [768, 768], replicated, may hold values from -0.21875 to 0.21875
- w_key: bfloat16 [768, 768], replicated, may hold values from -0.21875 to 0.21875
- w_value: bfloat16 [768, 768], replicated, may hold values from -0.21875 to 0.21875
- w_output: bfloat16 [768, 768], replicated, may hold values from -1.75 to 1.75
- rel_bias: float32 [32, 12], replicated, may hold values from -6 to 6
- gain_two: float32 [768], replicated, may hold values from 0.5 to 1.5
- w_router: bfloat16 [768, 8], replicated, may hold values from -0.15625 to 0.15625
- w_in: bfloat16 [8, 768, 3072], P('exp'), may hold values from -0.21875 to 0.21875
- w_out: bfloat16 [8, 3072, 768], P('exp'), may hold values from -0.109375 to 0.109375
- cotangent: bfloat16 [16, 1024, 768], P('exp', 'seq'), may hold values from -6 to 6
Outputs:
- mixed: bfloat16 [16, 1024, 768], P('exp', 'seq')
- grad_tokens: float32 [16, 1024, 768], P('exp', 'seq')
- grad_gain_one: float32 [768], replicated
- grad_query: float32 [768, 768], replicated
- grad_key: float32 [768, 768], replicated
- grad_value: float32 [768, 768], replicated
- grad_output: float32 [768, 768], replicated
- grad_rel_bias: float32 [32, 12], replicated
- grad_gain_two: float32 [768], replicated
- grad_router: float32 [768, 8], replicated
- grad_in: float32 [8, 768, 3072], P('exp', None, 'seq')
- grad_out: float32 [8, 3072, 768], P('exp', 'seq')
The draws below stay inside these ranges and needn't reach their ends.
Inputs may be any that keep to these rules, and one draw needn't show every extreme that they name: `lengths`: in each aligned block of 2 sequences, one has length 1024.
All inputs are finite; a program needn't handle non-finite values.
Results may differ from the reference program's by a relative error of at most 0.015.
Values may be sent and summed in bfloat16 or wider, within the bound.
No kernel may reach another device: no remote copies, remote signals or barrier semaphores. Data moves between devices by JAX's collectives and lax.ppermute only.
A program may use at most 256 MiB of HBM per device.

```python
import jax
import jax.numpy as jnp
from jax import lax

D = 768
HEADS = 12
HEAD_DIM = 64
FF = 3072
BUCKETS = 32
LENGTH = 1024
SEQS_DEV = 2
EXPERTS = 8
BLOCK = 256
SEQS = 16
CAP = 80
N_SEQ = 4
N_EXP = 8


def draw_lengths(key, part):
    key = jax.random.fold_in(key, 11)
    first_key, second_key = jax.random.split(key)
    shortest = max(LENGTH // 8, 1)
    drawn = jax.random.randint(first_key, (SEQS,), shortest, LENGTH + 1)
    chosen = jax.random.randint(second_key, (SEQS // SEQS_DEV,), 0, SEQS_DEV)
    full_mark = (jnp.arange(SEQS_DEV)[None, :] == chosen[:, None]).reshape(-1)
    return jnp.where(full_mark, LENGTH, drawn).astype(jnp.int32)


def set_ends(entries, key, least, top_value):
    longest = entries.shape.index(max(entries.shape))
    spots = []
    for shift in (0, 1):
        where = [jax.random.randint(jax.random.fold_in(key, axis), (), 0, length) for axis, length in enumerate(entries.shape)]
        where[longest] = (where[longest] + shift) % entries.shape[longest]
        spots.append(tuple(where))
    return entries.at[spots[0]].set(least).at[spots[1]].set(top_value)


def levels(own_key, shape, cuts, smallest, largest):
    level, own = 1.0, jax.random.fold_in(own_key, 6)
    for dim, shards_of in cuts:
        steps = jnp.exp(jax.random.uniform(jax.random.fold_in(own, dim), (shards_of,), jnp.float32, smallest / len(cuts), largest / len(cuts)))
        level = level * jnp.repeat(steps, shape[dim] // shards_of).reshape([-1 if axis == dim else 1 for axis in range(len(shape))])
    return level


def distinct(own_key, rows, number_of, top, lift):
    order = jax.random.permutation(jax.random.fold_in(own_key, 1), number_of)
    favour = order
    for power in range(3):
        favour = favour * favour // number_of
    favour = favour * lift // number_of
    tickets = jax.random.randint(jax.random.fold_in(own_key, 2), (rows, number_of), 0, 4096) + favour
    fixed_rows = jax.random.permutation(jax.random.fold_in(own_key, 3), rows)[jnp.arange(number_of) % rows]
    tickets = jnp.where(jnp.arange(rows)[:, None] == fixed_rows[None, :], 1 << 14, tickets)
    priority = tickets * number_of + jnp.arange(number_of)
    return lax.top_k(priority.astype(jnp.int32), top)[1].astype(jnp.int32)


def centred(stream_key, extent, width, limit, shards=(), kind=jnp.bfloat16):
    level = levels(stream_key, extent, shards, -0.22, 0.18) if shards else 1.0
    array = jax.random.normal(stream_key, extent, jnp.float32) * width * level
    return jnp.minimum(jnp.maximum(array, -limit), limit).astype(kind)


def setup_inputs(seed: int = 0) -> dict:
    keys = jax.random.split(jax.random.key(seed), 16)
    return {
        "tokens": centred(keys[0], (SEQS, LENGTH, D), 1.0, 6.0, ((0, 8), (1, 4))),
        "lengths": draw_lengths(jax.random.fold_in(keys[15], 71), 0),
        "routes": distinct(keys[2], SEQS * LENGTH, EXPERTS, 1, 1024).reshape((SEQS, LENGTH, 1)),
        "bucket_table": set_ends(jax.random.randint(keys[3], (2 * LENGTH - 1,), 0, BUCKETS), jax.random.fold_in(keys[3], 1), 0, BUCKETS - 1).astype(jnp.int32),
        "gain_one": jnp.clip(1.0 + 0.1 * jax.random.normal(keys[4], (D,), jnp.float32), 0.5, 1.5),
        "w_query": centred(keys[5], (D, D), D ** -0.5, 0.21875),
        "w_key": centred(keys[6], (D, D), D ** -0.5, 0.21875),
        "w_value": centred(keys[7], (D, D), D ** -0.5, 0.21875),
        "w_output": centred(keys[8], (D, D), (max(D // 64, 2)) ** -0.5, 1.75),
        "rel_bias": centred(keys[9], (BUCKETS, HEADS), 1.0, 6.0, (), jnp.float32),
        "gain_two": jnp.clip(1.0 + 0.1 * jax.random.normal(keys[10], (D,), jnp.float32), 0.5, 1.5),
        "w_router": centred(keys[11], (D, EXPERTS), (2 * D) ** -0.5, 0.15625),
        "w_in": centred(keys[12], (EXPERTS, D, FF), D ** -0.5, 0.21875, ((0, 8),)),
        "w_out": centred(keys[13], (EXPERTS, FF, D), FF ** -0.5, 0.109375, ((0, 8),)),
        "cotangent": centred(keys[14], (SEQS, LENGTH, D), 1.0, 6.0, ((0, 8), (1, 4))),
    }


EPS = 1e-06
NEG = -1e+30
HIGH_PRECISION = lax.Precision.HIGHEST

@jax.custom_vjp
def reduced_cast(v):
    return lax.optimization_barrier(v.astype(jnp.bfloat16)).astype(jnp.float32)

@jax.custom_vjp
def reduced_cast_backward(v):
    return v

def low_keep(v):
    return (reduced_cast(v), None)

def low_pass(kept, grad):
    return (grad,)

def back_keep(v):
    return (v, None)

def back_low(kept, grad):
    return (reduced_cast(grad),)
reduced_cast.defvjp(low_keep, low_pass)
reduced_cast_backward.defvjp(back_keep, back_low)

def rms_norm(values_in, gain):
    return values_in * lax.rsqrt(lax.optimization_barrier(jnp.mean(values_in * values_in, axis=-1, keepdims=True)) + EPS) * gain

def to_groups(source):
    shaped = source.reshape((N_EXP, SEQS_DEV, N_SEQ, BLOCK) + source.shape[2:])
    return jnp.swapaxes(shaped, 1, 2).reshape((N_EXP * N_SEQ, SEQS_DEV * BLOCK) + source.shape[2:])

def from_groups(source):
    shaped = source.reshape((N_EXP, N_SEQ, SEQS_DEV, BLOCK) + source.shape[2:])
    return jnp.swapaxes(shaped, 1, 2).reshape((SEQS, LENGTH) + source.shape[2:])

def reference(tokens, lengths, routes, bucket_table, gain_one, w_query, w_key, w_value, w_output, rel_bias, gain_two, w_router, w_in, w_out, cotangent):
    score_scale = HEAD_DIM ** (-0.5)
    places = jnp.arange(LENGTH, dtype=jnp.int32)
    present = (places[None, :] < lengths[:, None]).astype(jnp.float32)
    routed = routes[:, :, 0]
    route_groups = to_groups(routed)
    present_groups = to_groups(present)
    expert_ids = jnp.arange(EXPERTS, dtype=jnp.int32)
    live_hits = ((route_groups[:, :, None] == expert_ids[None, None, :]) & (present_groups[:, :, None] > 0)).astype(jnp.int32)
    running = jnp.cumsum(live_hits, axis=1)
    slot_index = lax.optimization_barrier(jnp.sum(live_hits * (running - 1), axis=-1))
    kept_groups = (present_groups > 0) & (slot_index < CAP)
    group_ids = jnp.arange(N_EXP * N_SEQ, dtype=jnp.int32)[:, None]
    slots_all = EXPERTS * N_SEQ * N_EXP * CAP
    destin = ((route_groups * N_SEQ + group_ids % N_SEQ) * N_EXP + group_ids // N_SEQ) * CAP + slot_index
    destin = jnp.where(kept_groups, destin, slots_all).reshape(-1)
    kept = from_groups(kept_groups.astype(jnp.float32))
    chosen = (routed[:, :, None] == expert_ids[None, None, :]).astype(jnp.float32)
    offsets = places[None, :] - places[:, None] + LENGTH - 1

    def forward(layer_inputs, query_w, key_w, value_w, output_weight, bias_table, gain_a, gain_b, router_weight, first_w, second_w):
        normalized_rows = reduced_cast(rms_norm(layer_inputs, gain_a))

        def project(weight_matrix):
            return reduced_cast_backward(reduced_cast(jnp.einsum('hkw,wa->hka', normalized_rows, weight_matrix, precision=HIGH_PRECISION)))
        queries, keys_all, values_all = (project(query_w), project(key_w), project(value_w))
        bias = jnp.transpose(bias_table[bucket_table][offsets], (2, 0, 1))

        def attend(pieces):
            query_seq, key_seq, value_seq, key_mask = pieces
            query_heads = query_seq.reshape(LENGTH, HEADS, HEAD_DIM)
            key_heads = key_seq.reshape(LENGTH, HEADS, HEAD_DIM)
            value_heads = value_seq.reshape(LENGTH, HEADS, HEAD_DIM)
            scores = jnp.einsum('ihd,jhd->hij', query_heads, key_heads, precision=HIGH_PRECISION) * score_scale + bias
            scores = jnp.where(key_mask[None, None, :] > 0, scores, NEG)
            probs = jax.nn.softmax(reduced_cast_backward(scores), axis=-1)
            result = jnp.einsum('hij,jhd->ihd', reduced_cast(probs), value_heads, precision=HIGH_PRECISION)
            return reduced_cast_backward(reduced_cast(result.reshape(LENGTH, D)))
        attention_output = lax.map(jax.checkpoint(attend), (queries, keys_all, values_all, present))
        residual_after_attention = layer_inputs + reduced_cast_backward(jnp.einsum('hkw,wa->hka', attention_output, output_weight, precision=HIGH_PRECISION))
        routed_input = reduced_cast(rms_norm(residual_after_attention, gain_b))
        router_logits = reduced_cast_backward(jnp.einsum('hkw,wa->hka', routed_input, router_weight, precision=HIGH_PRECISION))
        gate_value = EXPERTS * lax.optimization_barrier(jnp.sum(jax.nn.softmax(router_logits, axis=-1) * chosen, axis=-1))
        flat_rows = to_groups(routed_input).reshape(-1, D)
        buffer = jnp.zeros((slots_all + 1, D), jnp.float32).at[destin].add(flat_rows)[:slots_all]
        expert_rows = reduced_cast_backward(buffer).reshape(EXPERTS, N_SEQ * N_EXP * CAP, D)
        pre_act = reduced_cast_backward(jnp.einsum('erd,edf->erf', expert_rows, first_w, precision=HIGH_PRECISION))
        hidden = reduced_cast(jax.nn.gelu(pre_act, approximate=True))
        expert_out = reduced_cast_backward(reduced_cast(jnp.einsum('erf,efd->erd', hidden, second_w, precision=HIGH_PRECISION)))
        padded = jnp.concatenate([expert_out.reshape(slots_all, D), jnp.zeros((1, D), jnp.float32)], axis=0)
        returned = from_groups(padded[destin].reshape(N_EXP * N_SEQ, SEQS_DEV * BLOCK, D))
        return present[:, :, None] * (residual_after_attention + (gate_value * kept)[:, :, None] * returned)
    floats = (tokens, w_query, w_key, w_value, w_output, rel_bias, gain_one, gain_two, w_router, w_in, w_out)
    arrays = tuple((item.astype(jnp.float32) for item in floats))
    mixed, pull = jax.vjp(forward, *arrays)
    grads = pull(cotangent.astype(jnp.float32))
    return (mixed.astype(jnp.bfloat16), grads[0], grads[6], grads[1], grads[2], grads[3], grads[4], grads[5], grads[7], grads[8], grads[9], grads[10])
```

```python
import functools

import jax
import jax.numpy as jnp
from jax import lax
from jax.experimental import pallas as pl
from jax.experimental.pallas import tpu as pltpu
from jax.sharding import PartitionSpec as P

EPS = 1e-06
NEG = -1e30
HIGH_PRECISION = lax.Precision.HIGHEST
LANES = 128
VMEM_BYTES = 48 * 1024 * 1024
BF = jnp.bfloat16
F32 = jnp.float32


def matmul_f32(left, right):
    return jnp.dot(left, right, preferred_element_type=F32)


def dot_dims(left, right, left_dim, right_dim):
    return lax.dot_general(
        left, right, (((left_dim,), (right_dim,)), ((), ())), preferred_element_type=F32
    )


def inner_rows(left, right):
    return dot_dims(left, right, 0, 0)


def rms_norm(values_in, gain):
    return (
        values_in * lax.rsqrt(jnp.mean(values_in * values_in, axis=-1, keepdims=True) + EPS) * gain
    )


def gelu_tanh(values_in):
    return jax.nn.gelu(values_in, approximate=True)


def swap(value, bit):
    ways = lax.axis_size("seq")
    return lax.ppermute(value, "seq", [(i, i ^ bit) for i in range(ways)])


def trade(value, bits):
    peers = lax.axis_size("exp")
    return lax.ppermute(value, "exp", [(i, i ^ bits) for i in range(peers)])


def gather_pieces(value, rows):
    px, py = swap(value, 1), swap(value, 2)
    return px, py, swap(px[:rows], 2), swap(py[rows:], 1)


def base_kernel(row_ref, base_ref):
    row = row_ref[0]
    wide = jnp.broadcast_to(row, (LANES, row.shape[1]))
    base_ref[0] = pltpu.roll(wide, 0, 1, stride=1, stride_axis=0)


def make_base(bias_rows):
    heads_here, _, wide = bias_rows.shape
    return pl.pallas_call(
        base_kernel,
        grid=(heads_here,),
        in_specs=[pl.BlockSpec((1, 1, wide), lambda h: (h, 0, 0))],
        out_specs=pl.BlockSpec((1, LANES, wide), lambda h: (h, 0, 0)),
        out_shape=jax.ShapeDtypeStruct((heads_here, LANES, wide), F32),
    )(bias_rows)


def forward_kernel(
    heads_here,
    head_dim,
    scale,
    info_ref,
    own_ref,
    px_ref,
    py_ref,
    pd_ref,
    weight_ref,
    base_ref,
    out_ref,
    probs_ref,
    q_ref,
    k_ref,
    v_ref,
    rows_ref,
    k_rows,
    v_cols,
    mask_col,
):
    me, length = info_ref[0], info_ref[1]
    head = pl.program_id(0)
    span = rows_ref.shape[0]
    block_len = own_ref.shape[0]
    group = heads_here * head_dim
    tiles = span // LANES

    @pl.when(head == 0)
    def _():
        for step, piece in enumerate((own_ref, px_ref, py_ref, pd_ref)):
            start = pl.multiple_of((me ^ step) * block_len, block_len)
            rows_ref[pl.ds(start, block_len), :] = piece[...]
        rows = rows_ref[...]
        weights = weight_ref[...].reshape(3 * group, weight_ref.shape[2])
        cols = dot_dims(weights, rows, 1, 1).astype(BF)
        k_all = dot_dims(rows, weight_ref[1], 1, 1).astype(BF)
        v_all = dot_dims(rows, weight_ref[2], 1, 1).astype(BF)
        for h in range(heads_here):
            lo, hi = h * head_dim, (h + 1) * head_dim
            q_ref[h] = (cols[lo:hi].astype(F32) * scale).astype(BF)
            k_ref[h] = cols[group + lo : group + hi]
            v_cols[h] = cols[2 * group + lo : 2 * group + hi]
            k_rows[h] = k_all[:, lo:hi]
            v_ref[h] = v_all[:, lo:hi]
        places = lax.broadcasted_iota(jnp.int32, mask_col.shape, 0)
        mask_col[...] = jnp.where(places < length, 0.0, NEG)

    key_rows = k_rows[head]
    value_cols = v_cols[head]
    mask = jnp.concatenate([mask_col[...]] * (block_len // LANES), axis=1)
    for c in range(span // block_len):
        cols = slice(c * block_len, (c + 1) * block_len)
        first = c * block_len // LANES + tiles - 1
        scores = dot_dims(key_rows, q_ref[head, :, cols], 1, 0) + mask
        bias = jnp.concatenate(
            [
                base_ref[0, :, (first - a) * LANES : (first - a) * LANES + block_len]
                for a in range(tiles)
            ],
            axis=0,
        )
        scores = scores + bias
        top = jnp.max(scores, axis=0, keepdims=True)
        powers = jnp.exp(scores - top)
        total = jnp.sum(powers, axis=0, keepdims=True)
        probs = (powers * (1.0 / total)).astype(BF)
        probs_ref[0, :, cols] = probs
        out_ref[me ^ c] = dot_dims(value_cols, probs, 1, 0).astype(BF)


def attention_forward(info, own, px, py, diag, seq_id, weights, base):
    _, block_len, width = own.shape
    _, group, _ = weights.shape
    heads_here, _, wide = base.shape
    head_dim = group // heads_here
    span = 4 * block_len
    piece = pl.BlockSpec((None, block_len, width), lambda h, _: (seq_id, 0, 0))
    full = lambda *shape: pl.BlockSpec(shape, lambda h, _: (0,) * len(shape))
    out_shape = (
        jax.ShapeDtypeStruct((4, group, block_len), BF),
        jax.ShapeDtypeStruct((heads_here, span, span), BF),
        jax.ShapeDtypeStruct((heads_here, head_dim, span), BF),
        jax.ShapeDtypeStruct((heads_here, head_dim, span), BF),
        jax.ShapeDtypeStruct((heads_here, span, head_dim), BF),
        jax.ShapeDtypeStruct((span, width), BF),
    )
    return pl.pallas_call(
        functools.partial(forward_kernel, heads_here, head_dim, head_dim ** (-0.5)),
        grid_spec=pltpu.PrefetchScalarGridSpec(
            num_scalar_prefetch=1,
            grid=(heads_here,),
            in_specs=[
                piece,
                piece,
                piece,
                full(block_len, width),
                full(3, group, width),
                pl.BlockSpec((1, LANES, wide), lambda h, _: (h, 0, 0)),
            ],
            out_specs=(
                pl.BlockSpec((4, head_dim, block_len), lambda h, _: (0, h, 0)),
                pl.BlockSpec((1, span, span), lambda h, _: (h, 0, 0)),
                full(heads_here, head_dim, span),
                full(heads_here, head_dim, span),
                full(heads_here, span, head_dim),
                full(span, width),
            ),
            scratch_shapes=[
                pltpu.VMEM((heads_here, span, head_dim), BF),
                pltpu.VMEM((heads_here, head_dim, span), BF),
                pltpu.VMEM((span, LANES), F32),
            ],
        ),
        out_shape=out_shape,
        compiler_params=pltpu.CompilerParams(vmem_limit_bytes=VMEM_BYTES),
        cost_estimate=pl.CostEstimate(
            flops=6 * heads_here * span * span * 256 * 2,
            bytes_accessed=heads_here * span * span * 2,
            transcendentals=heads_here * span * span,
        ),
        name="attention_forward",
    )(info, own, px, py, diag, weights, base)


def backward_kernel(
    scale,
    info_ref,
    g0_ref,
    g1_ref,
    g2_ref,
    g3_ref,
    probs_ref,
    q_ref,
    k_ref,
    v_ref,
    rows_ref,
    out_ref,
    weight_ref,
    rel_ref,
    grad_cols,
    rel_sum,
    dq_cols,
):
    me = info_ref[0]
    head_dim, span = q_ref.shape[1], q_ref.shape[2]
    block_len = g0_ref.shape[1]
    tiles = span // LANES
    for step, piece in enumerate((g0_ref, g1_ref, g2_ref, g3_ref)):
        start = pl.multiple_of((me ^ step) * block_len, block_len)
        grad_cols[:, pl.ds(start, block_len)] = piece[...]
    rel_sum[...] = jnp.zeros_like(rel_sum)
    values, keys = v_ref[0], k_ref[0]
    dk = jnp.zeros((head_dim, span), F32)
    dv = jnp.zeros((head_dim, span), F32)
    for c in range(span // block_len):
        cols = slice(c * block_len, (c + 1) * block_len)
        first = c * block_len // LANES + tiles - 1
        grads = grad_cols[:, cols]
        low = probs_ref[0, :, cols]
        probs = low.astype(F32)
        grad_probs = dot_dims(values, grads, 1, 0)
        weighted = probs * grad_probs
        inner = jnp.sum(weighted, axis=0, keepdims=True)
        grad_scores = weighted - probs * inner
        for a in range(tiles):
            spot = slice((first - a) * LANES, (first - a) * LANES + block_len)
            rel_sum[:, spot] += grad_scores[a * LANES : (a + 1) * LANES]
        grad_low = grad_scores.astype(BF)
        dv = dv + dot_dims(grads, low, 1, 1)
        dk = dk + dot_dims(q_ref[0, :, cols], grad_low, 1, 1)
        dq = (dot_dims(keys, grad_low, 1, 0) * scale).astype(BF)
        dq_cols[:, cols] = dq
        out_ref[me ^ c, 0] = dq
    dk, dv = dk.astype(BF), dv.astype(BF)
    for c in range(span // block_len):
        cols = slice(c * block_len, (c + 1) * block_len)
        out_ref[me ^ c, 1] = dk[:, cols]
        out_ref[me ^ c, 2] = dv[:, cols]
    rows = rows_ref[...]
    weight_ref[0] = matmul_f32(dq_cols[...], rows)
    weight_ref[1] = matmul_f32(dk, rows)
    weight_ref[2] = matmul_f32(dv, rows)
    fold = rel_sum[...]
    wide = fold.shape[1]
    half = LANES // 2
    while half >= 1:
        fold = fold[:half] + pltpu.roll(fold[half:], wide - half, 1)
        half //= 2
    rel_ref[0] = fold


def attention_backward(info, pieces, probs, q, k, v, rows):
    heads_here, head_dim, span = q.shape
    width = rows.shape[1]
    group = heads_here * head_dim
    block_len = span // 4
    wide = 2 * span
    piece = pl.BlockSpec((head_dim, block_len), lambda h, _: (h, 0))
    per_head = lambda *shape: pl.BlockSpec((1,) + shape, lambda h, _: (h,) + (0,) * len(shape))
    return pl.pallas_call(
        functools.partial(backward_kernel, head_dim ** (-0.5)),
        grid_spec=pltpu.PrefetchScalarGridSpec(
            num_scalar_prefetch=1,
            grid=(heads_here,),
            in_specs=[piece] * 4
            + [
                per_head(span, span),
                per_head(head_dim, span),
                per_head(head_dim, span),
                per_head(span, head_dim),
                pl.BlockSpec((span, width), lambda h, _: (0, 0)),
            ],
            out_specs=(
                pl.BlockSpec((4, 3, head_dim, block_len), lambda h, _: (0, 0, h, 0)),
                pl.BlockSpec((3, head_dim, width), lambda h, _: (0, h, 0)),
                pl.BlockSpec((1, 1, wide), lambda h, _: (h, 0, 0)),
            ),
            scratch_shapes=[
                pltpu.VMEM((head_dim, span), BF),
                pltpu.VMEM((LANES, wide), F32),
                pltpu.VMEM((head_dim, span), BF),
            ],
        ),
        out_shape=(
            jax.ShapeDtypeStruct((4, 3, group, block_len), BF),
            jax.ShapeDtypeStruct((3, group, width), F32),
            jax.ShapeDtypeStruct((heads_here, 1, wide), F32),
        ),
        compiler_params=pltpu.CompilerParams(vmem_limit_bytes=VMEM_BYTES),
        cost_estimate=pl.CostEstimate(
            flops=8 * heads_here * span * span * 256 * 2,
            bytes_accessed=heads_here * span * span * 2,
            transcendentals=0,
        ),
        name="attention_backward",
    )(info, *pieces, probs, q, k, v, rows)


def expert_kernel(
    experts,
    counts,
    mine_ref,
    *refs,
):
    pieces = len(counts)
    row_refs, grad_refs = refs[:pieces], refs[pieces : 2 * pieces]
    router_ref, first_ref, second_ref = refs[2 * pieces : 2 * pieces + 3]
    refs = refs[2 * pieces + 3 :]
    back_refs, mixed_refs = refs[:pieces], refs[pieces : 2 * pieces]
    hidden_ref, pre_ref, rows_t_ref, made_t_ref, router_grad_ref = refs[2 * pieces : 2 * pieces + 5]
    rows_all, grads_all, made_all, prob_all, out_sum, back_sum = refs[2 * pieces + 5 :]
    step, steps = pl.program_id(0), pl.num_programs(0)
    lanes = lax.broadcasted_iota(jnp.int32, prob_all.shape, 1)
    is_mine = lanes == mine_ref[0]

    @pl.when(step == 0)
    def _():
        start = 0
        for piece in range(pieces):
            rows_all[start : start + counts[piece], :] = row_refs[piece][...]
            grads_all[start : start + counts[piece], :] = grad_refs[piece][...]
            start += counts[piece]
        logits = matmul_f32(rows_all[...], router_ref[...])
        logits = jnp.where(lanes < experts, logits, NEG)
        powers = jnp.exp(logits - jnp.max(logits, axis=1, keepdims=True))
        prob = powers / jnp.sum(powers, axis=1, keepdims=True)
        prob_all[...] = prob
        gate = experts * jnp.sum(jnp.where(is_mine, prob, 0.0), axis=1, keepdims=True)
        made_all[...] = (gate * grads_all[...].astype(F32)).astype(BF)
        out_sum[...] = jnp.zeros_like(out_sum)
        back_sum[...] = jnp.zeros_like(back_sum)

    first, second = first_ref[...], second_ref[...]
    pre = matmul_f32(rows_all[...], first)
    grad_hidden = dot_dims(made_all[...], second, 1, 1)
    square = pre * pre
    curve = jnp.tanh(pre * (0.7978845608028654 + 0.035677408136300125 * square))
    half = 0.5 + 0.5 * curve
    hidden = (pre * half).astype(BF)
    slope = half + pre * (0.5 - 0.5 * curve * curve) * (
        0.7978845608028654 + 0.10703222440890037 * square
    )
    grad_pre = (grad_hidden * slope).astype(BF)
    hidden_ref[...] = hidden
    pre_ref[...] = grad_pre
    out_sum[...] += matmul_f32(hidden, second)
    back_sum[...] += dot_dims(grad_pre, first, 1, 1)

    @pl.when(step == steps - 1)
    def _():
        prob = prob_all[...]
        prob_mine = jnp.sum(jnp.where(is_mine, prob, 0.0), axis=1, keepdims=True)
        expert_out = out_sum[...].astype(BF).astype(F32)
        upper = experts * jnp.sum(
            grads_all[...].astype(F32) * expert_out, axis=1, keepdims=True
        )
        inner = prob_mine * upper
        grad_logits = (prob * (jnp.where(is_mine, upper, 0.0) - inner)).astype(BF)
        back = (back_sum[...] + dot_dims(grad_logits, router_ref[...], 1, 1)).astype(BF)
        mixed = (experts * prob_mine * expert_out).astype(BF)
        start = 0
        for piece in range(pieces):
            back_refs[piece][...] = back[start : start + counts[piece]]
            mixed_refs[piece][...] = mixed[start : start + counts[piece]]
            start += counts[piece]
        rows_t_ref[...] = rows_all[...].T
        made_t_ref[...] = made_all[...].T
        router_grad_ref[...] = dot_dims(grad_logits, rows_all[...], 0, 0)


def expert_pass(mine, experts, row_pieces, grad_pieces, router, first, second):
    width, hidden_width = first.shape
    counts = tuple(piece.shape[0] for piece in row_pieces)
    total = sum(counts)
    tile = hidden_width // 6
    whole = lambda *shape: pl.BlockSpec(shape, lambda f, _: (0,) * len(shape))
    piece_specs = [whole(count, width) for count in counts]
    piece_shapes = [jax.ShapeDtypeStruct((count, width), BF) for count in counts]
    return pl.pallas_call(
        functools.partial(expert_kernel, experts, counts),
        grid_spec=pltpu.PrefetchScalarGridSpec(
            num_scalar_prefetch=1,
            grid=(hidden_width // tile,),
            in_specs=piece_specs * 2
            + [
                whole(width, LANES),
                pl.BlockSpec((width, tile), lambda f, _: (0, f)),
                pl.BlockSpec((tile, width), lambda f, _: (f, 0)),
            ],
            out_specs=piece_specs * 2
            + [
                pl.BlockSpec((total, tile), lambda f, _: (0, f)),
                pl.BlockSpec((total, tile), lambda f, _: (0, f)),
                whole(width, total),
                whole(width, total),
                whole(LANES, width),
            ],
            scratch_shapes=[
                pltpu.VMEM((total, width), BF),
                pltpu.VMEM((total, width), BF),
                pltpu.VMEM((total, width), BF),
                pltpu.VMEM((total, LANES), F32),
                pltpu.VMEM((total, width), F32),
                pltpu.VMEM((total, width), F32),
            ],
        ),
        out_shape=piece_shapes * 2
        + [
            jax.ShapeDtypeStruct((total, hidden_width), BF),
            jax.ShapeDtypeStruct((total, hidden_width), BF),
            jax.ShapeDtypeStruct((width, total), BF),
            jax.ShapeDtypeStruct((width, total), BF),
            jax.ShapeDtypeStruct((LANES, width), F32),
        ],
        compiler_params=pltpu.CompilerParams(vmem_limit_bytes=VMEM_BYTES),
        cost_estimate=pl.CostEstimate(
            flops=8 * total * width * hidden_width,
            bytes_accessed=4 * width * hidden_width + 4 * total * hidden_width,
            transcendentals=total * hidden_width,
        ),
        name="expert_pass",
    )(mine, *row_pieces, *grad_pieces, router, first, second)


def chunk_kernel(_, left_ref, right_ref, out_ref):
    out_ref[0] = matmul_f32(left_ref[...], right_ref[...]).astype(BF)


def weight_chunks(picks, left, right, ways):
    width, total = left.shape
    chunk = right.shape[1] // ways
    count = picks.shape[0]
    return pl.pallas_call(
        chunk_kernel,
        grid_spec=pltpu.PrefetchScalarGridSpec(
            num_scalar_prefetch=1,
            grid=(count,),
            in_specs=[
                pl.BlockSpec((width, total), lambda i, picks: (0, 0)),
                pl.BlockSpec((total, chunk), lambda i, picks: (0, picks[i])),
            ],
            out_specs=pl.BlockSpec((1, width, chunk), lambda i, picks: (i, 0, 0)),
        ),
        out_shape=jax.ShapeDtypeStruct((count, width, chunk), BF),
        compiler_params=pltpu.CompilerParams(vmem_limit_bytes=VMEM_BYTES),
        cost_estimate=pl.CostEstimate(
            flops=2 * count * width * total * chunk,
            bytes_accessed=2 * count * (total + width) * chunk,
            transcendentals=0,
        ),
        name="weight_chunks",
    )(picks, left, right)


def final_kernel(rows, info_ref, *refs):
    pieces, halves = refs[:10], refs[10:12]
    query_ref, key_ref, value_ref, output_ref, extra_ref, whole = refs[12:]
    me, core, chip = info_ref[0], info_ref[1], info_ref[2]
    chips = pieces[0].shape[0] // rows
    group3 = 3 * (query_ref.shape[0] // 4)
    group = group3 // 3

    def place(step, other, first, ref):
        for i in range(ref.shape[0] // rows):
            spot = ((core ^ other) * chips + (chip ^ (first + i))) * rows
            whole[me ^ step, pl.ds(pl.multiple_of(spot, 16), rows), :] = ref[
                i * rows : (i + 1) * rows, :
            ]

    for other in range(2):
        own, px, py, d0, d1 = pieces[5 * other : 5 * other + 5]
        place(0, other, 0, own)
        place(1, other, 0, px)
        place(2, other, 0, py)
        place(3, other, 0, d0)
        place(3, other, chips // 2, d1)
    for kind, ref in enumerate((query_ref, key_ref, value_ref)):
        joined = jnp.concatenate(
            [whole[c, kind * group : (kind + 1) * group, :] for c in range(4)], axis=0
        )
        ref[...] = joined.astype(F32).T
    extra_ref[...] = whole[:, group3:, :].astype(F32)
    part = output_ref.shape[0] // (2 * chips)
    for other, ref in enumerate(halves):
        for i in range(chips):
            spot = ((core ^ other) * chips + (chip ^ i)) * part
            output_ref[pl.ds(pl.multiple_of(spot, 16), part), :] = ref[
                i * part : (i + 1) * part, :
            ].astype(F32)


def final_pass(info, pieces, halves, rows, width):
    span_rows = 2 * pieces[0].shape[0]
    extra = span_rows - 3 * (width // 4)
    square = jax.ShapeDtypeStruct((width, width), F32)
    return pl.pallas_call(
        functools.partial(final_kernel, rows),
        in_specs=[pl.BlockSpec(memory_space=pltpu.SMEM)]
        + [pl.BlockSpec(memory_space=pltpu.VMEM)] * (len(pieces) + len(halves)),
        out_shape=(square, square, square, square, jax.ShapeDtypeStruct((4, extra, width), F32)),
        scratch_shapes=[pltpu.VMEM((4, span_rows, width), BF)],
        compiler_params=pltpu.CompilerParams(vmem_limit_bytes=VMEM_BYTES),
        name="final_pass",
    )(info, *pieces, *halves)


def on_device(
    tokens,
    lengths,
    routes,
    bucket_table,
    gain_one,
    w_query,
    w_key,
    w_value,
    w_output,
    rel_bias,
    gain_two,
    w_router,
    w_in,
    w_out,
    cotangent,
):
    seqs, block_len, width = tokens.shape
    buckets, heads = rel_bias.shape
    experts = w_router.shape[1]
    ways = lax.axis_size("seq")
    me = lax.axis_index("seq")
    mine = lax.axis_index("exp")
    span = block_len * ways
    group = width // ways
    heads_here = heads // ways
    total_rows = seqs * block_len
    capacity = (5 * total_rows + 4 * experts - 1) // (4 * experts)
    order = me ^ jnp.arange(ways, dtype=jnp.int32)

    peers = lax.axis_size("exp")
    chips = peers // 2
    paired = peers == 8
    core, chip = mine % 2, mine // 2

    layer_inputs = tokens.reshape(total_rows, width).astype(F32)
    normed = rms_norm(layer_inputs, gain_one).astype(BF).reshape(tokens.shape)
    px, py, *diagonals = gather_pieces(normed, 1)

    positions = me * block_len + jnp.arange(block_len, dtype=jnp.int32)
    present = (positions[None, :] < lengths[:, None]).astype(F32).reshape(total_rows)
    routed = routes.reshape(total_rows)
    chosen = (routed[:, None] == jnp.arange(experts, dtype=jnp.int32)[None, :]).astype(F32)
    live_hits = chosen * present[:, None]
    row_ids = jnp.arange(total_rows, dtype=jnp.int32)
    lower = (row_ids[:, None] >= row_ids[None, :]).astype(BF)
    running = matmul_f32(lower, live_hits.astype(BF))
    slot_index = jnp.sum(live_hits * (running - 1.0), axis=-1)
    kept = present * (slot_index < capacity).astype(F32)
    if paired:
        away = routed ^ mine
        place = (away % 2) * chips + away // 2
    else:
        place = routed
    destin = place.astype(F32) * capacity + slot_index
    slot_ids = jnp.arange(experts * capacity, dtype=jnp.int32).astype(F32)
    placing = ((destin[None, :] == slot_ids[:, None]) & (kept[None, :] > 0)).astype(BF)
    placing_back = placing.T
    cotangent_rows = cotangent.reshape(total_rows, width)
    side = chips * capacity

    def exchange(rows):
        sent = rows.reshape(experts, capacity, width)
        return lax.all_to_all(sent, "exp", split_axis=0, concat_axis=0, tiled=True).reshape(
            experts * capacity, width
        )

    def to_experts(rows):
        sent = matmul_f32(placing, rows).astype(BF)
        if not paired:
            return [exchange(sent)]
        near = sent[:side].reshape(chips, capacity, width)
        other = trade(sent[side:], 1).reshape(chips, capacity, width)
        far = [
            trade(jnp.concatenate([near[k], other[k]], axis=0), 2 * k) for k in range(1, chips)
        ]
        return [near[0], other[0]] + far

    def from_experts(pieces):
        if not paired:
            return exchange(pieces[0])
        far = [trade(pieces[k + 1], 2 * k) for k in range(1, chips)]
        other = trade(jnp.concatenate([pieces[1]] + [p[capacity:] for p in far], axis=0), 1)
        return jnp.concatenate([pieces[0]] + [p[:capacity] for p in far] + [other], axis=0)

    grad_arrived = to_experts(cotangent_rows)

    joined = jnp.stack([w_query.T, w_key.T, w_value.T]).reshape(3, ways, group, width)
    joined = jnp.moveaxis(joined, 1, 0)[order]
    own_weights = joined[0]
    output_weights = w_output.reshape(ways, group, width)[order]
    wide = 2 * span
    padded = jnp.concatenate([bucket_table, jnp.full((1,), -1, jnp.int32)])
    turned = jnp.roll(jnp.flip(padded), -LANES)
    lookup = (jnp.arange(buckets, dtype=jnp.int32)[:, None] == turned[None, :]).astype(F32)
    own_bias = lax.dynamic_slice_in_dim(rel_bias, me * heads_here, heads_here, 1)
    bias_rows = jnp.dot(own_bias.T, lookup, precision=HIGH_PRECISION)
    base = make_base(bias_rows[:, None, :])

    infos = [jnp.stack([me, lengths[s]]) for s in range(seqs)]
    saved, attended = [], []
    for s in range(seqs):
        piece = diagonals[s].reshape(block_len, width)
        out, *rest = attention_forward(infos[s], normed, px, py, piece, s, own_weights, base)
        saved.append(rest)
        attended.append([out[0]] + [swap(out[step], step) for step in range(1, ways)])
    attended_cols = jnp.concatenate(
        [jnp.concatenate([attended[s][step] for s in range(seqs)], axis=1) for step in range(ways)],
        axis=0,
    )
    output_flat = output_weights.reshape(width, width)
    residual = layer_inputs + dot_dims(attended_cols, output_flat, 0, 0)
    routed_input = rms_norm(residual, gain_two).astype(BF)
    routed_input, *grad_arrived = lax.optimization_barrier((routed_input, *grad_arrived))

    expert_rows = to_experts(routed_input)
    router = jnp.pad(w_router, ((0, 0), (0, LANES - experts)))
    results = expert_pass(
        mine.reshape(1), experts, expert_rows, grad_arrived, router, w_in[0], w_out[0]
    )
    count = len(expert_rows)
    grad_back = from_experts(results[:count])
    hidden, grad_pre, rows_t, made_t, router_rows = results[2 * count :]
    chunk = lambda step, left, right: weight_chunks((me ^ step).reshape(1), left, right, ways)[0]
    first_3, second_3 = chunk(3, rows_t, grad_pre), chunk(3, made_t, hidden)
    first_3, second_3 = swap(first_3, 1), swap(second_3, 2)
    first_1, second_2 = chunk(1, rows_t, grad_pre), chunk(2, made_t, hidden)
    first_1, second_2 = swap(first_1, 1), swap(second_2, 2)
    first_2, second_1 = chunk(2, rows_t, grad_pre), chunk(1, made_t, hidden)
    first_0, second_0 = chunk(0, rows_t, grad_pre), chunk(0, made_t, hidden)
    add = lambda *terms: sum(term.astype(F32) for term in terms)
    first_2 = swap(add(first_2, first_3).astype(BF), 2)
    second_1 = swap(add(second_1, second_3).astype(BF), 1)
    grad_first = add(first_0, first_1, first_2)
    grad_second = add(second_0, second_1, second_2).T

    grad_routed = matmul_f32(placing_back, grad_back)
    grad_x_norm, gain_two_row = jax.vjp(rms_norm, residual, gain_two)[1](grad_routed)
    grad_x_one = cotangent_rows.astype(F32) * present[:, None] + grad_x_norm
    grad_branch = grad_x_one.astype(BF)
    grad_attended = dot_dims(output_flat, grad_branch, 1, 1).astype(BF)
    grad_attended = grad_attended.reshape(ways, group, seqs, block_len)
    returned = from_experts(results[count : 2 * count])
    picked = matmul_f32(placing_back, returned)
    mixed = (present[:, None] * (residual + picked)).astype(BF)

    grad_output = matmul_f32(attended_cols, grad_branch).astype(BF)
    grad_output = grad_output.reshape(ways, group, width)[order].reshape(width, width)
    if paired:
        part = width // 2
        kept_half = lax.dynamic_slice_in_dim(grad_output, core * part, part, 0)
        sent_half = lax.dynamic_slice_in_dim(grad_output, (1 - core) * part, part, 0)
        half = add(kept_half, trade(sent_half, 1)).astype(BF)
        part = part // chips
        spots = [
            lax.dynamic_slice_in_dim(half, (chip ^ k) * part, part, 0) for k in range(chips)
        ]
        spot = add(spots[0], *[trade(spots[k], 2 * k) for k in range(1, chips)]).astype(BF)
        spot = add(spot, swap(spot, 1)).astype(BF)
        spot = add(spot, swap(spot, 2)).astype(BF)
        near = jnp.concatenate([spot] + [trade(spot, 2 * k) for k in range(1, chips)], axis=0)
        output_halves = [near, trade(near, 1)]
    else:
        grad_output = lax.psum(grad_output, ("seq", "exp")).astype(F32)

    weight_sum, rel_sum, grad_pieces = 0.0, 0.0, []
    for s in range(seqs):
        sent = [grad_attended[step, :, s] for step in range(ways)]
        pieces = [sent[0]] + [swap(sent[step], step) for step in range(1, ways)]
        probs, q, k, v, rows = saved[s]
        back, weight_part, rel_part = attention_backward(infos[s], pieces, probs, q, k, v, rows)
        weight_sum = weight_sum + weight_part
        rel_sum = rel_sum + rel_part
        grad_pieces.append([back[0]] + [swap(back[step], step) for step in range(1, ways)])

    gain_one_row = jnp.sum(own_weights.astype(F32) * weight_sum, axis=(0, 1)) / gain_one
    rel_part = jnp.dot(rel_sum[:, 0], lookup.T, precision=HIGH_PRECISION).reshape(1, -1)
    rel_row = jnp.pad(rel_part, ((0, 0), (0, width - heads_here * buckets)))
    extras = jnp.concatenate(
        [gain_one_row[None], gain_two_row[None], rel_row, router_rows[:experts]], axis=0
    )
    extra_rows = -(-extras.shape[0] // 64) * 64
    extras = jnp.pad(extras, ((0, extra_rows - extras.shape[0]), (0, 0)))
    packed = jnp.concatenate([weight_sum.reshape(3 * group, width), extras], 0).astype(BF)
    if paired:
        part = packed.shape[0] // 2
        kept_half = lax.dynamic_slice_in_dim(packed, core * part, part, 0)
        sent_half = lax.dynamic_slice_in_dim(packed, (1 - core) * part, part, 0)
        half = add(kept_half, trade(sent_half, 1)).astype(BF)
        part = part // chips
        spots = [
            lax.dynamic_slice_in_dim(half, (chip ^ k) * part, part, 0) for k in range(chips)
        ]
        spot = add(spots[0], *[trade(spots[k], 2 * k) for k in range(1, chips)]).astype(BF)
        near = jnp.concatenate([spot] + [trade(spot, 2 * k) for k in range(1, chips)], axis=0)
        pieces = [near, *gather_pieces(near, near.shape[0] // 2)]
        pieces = pieces + [trade(piece, 1) for piece in pieces]
        info = jnp.stack([me, core, chip])
        *summed, grad_output, extras = final_pass(info, pieces, output_halves, part, width)
    else:
        packed = lax.all_gather(lax.psum(packed, "exp"), "seq").astype(F32)
        dense = packed[:, : 3 * group].reshape(ways, 3, group, width)
        summed = [dense[:, kind].reshape(width, width).T for kind in range(3)]
        extras = packed[:, 3 * group :]
    grad_gain_one = jnp.sum(extras[:, 0], axis=0)
    grad_gain_two = jnp.sum(extras[:, 1], axis=0)
    grad_rel = extras[:, 2, : heads_here * buckets].reshape(heads, buckets).T
    grad_router = jnp.sum(extras[:, 3 : 3 + experts], axis=0).T

    grad_cols = jnp.concatenate(
        [
            jnp.concatenate([grad_pieces[s][step] for s in range(seqs)], axis=-1)
            for step in range(ways)
        ],
        axis=0,
    ).reshape(ways * 3 * group, total_rows)
    grad_normed = dot_dims(grad_cols, joined.reshape(ways * 3 * group, width), 0, 0)
    grad_inputs = jax.vjp(lambda v: rms_norm(v, gain_one), layer_inputs)[1](grad_normed)[0]
    grad_tokens = (grad_x_one + grad_inputs).reshape(seqs, block_len, width)
    return (
        mixed.reshape(seqs, block_len, width),
        grad_tokens,
        grad_gain_one,
        summed[0],
        summed[1],
        summed[2],
        grad_output,
        grad_rel,
        grad_gain_two,
        grad_router,
        grad_first[None],
        grad_second[None],
    )


def solution(mesh):
    in_specs = (
        P("exp", "seq", None),
        P("exp"),
        P("exp", "seq", None),
        P(),
        P(),
        P(),
        P(),
        P(),
        P(),
        P(),
        P(),
        P(),
        P("exp", None, None),
        P("exp", None, None),
        P("exp", "seq", None),
    )
    out_specs = (
        P("exp", "seq", None),
        P("exp", "seq", None),
        P(),
        P(),
        P(),
        P(),
        P(),
        P(),
        P(),
        P(),
        P("exp", None, "seq"),
        P("exp", "seq", None),
    )
    return jax.shard_map(
        on_device, mesh=mesh, in_specs=in_specs, out_specs=out_specs, check_vma=False
    )
```

```python
import functools

import jax
import jax.numpy as jnp
from jax import lax
from jax.experimental import pallas as pl
from jax.experimental.pallas import tpu as pltpu
from jax.sharding import PartitionSpec as P

EPS = 1e-06
NEG = -1e30
HIGH_PRECISION = lax.Precision.HIGHEST
LANES = 128
VMEM_BYTES = 60 * 1024 * 1024
SMALL_BYTES = 24 * 1024 * 1024
BF = jnp.bfloat16
F32 = jnp.float32


def matmul_f32(left, right):
    return jnp.dot(left, right, preferred_element_type=F32)


def dot_dims(left, right, left_dim, right_dim):
    return lax.dot_general(
        left, right, (((left_dim,), (right_dim,)), ((), ())), preferred_element_type=F32
    )


def rms_norm(values_in, gain):
    return (
        values_in * lax.rsqrt(jnp.mean(values_in * values_in, axis=-1, keepdims=True) + EPS) * gain
    )


def swap(value, bit):
    ways = lax.axis_size("seq")
    return lax.ppermute(value, "seq", [(i, i ^ bit) for i in range(ways)])


def trade(value, bits):
    peers = lax.axis_size("exp")
    return lax.ppermute(value, "exp", [(i, i ^ bits) for i in range(peers)])


def multi(start, step):
    return pl.multiple_of(start, step)


def prep_kernel(group, info_ref, *refs):
    windows, row_ref = refs[:6], refs[6]
    weight_ref, base_ref, turned = refs[7:]
    offset = (info_ref[0] * group) % LANES
    for kind in range(3):
        left, right = windows[2 * kind][...], windows[2 * kind + 1][...]
        turned[...] = jnp.concatenate([left, right], axis=1).T
        weight_ref[kind] = turned[pl.ds(multi(offset, LANES // 2), group), :]
    for head in range(base_ref.shape[0]):
        row = row_ref[head]
        wide = jnp.broadcast_to(row, (LANES, row.shape[1]))
        base_ref[head] = pltpu.roll(wide, 0, 1, stride=1, stride_axis=0)


def prepare(info, weights, bias_rows, group):
    heads_here, _, wide = bias_rows.shape
    width = weights[0].shape[0]
    whole = lambda *shape: pl.BlockSpec(shape, lambda i, _: (0,) * len(shape))
    window = lambda side: pl.BlockSpec(
        (width, LANES), lambda i, info: (0, info[0] * group // LANES + side)
    )
    return pl.pallas_call(
        functools.partial(prep_kernel, group),
        grid_spec=pltpu.PrefetchScalarGridSpec(
            num_scalar_prefetch=1,
            grid=(1,),
            in_specs=[window(0), window(1)] * 3 + [whole(heads_here, 1, wide)],
            out_specs=(whole(3, group, width), whole(heads_here, LANES, wide)),
            scratch_shapes=[pltpu.VMEM((2 * LANES, width), BF)],
        ),
        out_shape=(
            jax.ShapeDtypeStruct((3, group, width), BF),
            jax.ShapeDtypeStruct((heads_here, LANES, wide), F32),
        ),
        compiler_params=pltpu.CompilerParams(vmem_limit_bytes=VMEM_BYTES),
        name="prepare",
    )(info, *[weight for weight in weights for _ in range(2)], bias_rows)


def forward_kernel(heads_here, head_dim, scale, seq_id, info_ref, *refs):
    own_ref, px_ref, py_ref, pd_ref, weight_ref, base_ref = refs[:6]
    outs = refs[6:10]
    probs_ref, q_ref, k_ref, v_ref, rows_ref, sum_ref, inverse_ref = refs[10:17]
    key_rows, value_cols, query_cols, mask_col, out_cols = refs[17:]
    me, length = info_ref[0], info_ref[4 + seq_id]
    head = pl.program_id(0)
    span = rows_ref.shape[0]
    block_len = own_ref.shape[0]
    group = heads_here * head_dim
    tiles = span // LANES
    width = weight_ref.shape[2]

    @pl.when(head == 0)
    def _():
        for step, piece in enumerate((own_ref, px_ref, py_ref, pd_ref)):
            start = multi((me ^ step) * block_len, block_len)
            rows_ref[pl.ds(start, block_len), :] = piece[...]
        rows = rows_ref[...]
        weights = weight_ref[...].reshape(3 * group, width)
        cols = dot_dims(weights, rows, 1, 1).astype(BF)
        spare = jnp.zeros((key_rows.shape[1] - group, width), BF)
        key_rows[...] = dot_dims(
            rows, jnp.concatenate([weight_ref[1], spare], axis=0), 1, 1
        ).astype(BF)
        v_ref[...] = dot_dims(
            rows, jnp.concatenate([weight_ref[2], spare], axis=0), 1, 1
        ).astype(BF)
        places = lax.broadcasted_iota(jnp.int32, (span, LANES), 0)
        mask_col[...] = jnp.where(places < length, 0.0, NEG)
        ones = (lax.broadcasted_iota(jnp.int32, (16, span), 0) == 0).astype(BF)
        for h in range(heads_here):
            lo, hi = h * head_dim, (h + 1) * head_dim
            q_ref[h] = (cols[lo:hi].astype(F32) * scale).astype(BF)
            k_ref[h] = cols[group + lo : group + hi]
            value_cols[h, :head_dim] = cols[2 * group + lo : 2 * group + hi]
            value_cols[h, head_dim:] = ones

    share = LANES // head_dim
    keys = key_rows[:, pl.ds(multi(head // share * LANES, LANES), LANES)]
    values = value_cols[head]
    query_cols[...] = jnp.zeros_like(query_cols)
    query_cols[pl.ds(multi(head % share * head_dim, head_dim), head_dim), :] = q_ref[head]
    mask = jnp.concatenate([mask_col[...]] * (block_len // LANES), axis=1)
    for c in range(span // block_len):
        cols = slice(c * block_len, (c + 1) * block_len)
        first = c * block_len // LANES + tiles - 1
        bias = jnp.concatenate(
            [
                base_ref[0, :, (first - a) * LANES : (first - a) * LANES + block_len]
                for a in range(tiles)
            ],
            axis=0,
        )
        scores = dot_dims(keys, query_cols[:, cols], 1, 0) + bias + mask
        top = jnp.max(scores, axis=0, keepdims=True)
        probs_ref[0, :, cols] = jnp.exp(scores - top).astype(BF)
    result = dot_dims(values, probs_ref[0], 1, 0)
    inverse = 1.0 / result[head_dim : head_dim + 1]
    inverse_ref[0] = inverse
    result = result[:head_dim] * inverse
    sum_ref[0] = result
    out_cols[...] = result.astype(BF)
    for step, ref in enumerate(outs):
        ref[...] = out_cols[:, pl.ds(multi((me ^ step) * block_len, block_len), block_len)]


def attention_forward(info, own, px, py, diag, seq_id, weights, base):
    _, block_len, width = own.shape
    _, group, _ = weights.shape
    heads_here, _, wide = base.shape
    head_dim = group // heads_here
    span = 4 * block_len
    lanes = -(-group // LANES) * LANES
    piece = pl.BlockSpec((None, block_len, width), lambda h, _: (seq_id, 0, 0))
    full = lambda *shape: pl.BlockSpec(shape, lambda h, _: (0,) * len(shape))
    out_shape = (
        *[jax.ShapeDtypeStruct((group, block_len), BF)] * 4,
        jax.ShapeDtypeStruct((heads_here, span, span), BF),
        jax.ShapeDtypeStruct((heads_here, head_dim, span), BF),
        jax.ShapeDtypeStruct((heads_here, head_dim, span), BF),
        jax.ShapeDtypeStruct((span, lanes), BF),
        jax.ShapeDtypeStruct((span, width), BF),
        jax.ShapeDtypeStruct((heads_here, head_dim, span), F32),
        jax.ShapeDtypeStruct((heads_here, 1, span), F32),
    )
    return pl.pallas_call(
        functools.partial(forward_kernel, heads_here, head_dim, head_dim ** (-0.5), seq_id),
        grid_spec=pltpu.PrefetchScalarGridSpec(
            num_scalar_prefetch=1,
            grid=(heads_here,),
            in_specs=[
                piece,
                piece,
                piece,
                full(block_len, width),
                full(3, group, width),
                pl.BlockSpec((1, LANES, wide), lambda h, _: (h, 0, 0)),
            ],
            out_specs=(
                *[pl.BlockSpec((head_dim, block_len), lambda h, _: (h, 0))] * 4,
                pl.BlockSpec((1, span, span), lambda h, _: (h, 0, 0)),
                full(heads_here, head_dim, span),
                full(heads_here, head_dim, span),
                full(span, lanes),
                full(span, width),
                pl.BlockSpec((1, head_dim, span), lambda h, _: (h, 0, 0)),
                pl.BlockSpec((1, 1, span), lambda h, _: (h, 0, 0)),
            ),
            scratch_shapes=[
                pltpu.VMEM((span, lanes), BF),
                pltpu.VMEM((heads_here, head_dim + 16, span), BF),
                pltpu.VMEM((LANES, span), BF),
                pltpu.VMEM((span, LANES), F32),
                pltpu.VMEM((head_dim, span), BF),
            ],
        ),
        out_shape=out_shape,
        compiler_params=pltpu.CompilerParams(vmem_limit_bytes=VMEM_BYTES),
        cost_estimate=pl.CostEstimate(
            flops=6 * heads_here * span * span * 256 * 2,
            bytes_accessed=heads_here * span * span * 2,
            transcendentals=heads_here * span * span,
        ),
        name="attention_forward",
    )(info, own, px, py, diag, weights, base)


def middle_kernel(seqs, info_ref, *refs):
    pieces = refs[: 4 * seqs]
    token_ref, output_ref, gain_ref, place_ref = refs[4 * seqs : 4 * seqs + 4]
    sum_ref, sent_ref, cols_ref = refs[4 * seqs + 4 :]
    me = info_ref[0]
    group, block_len = pieces[0].shape
    for s in range(seqs):
        for step in range(4):
            start = multi((me ^ step) * group, 64)
            cols_ref[pl.ds(start, group), s * block_len : (s + 1) * block_len] = pieces[
                4 * s + step
            ][...]
    residual = token_ref[...].astype(F32) + dot_dims(cols_ref[...], output_ref[...], 0, 0)
    sum_ref[...] = residual
    routed = rms_norm(residual, gain_ref[...]).astype(BF)
    sent_ref[...] = matmul_f32(place_ref[...], routed).astype(BF)


def middle_forward(info, pieces, tokens, w_output, gain, placing):
    rows, width = tokens.shape
    slots = placing.shape[0]
    return pl.pallas_call(
        functools.partial(middle_kernel, len(pieces) // 4),
        in_specs=[pl.BlockSpec(memory_space=pltpu.SMEM)]
        + [pl.BlockSpec(memory_space=pltpu.VMEM)] * (len(pieces) + 4),
        out_shape=(
            jax.ShapeDtypeStruct((rows, width), F32),
            jax.ShapeDtypeStruct((slots, width), BF),
            jax.ShapeDtypeStruct((width, rows), BF),
        ),
        compiler_params=pltpu.CompilerParams(vmem_limit_bytes=VMEM_BYTES),
        name="middle_forward",
    )(info, *pieces, tokens, w_output, gain, placing)


def turn_kernel(counts, seqs, info_ref, *refs):
    pieces = refs[: len(counts)]
    back_ref, sum_ref, gain_ref, cot_ref, here_ref, output_ref, attended_ref = refs[
        len(counts) : len(counts) + 7
    ]
    x_ref, grad_out, gain_out, *outs = refs[len(counts) + 7 : len(counts) + 14]
    rows_all, cols = refs[len(counts) + 14 :]
    me = info_ref[0]
    start = 0
    for piece, count in zip(pieces, counts, strict=True):
        rows_all[start : start + count, :] = piece[:count, :]
        start += count
    grads = matmul_f32(back_ref[...], rows_all[...])
    values, gain = sum_ref[...], gain_ref[...]
    root = lax.rsqrt(jnp.mean(values * values, axis=1, keepdims=True) + EPS)
    scaled = values * root
    gain_out[...] = jnp.sum(grads * scaled, axis=0, keepdims=True)
    grads = grads * gain
    inner = jnp.mean(grads * scaled, axis=1, keepdims=True)
    grad_x = cot_ref[...].astype(F32) * here_ref[...] + root * (grads - scaled * inner)
    x_ref[...] = grad_x
    branch = grad_x.astype(BF)
    grad_out[...] = matmul_f32(attended_ref[...], branch).astype(BF)
    cols[...] = dot_dims(output_ref[...], branch, 1, 1).astype(BF)
    _, group, block_len = outs[0].shape
    for step, out in enumerate(outs):
        start = multi((me ^ step) * group, 64)
        for s in range(seqs):
            out[s] = cols[pl.ds(start, group), s * block_len : (s + 1) * block_len]


def turn_back(
    info, pieces, counts, placing_back, residual, gain, cotangent, present, w_output, attended, seqs
):
    rows, width = residual.shape
    out = jax.ShapeDtypeStruct((seqs, width // 4, rows // seqs), BF)
    return pl.pallas_call(
        functools.partial(turn_kernel, counts, seqs),
        in_specs=[pl.BlockSpec(memory_space=pltpu.SMEM)]
        + [pl.BlockSpec(memory_space=pltpu.VMEM)] * (len(pieces) + 7),
        out_shape=(
            jax.ShapeDtypeStruct((rows, width), F32),
            jax.ShapeDtypeStruct((width, width), BF),
            jax.ShapeDtypeStruct((1, width), F32),
            out,
            out,
            out,
            out,
        ),
        scratch_shapes=[
            pltpu.VMEM((sum(counts), width), BF),
            pltpu.VMEM((width, rows), BF),
        ],
        compiler_params=pltpu.CompilerParams(vmem_limit_bytes=VMEM_BYTES),
        name="turn_back",
    )(info, *pieces, placing_back, residual, gain, cotangent, present, w_output, attended)


def backward_kernel(seqs, scale, experts, info_ref, *refs):
    pieces = refs[:4]
    groups = refs[4 : 4 + 7 * seqs]
    own_ref, lookup_ref, gain_ref, gain_two_ref, router_ref = refs[4 + 7 * seqs : 9 + 7 * seqs]
    outs = refs[9 + 7 * seqs : 13 + 7 * seqs]
    kept_ref, sent_ref, grad_cols, rel_sum, out_cols, weight_sum, packed, gain_sum, folds = refs[
        13 + 7 * seqs : 22 + 7 * seqs
    ]
    wide_cols, scores_all = refs[22 + 7 * seqs :]
    head, heads = pl.program_id(0), pl.num_programs(0)
    me = info_ref[0]
    head_dim, span = grad_cols.shape
    block_len = span // 4
    tiles = span // LANES
    rel_sum[...] = jnp.zeros_like(rel_sum)
    share = LANES // head_dim
    half = multi(head % share * head_dim, head_dim)
    wide_cols[...] = jnp.zeros_like(wide_cols)
    for s in range(seqs):
        probs_ref, q_ref, k_ref, v_ref, rows_ref, sum_ref, inverse_ref = groups[7 * s : 7 * s + 7]
        for step, piece in enumerate(pieces):
            start = multi((me ^ step) * block_len, block_len)
            grad_cols[:, pl.ds(start, block_len)] = piece[s]
        grads = (grad_cols[...].astype(F32) * inverse_ref[0]).astype(BF)
        inner = jnp.sum(grads.astype(F32) * sum_ref[0], axis=0, keepdims=True)
        wide_cols[pl.ds(half, head_dim), :] = grads
        values = v_ref[...]
        for c in range(span // block_len):
            cols = slice(c * block_len, (c + 1) * block_len)
            first = c * block_len // LANES + tiles - 1
            grad_probs = dot_dims(values, wide_cols[:, cols], 1, 0)
            grad_scores = probs_ref[0, :, cols].astype(F32) * (grad_probs - inner[:, cols])
            for a in range(tiles):
                spot = slice((first - a) * LANES, (first - a) * LANES + block_len)
                rel_sum[:, spot] += grad_scores[a * LANES : (a + 1) * LANES]
            scores_all[:, cols] = grad_scores.astype(BF)
        low = scores_all[...]
        out_cols[0] = (dot_dims(k_ref[0], low, 1, 0) * scale).astype(BF)
        out_cols[1] = matmul_f32(low, q_ref[0].T).astype(BF).T
        out_cols[2] = matmul_f32(probs_ref[0], grads.T).astype(BF).T
        rows = rows_ref[...]
        for kind in range(3):
            product = matmul_f32(out_cols[kind], rows)
            if s == 0:
                weight_sum[kind] = product
            else:
                weight_sum[kind] += product
        for step, out in enumerate(outs):
            start = multi((me ^ step) * block_len, block_len)
            for kind in range(3):
                out[s, kind] = out_cols[kind, :, pl.ds(start, block_len)]
    fold = rel_sum[...]
    wide = fold.shape[1]
    half = LANES // 2
    while half >= 1:
        fold = fold[:half] + pltpu.roll(fold[half:], wide - half, 1)
        half //= 2
    sums = weight_sum[...]
    for kind in range(3):
        start = multi((3 * head + kind) * head_dim, head_dim)
        packed[pl.ds(start, head_dim), :] = sums[kind].astype(BF)

    @pl.when(head == 0)
    def _():
        gain_sum[...] = jnp.zeros_like(gain_sum)
        folds[...] = jnp.zeros_like(folds)

    gain_sum[...] += jnp.sum(own_ref[...].astype(F32) * sums, axis=(0, 1))[None]
    folds[pl.ds(head, 1), :] = fold

    @pl.when(head == heads - 1)
    def _():
        count = weight_sum.shape[2] // (4 * head_dim)
        buckets, width = lookup_ref.shape[0], packed.shape[1]
        rel = lax.dot_general(
            folds[...],
            lookup_ref[...],
            (((1,), (1,)), ((), ())),
            precision=HIGH_PRECISION,
            preferred_element_type=F32,
        )
        rel_row = jnp.concatenate([rel[h : h + 1] for h in range(count)], axis=1)
        rel_row = jnp.pad(rel_row, ((0, 0), (0, width - count * buckets)))
        small = [gain_sum[...] / gain_ref[...], gain_two_ref[...], rel_row, router_ref[:experts]]
        small = jnp.concatenate(small, axis=0)
        start = 3 * count * head_dim
        spare = packed.shape[0] - start - small.shape[0]
        packed[start:, :] = jnp.pad(small, ((0, spare), (0, 0))).astype(BF)
        half, core = packed.shape[0] // 2, info_ref[2]
        kept_ref[...] = packed[pl.ds(multi(core * half, 16), half), :]
        sent_ref[...] = packed[pl.ds(multi((1 - core) * half, 16), half), :]


def attention_backward(
    info, pieces, saved, own_weights, lookup, gain_one, gain_two_row, router_rows, experts
):
    seqs = len(saved)
    heads, head_dim, span = saved[0][1].shape
    width = saved[0][4].shape[1]
    block_len = span // 4
    total = 3 * heads * head_dim + -(-(3 + experts) // 64) * 64
    per_head = lambda *shape: pl.BlockSpec((1,) + shape, lambda h, _: (h,) + (0,) * len(shape))
    whole = lambda *shape: pl.BlockSpec(shape, lambda h, _: (0,) * len(shape))
    group_specs = [
        per_head(span, span),
        per_head(head_dim, span),
        per_head(head_dim, span),
        pl.BlockSpec((span, LANES), lambda h, _: (0, h // (LANES // head_dim))),
        whole(span, width),
        per_head(head_dim, span),
        per_head(1, span),
    ]
    out_spec = pl.BlockSpec((seqs, 3, head_dim, block_len), lambda h, _: (0, 0, h, 0))
    out_type = jax.ShapeDtypeStruct((seqs, 3, heads * head_dim, block_len), BF)
    half_type = jax.ShapeDtypeStruct((total // 2, width), BF)
    return pl.pallas_call(
        functools.partial(backward_kernel, seqs, head_dim ** (-0.5), experts),
        grid_spec=pltpu.PrefetchScalarGridSpec(
            num_scalar_prefetch=1,
            grid=(heads,),
            in_specs=[pl.BlockSpec((seqs, head_dim, block_len), lambda h, _: (0, h, 0))] * 4
            + group_specs * seqs
            + [
                pl.BlockSpec((3, head_dim, width), lambda h, _: (0, h, 0)),
                whole(*lookup.shape),
                whole(1, width),
                whole(1, width),
                whole(*router_rows.shape),
            ],
            out_specs=[out_spec] * 4 + [whole(*half_type.shape)] * 2,
            scratch_shapes=[
                pltpu.VMEM((head_dim, span), BF),
                pltpu.VMEM((LANES, 2 * span), F32),
                pltpu.VMEM((3, head_dim, span), BF),
                pltpu.VMEM((3, head_dim, width), F32),
                pltpu.VMEM((total, width), BF),
                pltpu.VMEM((1, width), F32),
                pltpu.VMEM((8, 2 * span), F32),
                pltpu.VMEM((LANES, span), BF),
                pltpu.VMEM((span, span), BF),
            ],
        ),
        out_shape=[out_type] * 4 + [half_type] * 2,
        compiler_params=pltpu.CompilerParams(vmem_limit_bytes=VMEM_BYTES),
        cost_estimate=pl.CostEstimate(
            flops=8 * seqs * heads * span * span * 256 * 2,
            bytes_accessed=seqs * heads * span * span * 2,
            transcendentals=0,
        ),
        name="attention_backward",
    )(
        info,
        *pieces,
        *[array for group in saved for array in group],
        own_weights,
        lookup,
        gain_one,
        gain_two_row,
        router_rows,
    )


def pick_kernel(info_ref, *refs):
    pieces, out_ref = refs[:-1], refs[-1]
    rows = pieces[0].shape[0] // 2
    start = multi((1 - info_ref[2]) * rows, 16)
    for k, piece in enumerate(pieces):
        out_ref[k * rows : (k + 1) * rows, :] = piece[pl.ds(start, rows), :]


def pick_rows(info, pieces):
    rows, width = pieces[0].shape
    return pl.pallas_call(
        pick_kernel,
        in_specs=[pl.BlockSpec(memory_space=pltpu.SMEM)]
        + [pl.BlockSpec(memory_space=pltpu.VMEM)] * len(pieces),
        out_shape=jax.ShapeDtypeStruct((len(pieces) * rows // 2, width), BF),
        compiler_params=pltpu.CompilerParams(vmem_limit_bytes=SMALL_BYTES),
        name="pick_rows",
    )(info, *pieces)


def mix_kernel(info_ref, *refs):
    pieces, (other_ref, back_ref, sum_ref, here_ref, out_ref, rows_all) = refs[:-6], refs[-6:]
    rows = pieces[0].shape[0] // 2
    core, chip = info_ref[2], info_ref[3]
    for k, piece in enumerate(pieces):
        base = (chip ^ k) * 2
        own = piece[pl.ds(multi(core * rows, 16), rows), :]
        rows_all[pl.ds(multi((base + core) * rows, 16), rows), :] = own
        other = other_ref[k * rows : (k + 1) * rows, :]
        rows_all[pl.ds(multi((base + 1 - core) * rows, 16), rows), :] = other
    picked = matmul_f32(back_ref[...], rows_all[...])
    out_ref[...] = (here_ref[...] * (sum_ref[...] + picked)).astype(BF)


def mix_rows(info, pieces, other, placing_back, residual, present):
    rows, width = residual.shape
    return pl.pallas_call(
        mix_kernel,
        in_specs=[pl.BlockSpec(memory_space=pltpu.SMEM)]
        + [pl.BlockSpec(memory_space=pltpu.VMEM)] * (len(pieces) + 4),
        out_shape=jax.ShapeDtypeStruct((rows, width), BF),
        scratch_shapes=[pltpu.VMEM((2 * other.shape[0], width), BF)],
        compiler_params=pltpu.CompilerParams(vmem_limit_bytes=VMEM_BYTES),
        name="mix_rows",
    )(info, *pieces, other, placing_back, residual, present)


def gather_sum_kernel(info_ref, parts_ref, kept_ref, sent_ref, total):
    total[...] = jnp.sum(parts_ref[...].astype(F32), axis=0)
    rows, core = kept_ref.shape[0], info_ref[2]
    kept_ref[...] = total[pl.ds(multi(core * rows, 8), rows), :].astype(BF)
    sent_ref[...] = total[pl.ds(multi((1 - core) * rows, 8), rows), :].astype(BF)


def gather_sum(info, parts):
    _, rows, width = parts.shape
    half = jax.ShapeDtypeStruct((rows // 2, width), BF)
    return pl.pallas_call(
        gather_sum_kernel,
        in_specs=[pl.BlockSpec(memory_space=pltpu.SMEM), pl.BlockSpec(memory_space=pltpu.VMEM)],
        out_shape=(half, half),
        scratch_shapes=[pltpu.VMEM((rows, width), F32)],
        compiler_params=pltpu.CompilerParams(vmem_limit_bytes=SMALL_BYTES),
        name="gather_sum",
    )(info, parts)


def split_kernel(info_ref, kept_ref, other_ref, kept_more_ref, other_more_ref, *refs):
    *outs, half, more = refs
    chip = info_ref[3]
    half[...] = (kept_ref[...].astype(F32) + other_ref[...].astype(F32)).astype(BF)
    more[...] = kept_more_ref[...].astype(F32) + other_more_ref[...].astype(F32)
    rows, small = half.shape[0] // len(outs), more.shape[0] // len(outs)
    for k, out in enumerate(outs):
        out[:rows, :] = half[pl.ds(multi((chip ^ k) * rows, 16), rows), :]
        extra = more[pl.ds(multi((chip ^ k) * small, 8), small), :]
        spare = out.shape[0] - rows - small
        out[rows:, :] = jnp.pad(extra, ((0, spare), (0, 0))).astype(BF)


def split_sum(info, kept, other, kept_more, other_more, chips):
    rows, width = kept.shape
    small = kept_more.shape[0]
    out = jax.ShapeDtypeStruct((rows // chips + -(-small // chips // 16) * 16, width), BF)
    return pl.pallas_call(
        split_kernel,
        in_specs=[pl.BlockSpec(memory_space=pltpu.SMEM)]
        + [pl.BlockSpec(memory_space=pltpu.VMEM)] * 4,
        out_shape=(out,) * chips,
        scratch_shapes=[pltpu.VMEM((rows, width), BF), pltpu.VMEM((small, width), F32)],
        compiler_params=pltpu.CompilerParams(vmem_limit_bytes=SMALL_BYTES),
        name="split_sum",
    )(info, kept, other, kept_more, other_more)


def tail_kernel(heads, seqs, info_ref, *refs):
    pieces = refs[: 4 * len(heads)]
    *weights, token_ref, gain_ref, x_ref, out_ref, cols = refs[4 * len(heads) :]
    me = info_ref[0]
    _, width, rows = cols.shape
    block_len, group = rows // seqs, width // 4
    offset = 0
    for part, count in enumerate(heads):
        for step in range(4):
            piece = pieces[4 * part + step]
            start = multi((me ^ step) * group + offset, 64)
            for s in range(seqs):
                for kind in range(3):
                    cols[
                        kind, pl.ds(start, count), s * block_len : (s + 1) * block_len
                    ] = piece[s, kind]
        offset += count
    turned = sum(matmul_f32(weights[kind][...], cols[kind]) for kind in range(3))
    values = token_ref[...].astype(F32)
    root = lax.rsqrt(jnp.mean(values * values, axis=1, keepdims=True) + EPS)
    scaled = values * root
    grads = turned.T * gain_ref[...]
    inner = jnp.mean(grads * scaled, axis=1, keepdims=True)
    out_ref[...] = x_ref[...] + root * (grads - scaled * inner)


def tail_pass(info, pieces, heads, weights, tokens, gain, grad_x, seqs):
    rows, width = tokens.shape
    return pl.pallas_call(
        functools.partial(tail_kernel, heads, seqs),
        in_specs=[pl.BlockSpec(memory_space=pltpu.SMEM)]
        + [pl.BlockSpec(memory_space=pltpu.VMEM)] * (len(pieces) + 6),
        out_shape=jax.ShapeDtypeStruct((rows, width), F32),
        scratch_shapes=[pltpu.VMEM((3, width, rows), BF)],
        compiler_params=pltpu.CompilerParams(vmem_limit_bytes=VMEM_BYTES),
        name="tail_pass",
    )(info, *pieces, *weights, tokens, gain, grad_x)


def gelu_both(pre):
    square = pre * pre
    curve = jnp.tanh(pre * (0.7978845608028654 + 0.035677408136300125 * square))
    half = 0.5 + 0.5 * curve
    slope = half + pre * (0.5 - 0.5 * curve * curve) * (
        0.7978845608028654 + 0.10703222440890037 * square
    )
    return pre * half, slope


def router_prob(rows, router, experts):
    logits = matmul_f32(rows, router)
    lanes = lax.broadcasted_iota(jnp.int32, logits.shape, 1)
    logits = jnp.where(lanes < experts, logits, NEG)
    powers = jnp.exp(logits - jnp.max(logits, axis=1, keepdims=True))
    return powers / jnp.sum(powers, axis=1, keepdims=True), lanes


def expert_kernel(experts, parts, counts, mine_ref, *refs):
    row_refs, grad_refs = refs[:parts], refs[parts : 2 * parts]
    router_ref, first_ref, second_ref = refs[2 * parts : 2 * parts + 3]
    refs = refs[2 * parts + 3 :]
    back_ref, mixed_refs = refs[0], refs[1 : 1 + len(counts)]
    router_grad_ref, rows_all, grads_all, made_all, prob_all, out_sum, back_sum, mixed = refs[
        1 + len(counts) :
    ]
    step, steps = pl.program_id(0), pl.num_programs(0)

    @pl.when(step == 0)
    def _():
        start = 0
        for row_ref, grad_ref in zip(row_refs, grad_refs, strict=True):
            rows_all[start : start + row_ref.shape[0], :] = row_ref[...]
            grads_all[start : start + row_ref.shape[0], :] = grad_ref[...]
            start += row_ref.shape[0]
        prob, lanes = router_prob(rows_all[...], router_ref[...], experts)
        prob_all[...] = prob
        is_mine = lanes == mine_ref[1]
        gate = experts * jnp.sum(jnp.where(is_mine, prob, 0.0), axis=1, keepdims=True)
        made_all[...] = (gate * grads_all[...].astype(F32)).astype(BF)
        out_sum[...] = jnp.zeros_like(out_sum)
        back_sum[...] = jnp.zeros_like(back_sum)

    first, second = first_ref[...], second_ref[...]
    pre = matmul_f32(rows_all[...], first)
    grad_hidden = dot_dims(made_all[...], second, 1, 1)
    hidden, slope = gelu_both(pre)
    out_sum[...] += matmul_f32(hidden.astype(BF), second)
    back_sum[...] += dot_dims((grad_hidden * slope).astype(BF), first, 1, 1)

    @pl.when(step == steps - 1)
    def _():
        prob = prob_all[...]
        is_mine = lax.broadcasted_iota(jnp.int32, prob.shape, 1) == mine_ref[1]
        prob_mine = jnp.sum(jnp.where(is_mine, prob, 0.0), axis=1, keepdims=True)
        expert_out = out_sum[...].astype(BF).astype(F32)
        upper = experts * jnp.sum(grads_all[...].astype(F32) * expert_out, axis=1, keepdims=True)
        inner = prob_mine * upper
        grad_logits = (prob * (jnp.where(is_mine, upper, 0.0) - inner)).astype(BF)
        back = back_sum[...] + dot_dims(grad_logits, router_ref[...], 1, 1)
        back_ref[...] = back.astype(BF)
        mixed[...] = (experts * prob_mine * expert_out).astype(BF)
        if len(counts) == 1:
            mixed_refs[0][...] = mixed[...]
        else:
            for k, (count, ref) in enumerate(zip(counts, mixed_refs, strict=True)):
                start = multi((mine_ref[3] ^ k) * count, 16)
                ref[...] = mixed[pl.ds(start, count), :]
        router_grad_ref[...] = dot_dims(grad_logits, rows_all[...], 0, 0)


def expert_pass(mine, experts, row_parts, grad_parts, counts, router, first, second):
    width, hidden_width = first.shape
    total = sum(counts)
    tile = hidden_width // 6
    whole = lambda *shape: pl.BlockSpec(shape, lambda f, _: (0,) * len(shape))
    part_specs = [whole(*part.shape) for part in row_parts]
    piece_specs = [whole(count, width) for count in counts]
    piece_shapes = [jax.ShapeDtypeStruct((count, width), BF) for count in counts]
    return pl.pallas_call(
        functools.partial(expert_kernel, experts, len(row_parts), counts),
        grid_spec=pltpu.PrefetchScalarGridSpec(
            num_scalar_prefetch=1,
            grid=(hidden_width // tile,),
            in_specs=part_specs * 2
            + [
                whole(width, LANES),
                pl.BlockSpec((width, tile), lambda f, _: (0, f)),
                pl.BlockSpec((tile, width), lambda f, _: (f, 0)),
            ],
            out_specs=[whole(total, width)] + piece_specs + [whole(LANES, width)],
            scratch_shapes=[
                pltpu.VMEM((total, width), BF),
                pltpu.VMEM((total, width), BF),
                pltpu.VMEM((total, width), BF),
                pltpu.VMEM((total, LANES), F32),
                pltpu.VMEM((total, width), F32),
                pltpu.VMEM((total, width), F32),
                pltpu.VMEM((total, width), BF),
            ],
        ),
        out_shape=[jax.ShapeDtypeStruct((total, width), BF)]
        + piece_shapes
        + [jax.ShapeDtypeStruct((LANES, width), F32)],
        compiler_params=pltpu.CompilerParams(vmem_limit_bytes=VMEM_BYTES),
        cost_estimate=pl.CostEstimate(
            flops=8 * total * width * hidden_width,
            bytes_accessed=4 * width * hidden_width,
            transcendentals=total * hidden_width,
        ),
        name="expert_pass",
    )(mine, *row_parts, *grad_parts, router, first, second)


def grads_kernel(experts, parts, prior, info_ref, *refs):
    row_refs, grad_refs = refs[:parts], refs[parts : 2 * parts]
    router_ref, first_ref, second_ref = refs[2 * parts : 2 * parts + 3]
    refs = refs[2 * parts + 3 :]
    if prior:
        (prior_first, prior_second), refs = refs[:2], refs[2:]
    grad_first, grad_second, rows_all, rows_t, made_all, hidden_all, pre_all = refs
    count = row_refs[0].shape[0]

    @pl.when(pl.program_id(0) == 0)
    def _():
        for part in range(parts):
            spot = slice(part * count, (part + 1) * count)
            rows = row_refs[part][...]
            prob, lanes = router_prob(rows, router_ref[...], experts)
            gate = experts * jnp.sum(
                jnp.where(lanes == info_ref[1], prob, 0.0), axis=1, keepdims=True
            )
            made_all[spot, :] = (gate * grad_refs[part][...].astype(F32)).astype(BF)
            rows_all[spot, :] = rows
        rows_t[...] = rows_all[...].T

    first, second = first_ref[...], second_ref[...]
    for part in range(parts):
        spot = slice(part * count, (part + 1) * count)
        pre = matmul_f32(row_refs[part][...], first)
        grad_hidden = dot_dims(made_all[spot, :], second, 1, 1)
        hidden, slope = gelu_both(pre)
        hidden_all[spot, :] = hidden.astype(BF)
        pre_all[spot, :] = (grad_hidden * slope).astype(BF)
    own_first = matmul_f32(rows_t[...], pre_all[...])
    own_second = dot_dims(hidden_all[...], made_all[...], 0, 0)
    if prior:
        own_first = own_first + prior_first[...]
        own_second = own_second + prior_second[...]
    grad_first[...] = own_first
    grad_second[...] = own_second


def expert_grads(info, experts, row_parts, grad_parts, router, first, second, prior):
    width, hidden_width = first.shape
    own = hidden_width // 4
    tile = 256
    tiles = own // tile
    total = sum(part.shape[0] for part in row_parts)
    whole = lambda *shape: pl.BlockSpec(shape, lambda t, _: (0,) * len(shape))
    part_specs = [whole(*part.shape) for part in row_parts]
    out_specs = [
        pl.BlockSpec((width, tile), lambda t, _: (0, t)),
        pl.BlockSpec((tile, width), lambda t, _: (t, 0)),
    ]
    return pl.pallas_call(
        functools.partial(grads_kernel, experts, len(row_parts), len(prior) > 0),
        grid_spec=pltpu.PrefetchScalarGridSpec(
            num_scalar_prefetch=1,
            grid=(tiles,),
            in_specs=part_specs * 2
            + [
                whole(width, LANES),
                pl.BlockSpec((width, tile), lambda t, info: (0, info[0] * tiles + t)),
                pl.BlockSpec((tile, width), lambda t, info: (info[0] * tiles + t, 0)),
            ]
            + out_specs[: len(prior)],
            out_specs=out_specs,
            scratch_shapes=[
                pltpu.VMEM((total, width), BF),
                pltpu.VMEM((width, total), BF),
                pltpu.VMEM((total, width), BF),
                pltpu.VMEM((total, tile), BF),
                pltpu.VMEM((total, tile), BF),
            ],
        ),
        out_shape=(
            jax.ShapeDtypeStruct((width, own), F32),
            jax.ShapeDtypeStruct((own, width), F32),
        ),
        compiler_params=pltpu.CompilerParams(vmem_limit_bytes=VMEM_BYTES),
        cost_estimate=pl.CostEstimate(
            flops=total * width,
            bytes_accessed=total * width // 64,
            transcendentals=0,
        ),
        name="expert_grads",
    )(info, *row_parts, *grad_parts, router, first, second, *prior)


def final_kernel(rows, head_dim, info_ref, *refs):
    pieces = refs[:10]
    query_ref, key_ref, value_ref, output_ref, small_ref, rel_ref, whole = refs[10:]
    me, core, chip = info_ref[0], info_ref[2], info_ref[3]
    each = whole.shape[1] // 8
    step_rows = output_ref.shape[0] // 32
    chips = pieces[0].shape[0] // rows
    for other in range(2):
        for step, first, ref in zip(
            (0, 1, 2, 3, 3), (0, 0, 0, 0, chips // 2), pieces[5 * other : 5 * other + 5], strict=True
        ):
            for i in range(ref.shape[0] // rows):
                c, z = me ^ step, chip ^ (first + i)
                spot = ((core ^ other) * chips + z) * each
                whole[c, pl.ds(multi(spot, 16), each), :] = ref[i * rows : i * rows + each, :]
                tail = ref[i * rows + each : (i + 1) * rows, :].astype(F32)
                spot = ((c * 2 + (core ^ other)) * chips + z) * step_rows
                output_ref[pl.ds(multi(spot, 8), step_rows), :] = tail[:step_rows]
    heads = query_ref.shape[0] // (4 * head_dim)
    for kind, ref in enumerate((query_ref, key_ref, value_ref)):
        joined = [
            whole[c, (3 * h + kind) * head_dim : (3 * h + kind + 1) * head_dim, :]
            for c in range(4)
            for h in range(heads)
        ]
        ref[...] = jnp.concatenate(joined, axis=0).astype(F32).T
    small = whole[:, 3 * heads * head_dim :, :].astype(F32)
    small_ref[...] = jnp.sum(small, axis=0)
    rel_ref[...] = small[:, 2, :]


def final_pass(info, pieces, rows, head_dim, total, width):
    square = jax.ShapeDtypeStruct((width, width), F32)
    extra = total - 3 * (width // 4)
    return pl.pallas_call(
        functools.partial(final_kernel, rows, head_dim),
        in_specs=[pl.BlockSpec(memory_space=pltpu.SMEM)]
        + [pl.BlockSpec(memory_space=pltpu.VMEM)] * len(pieces),
        out_shape=(
            square,
            square,
            square,
            square,
            jax.ShapeDtypeStruct((extra, width), F32),
            jax.ShapeDtypeStruct((4, width), F32),
        ),
        scratch_shapes=[pltpu.VMEM((4, total, width), BF)],
        compiler_params=pltpu.CompilerParams(vmem_limit_bytes=SMALL_BYTES),
        name="final_pass",
    )(info, *pieces)


def on_device(
    tokens,
    lengths,
    routes,
    bucket_table,
    gain_one,
    w_query,
    w_key,
    w_value,
    w_output,
    rel_bias,
    gain_two,
    w_router,
    w_in,
    w_out,
    cotangent,
):
    seqs, block_len, width = tokens.shape
    buckets, heads = rel_bias.shape
    experts = w_router.shape[1]
    ways = lax.axis_size("seq")
    me = lax.axis_index("seq")
    mine = lax.axis_index("exp")
    span = block_len * ways
    group = width // ways
    heads_here = heads // ways
    total_rows = seqs * block_len
    capacity = (5 * total_rows + 4 * experts - 1) // (4 * experts)

    peers = lax.axis_size("exp")
    chips = peers // 2
    paired = peers == 8
    core, chip = mine % 2, mine // 2

    layer_inputs = tokens.reshape(total_rows, width).astype(F32)
    normed = rms_norm(layer_inputs, gain_one).astype(BF).reshape(tokens.shape)
    px, py = swap(normed, 1), swap(normed, 2)

    positions = me * block_len + jnp.arange(block_len, dtype=jnp.int32)
    present = (positions[None, :] < lengths[:, None]).astype(F32).reshape(total_rows)
    routed = routes.reshape(total_rows)
    chosen = (routed[:, None] == jnp.arange(experts, dtype=jnp.int32)[None, :]).astype(F32)
    live_hits = chosen * present[:, None]
    row_ids = jnp.arange(total_rows, dtype=jnp.int32)
    lower = (row_ids[:, None] >= row_ids[None, :]).astype(BF)
    running = matmul_f32(lower, live_hits.astype(BF))
    slot_index = jnp.sum(live_hits * (running - 1.0), axis=-1)
    kept = present * (slot_index < capacity).astype(F32)
    destin = routed.astype(F32) * capacity + slot_index
    slot_ids = jnp.arange(experts * capacity, dtype=jnp.int32).astype(F32)
    placing = ((destin[None, :] == slot_ids[:, None]) & (kept[None, :] > 0)).astype(BF)
    placing_back = placing.T
    cotangent_rows = cotangent.reshape(total_rows, width)

    def exchange(rows):
        sent = rows.reshape(experts, capacity, width)
        return lax.all_to_all(sent, "exp", split_axis=0, concat_axis=0, tiled=True).reshape(
            experts * capacity, width
        )


    wide = 2 * span
    padded = jnp.concatenate([bucket_table, jnp.full((1,), -1, jnp.int32)])
    turned = jnp.roll(jnp.flip(padded), -LANES)
    lookup = (jnp.arange(buckets, dtype=jnp.int32)[:, None] == turned[None, :]).astype(F32)
    own_bias = lax.dynamic_slice_in_dim(rel_bias, me * heads_here, heads_here, 1)
    bias_rows = jnp.dot(own_bias.T, lookup, precision=HIGH_PRECISION)
    info = jnp.concatenate([jnp.stack([me, mine, core, chip]), lengths])
    own_weights, base = prepare(info, (w_query, w_key, w_value), bias_rows[:, None, :], group)

    held, _ = lax.optimization_barrier((cotangent_rows, own_weights))
    px, py, own_weights, base = lax.optimization_barrier((px, py, own_weights, base))
    diagonals = (swap(px[:1], 2), swap(py[1:], 1))
    cot_rows = exchange(matmul_f32(placing, held).astype(BF))
    saved, attended = [], []
    for s in range(seqs):
        piece = diagonals[s].reshape(block_len, width)
        if s == 1:
            info, cot_rows = lax.optimization_barrier((info, cot_rows))
        *outs, probs, q, k, v, rows, sums, inverse = attention_forward(
            info, normed, px, py, piece, s, own_weights, base
        )
        saved.append((probs, q, k, v, rows, sums, inverse))
        attended += [outs[0]] + [swap(outs[step], step) for step in range(1, ways)]
    attended, cot_rows = lax.optimization_barrier((attended, cot_rows))
    cot_all = [swap(cot_rows, 1), swap(cot_rows, 2)]
    gain_row = gain_two[None]
    residual, sent, attended_cols = middle_forward(
        info, attended, tokens.reshape(total_rows, width), w_output, gain_row, placing
    )

    rows = exchange(sent)
    row_all = [swap(rows, 1), swap(rows, 2)]
    router = jnp.pad(w_router, ((0, 0), (0, LANES - experts)))
    counts = (2 * capacity,) * chips if paired else (experts * capacity,)
    grad_back, *weighted_out, router_rows = expert_pass(
        info, experts, [rows], [cot_rows], counts, router, w_in[0], w_out[0]
    )
    grad_back, row_all, cot_all, cot_late = lax.optimization_barrier(
        (grad_back, row_all, cot_all, cot_rows)
    )
    cot_all.append(swap(cot_late, 3))
    grad_back = exchange(grad_back)
    grads_of = lambda row_parts, cot_parts, prior: expert_grads(
        info, experts, row_parts, cot_parts, router, w_in[0], w_out[0], prior
    )
    expert_sums = grads_of([rows, *row_all], [cot_rows, *cot_all[:2]], ())
    grad_back, cot_all[2], row_late, expert_sums = lax.optimization_barrier(
        (grad_back, cot_all[2], rows, expert_sums)
    )

    grad_x_one, grad_output, gain_two_row, *grad_pieces = turn_back(
        info,
        [grad_back],
        (experts * capacity,),
        placing_back,
        residual,
        gain_row,
        cotangent_rows,
        present[:, None],
        w_output,
        attended_cols,
        seqs,
    )
    grad_pieces = [grad_pieces[0]] + [swap(grad_pieces[k], k) for k in range(1, ways)]
    grad_pieces, row_late = lax.optimization_barrier((grad_pieces, row_late))
    row_far = swap(row_late, 3)
    add = lambda *terms: sum(term.astype(F32) for term in terms)
    grad_output = lax.all_to_all(
        grad_output.reshape(ways, group, width), "seq", split_axis=0, concat_axis=0, tiled=True
    )
    weighted_out, _ = lax.optimization_barrier((weighted_out, grad_x_one))
    if paired:
        returned = [weighted_out[0]] + [trade(weighted_out[k], 2 * k) for k in range(1, chips)]
    else:
        returned = exchange(weighted_out[0])

    head_dim = group // heads_here

    def tail(*pieces):
        return tail_pass(
            info,
            pieces,
            (group,),
            (w_query, w_key, w_value),
            tokens.reshape(total_rows, width),
            gain_one[None],
            grad_x_one,
            seqs,
        )

    *outs, kept_half, sent_half = attention_backward(
        info,
        grad_pieces,
        saved,
        own_weights,
        lookup,
        gain_one[None],
        gain_two_row,
        router_rows,
        experts,
    )
    kept_half, sent_half, returned, grad_output = lax.optimization_barrier(
        (kept_half, sent_half, returned, grad_output)
    )
    kept_more, sent_more = gather_sum(info, grad_output)
    sent_half, kept_more, sent_more = lax.optimization_barrier((sent_half, kept_more, sent_more))
    total = 2 * kept_half.shape[0]
    col_x, col_y = swap(outs[1], 1), swap(outs[2], 2)
    if paired:
        spots = split_sum(
            info, kept_half, trade(sent_half, 1), kept_more, trade(sent_more, 1), chips
        )
        spot = add(spots[0], *[trade(spots[k], 2 * k) for k in range(1, chips)]).astype(BF)
        row_far, _ = lax.optimization_barrier((row_far, spots[0]))
        expert_sums = grads_of([row_far], [cot_all[2]], expert_sums)
        spot, col_x, col_y, far_out, *expert_sums = lax.optimization_barrier(
            (spot, col_x, col_y, outs[3], *expert_sums)
        )
        col_far = swap(far_out, 3)
        near = jnp.concatenate([spot] + [trade(spot, 2 * k) for k in range(1, chips)], axis=0)
        near, col_far, returned = lax.optimization_barrier((near, col_far, returned))
        other = trade(pick_rows(info, returned), 1)
        grad_tokens = tail(outs[0], col_x, col_y, col_far)
        part = near.shape[0] // 2
        px, py = swap(near, 1), swap(near, 2)
        px, py, grad_tokens = lax.optimization_barrier((px, py, grad_tokens))
        mixed = mix_rows(info, returned, other, placing_back, residual, present[:, None])
        pieces = [near, px, py, swap(px[:part], 2), swap(py[part:], 1)]
        pieces = pieces + [trade(piece, 1) for piece in pieces]
        *summed, grad_output, small, rel = final_pass(
            info, pieces, spot.shape[0], head_dim, total, width
        )
    else:
        picked = matmul_f32(placing_back, returned)
        mixed = (present[:, None] * (residual + picked)).astype(BF)
        expert_sums = grads_of([row_far], [cot_all[2]], expert_sums)
        grad_tokens = tail(outs[0], col_x, col_y, swap(outs[3], 3))
        more = [jnp.where(core == side, kept_more, sent_more) for side in range(2)]
        more = lax.psum(jnp.concatenate(more, axis=0), "exp")
        grad_output = lax.all_gather(more, "seq", tiled=True).astype(F32)
        halves = [
            jnp.where(core == side, kept_half, sent_half) for side in range(2)
        ]
        packed = lax.psum(jnp.concatenate(halves, axis=0), "exp")
        packed = lax.all_gather(packed, "seq").astype(F32)
        small, rel = jnp.sum(packed[:, 3 * group :], axis=0), packed[:, 3 * group + 2]
        dense = packed[:, : 3 * group].reshape(ways, heads_here, 3, head_dim, width)
        summed = [dense[:, :, kind].reshape(width, width).T for kind in range(3)]
    grad_gain_one, grad_gain_two, grad_router = small[0], small[1], small[3 : 3 + experts].T
    grad_rel = rel[:, : heads_here * buckets].reshape(heads, buckets).T
    return (
        mixed.reshape(seqs, block_len, width),
        grad_tokens.reshape(seqs, block_len, width),
        grad_gain_one,
        summed[0],
        summed[1],
        summed[2],
        grad_output,
        grad_rel,
        grad_gain_two,
        grad_router,
        expert_sums[0][None],
        expert_sums[1][None],
    )


def solution(mesh):
    in_specs = (
        P("exp", "seq", None),
        P("exp"),
        P("exp", "seq", None),
        P(),
        P(),
        P(),
        P(),
        P(),
        P(),
        P(),
        P(),
        P(),
        P("exp", None, None),
        P("exp", None, None),
        P("exp", "seq", None),
    )
    out_specs = (
        P("exp", "seq", None),
        P("exp", "seq", None),
        P(),
        P(),
        P(),
        P(),
        P(),
        P(),
        P(),
        P(),
        P("exp", None, "seq"),
        P("exp", "seq", None),
    )
    return jax.shard_map(
        on_device, mesh=mesh, in_specs=in_specs, out_specs=out_specs, check_vma=False
    )
```

```python
import functools

import jax
import jax.numpy as jnp
from jax import lax
from jax.experimental import pallas as pl
from jax.experimental.pallas import tpu as pltpu
from jax.sharding import PartitionSpec as P

EPS = 1e-06
NEG = -1e30
HIGH_PRECISION = lax.Precision.HIGHEST
LANES = 128
VMEM_BYTES = 60 * 1024 * 1024
SMALL_BYTES = 24 * 1024 * 1024
BF = jnp.bfloat16
F32 = jnp.float32


def matmul_f32(left, right):
    return jnp.dot(left, right, preferred_element_type=F32)


def dot_dims(left, right, left_dim, right_dim):
    return lax.dot_general(
        left, right, (((left_dim,), (right_dim,)), ((), ())), preferred_element_type=F32
    )


def rms_norm(values_in, gain):
    return (
        values_in * lax.rsqrt(jnp.mean(values_in * values_in, axis=-1, keepdims=True) + EPS) * gain
    )


def swap(value, bit):
    ways = lax.axis_size("seq")
    return lax.ppermute(value, "seq", [(i, i ^ bit) for i in range(ways)])


def trade(value, bits):
    peers = lax.axis_size("exp")
    return lax.ppermute(value, "exp", [(i, i ^ bits) for i in range(peers)])


def multi(start, step):
    return pl.multiple_of(start, step)


def norm_kernel(token_ref, gain_ref, out_ref):
    out_ref[...] = rms_norm(token_ref[...].astype(F32), gain_ref[...]).astype(BF)


def norm_rows(tokens, gain):
    seqs, block_len, width = tokens.shape
    block = pl.BlockSpec((1, block_len, width), lambda s: (s, 0, 0))
    return pl.pallas_call(
        norm_kernel,
        grid=(seqs,),
        in_specs=[block, pl.BlockSpec((1, 1, width), lambda s: (0, 0, 0))],
        out_specs=block,
        out_shape=jax.ShapeDtypeStruct(tokens.shape, BF),
        compiler_params=pltpu.CompilerParams(vmem_limit_bytes=SMALL_BYTES),
        name="norm_rows",
    )(tokens, gain)


def prep_kernel(group, info_ref, *refs):
    windows, row_ref = refs[:6], refs[6]
    weight_ref, base_ref, turned = refs[7:]
    offset = (info_ref[0] * group) % LANES
    for kind in range(3):
        left, right = windows[2 * kind][...], windows[2 * kind + 1][...]
        turned[...] = jnp.concatenate([left, right], axis=1).T
        weight_ref[kind] = turned[pl.ds(multi(offset, LANES // 2), group), :]
    for head in range(base_ref.shape[0]):
        row = row_ref[head]
        wide = jnp.broadcast_to(row, (LANES, row.shape[1]))
        base_ref[head] = pltpu.roll(wide, 0, 1, stride=1, stride_axis=0)


def prepare(info, weights, bias_rows, group):
    heads_here, _, wide = bias_rows.shape
    width = weights[0].shape[0]
    whole = lambda *shape: pl.BlockSpec(shape, lambda i, _: (0,) * len(shape))
    window = lambda side: pl.BlockSpec(
        (width, LANES), lambda i, info: (0, info[0] * group // LANES + side)
    )
    return pl.pallas_call(
        functools.partial(prep_kernel, group),
        grid_spec=pltpu.PrefetchScalarGridSpec(
            num_scalar_prefetch=1,
            grid=(1,),
            in_specs=[window(0), window(1)] * 3 + [whole(heads_here, 1, wide)],
            out_specs=(whole(3, group, width), whole(heads_here, LANES, wide)),
            scratch_shapes=[pltpu.VMEM((2 * LANES, width), BF)],
        ),
        out_shape=(
            jax.ShapeDtypeStruct((3, group, width), BF),
            jax.ShapeDtypeStruct((heads_here, LANES, wide), F32),
        ),
        compiler_params=pltpu.CompilerParams(vmem_limit_bytes=VMEM_BYTES),
        name="prepare",
    )(info, *[weight for weight in weights for _ in range(2)], bias_rows)


def forward_kernel(heads_here, head_dim, scale, seq_id, info_ref, *refs):
    own_ref, px_ref, py_ref, pd_ref, weight_ref, base_ref = refs[:6]
    outs = refs[6:10]
    probs_ref, q_ref, k_ref, v_ref, rows_ref, sum_ref, inverse_ref = refs[10:17]
    key_rows, value_cols, query_cols, mask_col, out_cols = refs[17:]
    me, length = info_ref[0], info_ref[4 + seq_id]
    head = pl.program_id(0)
    span = rows_ref.shape[0]
    block_len = own_ref.shape[0]
    group = heads_here * head_dim
    tiles = span // LANES
    width = weight_ref.shape[2]

    @pl.when(head == 0)
    def _():
        for step, piece in enumerate((own_ref, px_ref, py_ref, pd_ref)):
            start = multi((me ^ step) * block_len, block_len)
            rows_ref[pl.ds(start, block_len), :] = piece[...]
        rows = rows_ref[...]
        weights = weight_ref[...].reshape(3 * group, width)
        cols = dot_dims(weights, rows, 1, 1).astype(BF)
        spare = jnp.zeros((key_rows.shape[1] - group, width), BF)
        key_rows[...] = dot_dims(
            rows, jnp.concatenate([weight_ref[1], spare], axis=0), 1, 1
        ).astype(BF)
        v_ref[...] = dot_dims(
            rows, jnp.concatenate([weight_ref[2], spare], axis=0), 1, 1
        ).astype(BF)
        places = lax.broadcasted_iota(jnp.int32, (span, LANES), 0)
        mask_col[...] = jnp.where(places < length, 0.0, NEG)
        ones = (lax.broadcasted_iota(jnp.int32, (16, span), 0) == 0).astype(BF)
        for h in range(heads_here):
            lo, hi = h * head_dim, (h + 1) * head_dim
            q_ref[h] = (cols[lo:hi].astype(F32) * scale).astype(BF)
            k_ref[h] = cols[group + lo : group + hi]
            value_cols[h, :head_dim] = cols[2 * group + lo : 2 * group + hi]
            value_cols[h, head_dim:] = ones

    share = LANES // head_dim
    keys = key_rows[:, pl.ds(multi(head // share * LANES, LANES), LANES)]
    values = value_cols[head]
    query_cols[...] = jnp.zeros_like(query_cols)
    query_cols[pl.ds(multi(head % share * head_dim, head_dim), head_dim), :] = q_ref[head]
    mask = jnp.concatenate([mask_col[...]] * (block_len // LANES), axis=1)
    for c in range(span // block_len):
        cols = slice(c * block_len, (c + 1) * block_len)
        first = c * block_len // LANES + tiles - 1
        bias = jnp.concatenate(
            [
                base_ref[0, :, (first - a) * LANES : (first - a) * LANES + block_len]
                for a in range(tiles)
            ],
            axis=0,
        )
        scores = dot_dims(keys, query_cols[:, cols], 1, 0) + bias + mask
        top = jnp.max(scores, axis=0, keepdims=True)
        probs_ref[0, :, cols] = jnp.exp(scores - top).astype(BF)
    result = dot_dims(values, probs_ref[0], 1, 0)
    inverse = 1.0 / result[head_dim : head_dim + 1]
    inverse_ref[0] = inverse
    result = result[:head_dim] * inverse
    sum_ref[0] = result
    out_cols[...] = result.astype(BF)
    for step, ref in enumerate(outs):
        ref[...] = out_cols[:, pl.ds(multi((me ^ step) * block_len, block_len), block_len)]


def attention_forward(info, own, px, py, diag, seq_id, weights, base):
    _, block_len, width = own.shape
    _, group, _ = weights.shape
    heads_here, _, wide = base.shape
    head_dim = group // heads_here
    span = 4 * block_len
    lanes = -(-group // LANES) * LANES
    piece = pl.BlockSpec((None, block_len, width), lambda h, _: (seq_id, 0, 0))
    full = lambda *shape: pl.BlockSpec(shape, lambda h, _: (0,) * len(shape))
    out_shape = (
        *[jax.ShapeDtypeStruct((group, block_len), BF)] * 4,
        jax.ShapeDtypeStruct((heads_here, span, span), BF),
        jax.ShapeDtypeStruct((heads_here, head_dim, span), BF),
        jax.ShapeDtypeStruct((heads_here, head_dim, span), BF),
        jax.ShapeDtypeStruct((span, lanes), BF),
        jax.ShapeDtypeStruct((span, width), BF),
        jax.ShapeDtypeStruct((heads_here, head_dim, span), F32),
        jax.ShapeDtypeStruct((heads_here, 1, span), F32),
    )
    return pl.pallas_call(
        functools.partial(forward_kernel, heads_here, head_dim, head_dim ** (-0.5), seq_id),
        grid_spec=pltpu.PrefetchScalarGridSpec(
            num_scalar_prefetch=1,
            grid=(heads_here,),
            in_specs=[
                piece,
                piece,
                piece,
                full(block_len, width),
                full(3, group, width),
                pl.BlockSpec((1, LANES, wide), lambda h, _: (h, 0, 0)),
            ],
            out_specs=(
                *[pl.BlockSpec((head_dim, block_len), lambda h, _: (h, 0))] * 4,
                pl.BlockSpec((1, span, span), lambda h, _: (h, 0, 0)),
                full(heads_here, head_dim, span),
                full(heads_here, head_dim, span),
                full(span, lanes),
                full(span, width),
                pl.BlockSpec((1, head_dim, span), lambda h, _: (h, 0, 0)),
                pl.BlockSpec((1, 1, span), lambda h, _: (h, 0, 0)),
            ),
            scratch_shapes=[
                pltpu.VMEM((span, lanes), BF),
                pltpu.VMEM((heads_here, head_dim + 16, span), BF),
                pltpu.VMEM((LANES, span), BF),
                pltpu.VMEM((span, LANES), F32),
                pltpu.VMEM((head_dim, span), BF),
            ],
        ),
        out_shape=out_shape,
        compiler_params=pltpu.CompilerParams(vmem_limit_bytes=VMEM_BYTES),
        cost_estimate=pl.CostEstimate(
            flops=6 * heads_here * span * span * 256 * 2,
            bytes_accessed=heads_here * span * span * 2,
            transcendentals=heads_here * span * span,
        ),
        name="attention_forward",
    )(info, own, px, py, diag, weights, base)


def middle_kernel(seqs, info_ref, *refs):
    pieces = refs[: 4 * seqs]
    token_ref, output_ref, gain_ref, place_ref = refs[4 * seqs : 4 * seqs + 4]
    sum_ref, sent_ref, cols_ref = refs[4 * seqs + 4 :]
    me = info_ref[0]
    group, block_len = pieces[0].shape
    for s in range(seqs):
        for step in range(4):
            start = multi((me ^ step) * group, 64)
            cols_ref[pl.ds(start, group), s * block_len : (s + 1) * block_len] = pieces[
                4 * s + step
            ][...]
    residual = token_ref[...].astype(F32) + dot_dims(cols_ref[...], output_ref[...], 0, 0)
    sum_ref[...] = residual
    routed = rms_norm(residual, gain_ref[...]).astype(BF)
    sent_ref[...] = matmul_f32(place_ref[...], routed).astype(BF)


def middle_forward(info, pieces, tokens, w_output, gain, placing):
    rows, width = tokens.shape
    slots = placing.shape[0]
    return pl.pallas_call(
        functools.partial(middle_kernel, len(pieces) // 4),
        in_specs=[pl.BlockSpec(memory_space=pltpu.SMEM)]
        + [pl.BlockSpec(memory_space=pltpu.VMEM)] * (len(pieces) + 4),
        out_shape=(
            jax.ShapeDtypeStruct((rows, width), F32),
            jax.ShapeDtypeStruct((slots, width), BF),
            jax.ShapeDtypeStruct((width, rows), BF),
        ),
        compiler_params=pltpu.CompilerParams(vmem_limit_bytes=VMEM_BYTES),
        name="middle_forward",
    )(info, *pieces, tokens, w_output, gain, placing)


def turn_kernel(counts, seqs, info_ref, *refs):
    pieces = refs[: len(counts)]
    back_ref, sum_ref, gain_ref, cot_ref, here_ref, output_ref, attended_ref = refs[
        len(counts) : len(counts) + 7
    ]
    x_ref, grad_out, gain_out, *outs = refs[len(counts) + 7 : len(counts) + 14]
    rows_all, cols = refs[len(counts) + 14 :]
    me = info_ref[0]
    start = 0
    for piece, count in zip(pieces, counts, strict=True):
        rows_all[start : start + count, :] = piece[:count, :]
        start += count
    grads = matmul_f32(back_ref[...], rows_all[...])
    values, gain = sum_ref[...], gain_ref[...]
    root = lax.rsqrt(jnp.mean(values * values, axis=1, keepdims=True) + EPS)
    scaled = values * root
    gain_out[...] = jnp.sum(grads * scaled, axis=0, keepdims=True)
    grads = grads * gain
    inner = jnp.mean(grads * scaled, axis=1, keepdims=True)
    grad_x = cot_ref[...].astype(F32) * here_ref[...] + root * (grads - scaled * inner)
    x_ref[...] = grad_x
    branch = grad_x.astype(BF)
    grad_out[...] = matmul_f32(attended_ref[...], branch).astype(BF)
    cols[...] = dot_dims(output_ref[...], branch, 1, 1).astype(BF)
    _, group, block_len = outs[0].shape
    for step, out in enumerate(outs):
        start = multi((me ^ step) * group, 64)
        for s in range(seqs):
            out[s] = cols[pl.ds(start, group), s * block_len : (s + 1) * block_len]


def turn_back(
    info, pieces, counts, placing_back, residual, gain, cotangent, present, w_output, attended, seqs
):
    rows, width = residual.shape
    out = jax.ShapeDtypeStruct((seqs, width // 4, rows // seqs), BF)
    return pl.pallas_call(
        functools.partial(turn_kernel, counts, seqs),
        in_specs=[pl.BlockSpec(memory_space=pltpu.SMEM)]
        + [pl.BlockSpec(memory_space=pltpu.VMEM)] * (len(pieces) + 7),
        out_shape=(
            jax.ShapeDtypeStruct((rows, width), F32),
            jax.ShapeDtypeStruct((width, width), BF),
            jax.ShapeDtypeStruct((1, width), F32),
            out,
            out,
            out,
            out,
        ),
        scratch_shapes=[
            pltpu.VMEM((sum(counts), width), BF),
            pltpu.VMEM((width, rows), BF),
        ],
        compiler_params=pltpu.CompilerParams(vmem_limit_bytes=VMEM_BYTES),
        name="turn_back",
    )(info, *pieces, placing_back, residual, gain, cotangent, present, w_output, attended)


def backward_kernel(seqs, scale, experts, info_ref, *refs):
    pieces = refs[:4]
    groups = refs[4 : 4 + 7 * seqs]
    own_ref, lookup_ref, gain_ref, gain_two_ref, router_ref = refs[4 + 7 * seqs : 9 + 7 * seqs]
    outs = refs[9 + 7 * seqs : 13 + 7 * seqs]
    kept_ref, sent_ref, grad_cols, rel_sum, out_cols, weight_sum, packed, gain_sum, folds = refs[
        13 + 7 * seqs : 22 + 7 * seqs
    ]
    wide_cols, scores_all = refs[22 + 7 * seqs :]
    head, heads = pl.program_id(0), pl.num_programs(0)
    me = info_ref[0]
    head_dim, span = grad_cols.shape
    block_len = span // 4
    tiles = span // LANES
    rel_sum[...] = jnp.zeros_like(rel_sum)
    share = LANES // head_dim
    half = multi(head % share * head_dim, head_dim)
    wide_cols[...] = jnp.zeros_like(wide_cols)
    for s in range(seqs):
        probs_ref, q_ref, k_ref, v_ref, rows_ref, sum_ref, inverse_ref = groups[7 * s : 7 * s + 7]
        for step, piece in enumerate(pieces):
            start = multi((me ^ step) * block_len, block_len)
            grad_cols[:, pl.ds(start, block_len)] = piece[s]
        grads = (grad_cols[...].astype(F32) * inverse_ref[0]).astype(BF)
        inner = jnp.sum(grads.astype(F32) * sum_ref[0], axis=0, keepdims=True)
        wide_cols[pl.ds(half, head_dim), :] = grads
        values = v_ref[...]
        for c in range(span // block_len):
            cols = slice(c * block_len, (c + 1) * block_len)
            first = c * block_len // LANES + tiles - 1
            grad_probs = dot_dims(values, wide_cols[:, cols], 1, 0)
            grad_scores = probs_ref[0, :, cols].astype(F32) * (grad_probs - inner[:, cols])
            for a in range(tiles):
                spot = slice((first - a) * LANES, (first - a) * LANES + block_len)
                rel_sum[:, spot] += grad_scores[a * LANES : (a + 1) * LANES]
            scores_all[:, cols] = grad_scores.astype(BF)
        low = scores_all[...]
        out_cols[0] = (dot_dims(k_ref[0], low, 1, 0) * scale).astype(BF)
        out_cols[1] = matmul_f32(low, q_ref[0].T).astype(BF).T
        out_cols[2] = matmul_f32(probs_ref[0], grads.T).astype(BF).T
        rows = rows_ref[...]
        for kind in range(3):
            product = matmul_f32(out_cols[kind], rows)
            if s == 0:
                weight_sum[kind] = product
            else:
                weight_sum[kind] += product
        for step, out in enumerate(outs):
            start = multi((me ^ step) * block_len, block_len)
            for kind in range(3):
                out[s, kind] = out_cols[kind, :, pl.ds(start, block_len)]
    fold = rel_sum[...]
    wide = fold.shape[1]
    half = LANES // 2
    while half >= 1:
        fold = fold[:half] + pltpu.roll(fold[half:], wide - half, 1)
        half //= 2
    sums = weight_sum[...]
    for kind in range(3):
        start = multi((3 * head + kind) * head_dim, head_dim)
        packed[pl.ds(start, head_dim), :] = sums[kind].astype(BF)

    @pl.when(head == 0)
    def _():
        gain_sum[...] = jnp.zeros_like(gain_sum)
        folds[...] = jnp.zeros_like(folds)

    gain_sum[...] += jnp.sum(own_ref[...].astype(F32) * sums, axis=(0, 1))[None]
    folds[pl.ds(head, 1), :] = fold

    @pl.when(head == heads - 1)
    def _():
        count = weight_sum.shape[2] // (4 * head_dim)
        buckets, width = lookup_ref.shape[0], packed.shape[1]
        rel = lax.dot_general(
            folds[...],
            lookup_ref[...],
            (((1,), (1,)), ((), ())),
            precision=HIGH_PRECISION,
            preferred_element_type=F32,
        )
        rel_row = jnp.concatenate([rel[h : h + 1] for h in range(count)], axis=1)
        rel_row = jnp.pad(rel_row, ((0, 0), (0, width - count * buckets)))
        small = [gain_sum[...] / gain_ref[...], gain_two_ref[...], rel_row, router_ref[:experts]]
        small = jnp.concatenate(small, axis=0)
        start = 3 * count * head_dim
        spare = packed.shape[0] - start - small.shape[0]
        packed[start:, :] = jnp.pad(small, ((0, spare), (0, 0))).astype(BF)
        half, core = packed.shape[0] // 2, info_ref[2]
        kept_ref[...] = packed[pl.ds(multi(core * half, 16), half), :]
        sent_ref[...] = packed[pl.ds(multi((1 - core) * half, 16), half), :]


def attention_backward(
    info, pieces, saved, own_weights, lookup, gain_one, gain_two_row, router_rows, experts
):
    seqs = len(saved)
    heads, head_dim, span = saved[0][1].shape
    width = saved[0][4].shape[1]
    block_len = span // 4
    total = 3 * heads * head_dim + -(-(3 + experts) // 64) * 64
    per_head = lambda *shape: pl.BlockSpec((1,) + shape, lambda h, _: (h,) + (0,) * len(shape))
    whole = lambda *shape: pl.BlockSpec(shape, lambda h, _: (0,) * len(shape))
    group_specs = [
        per_head(span, span),
        per_head(head_dim, span),
        per_head(head_dim, span),
        pl.BlockSpec((span, LANES), lambda h, _: (0, h // (LANES // head_dim))),
        whole(span, width),
        per_head(head_dim, span),
        per_head(1, span),
    ]
    out_spec = pl.BlockSpec((seqs, 3, head_dim, block_len), lambda h, _: (0, 0, h, 0))
    out_type = jax.ShapeDtypeStruct((seqs, 3, heads * head_dim, block_len), BF)
    half_type = jax.ShapeDtypeStruct((total // 2, width), BF)
    return pl.pallas_call(
        functools.partial(backward_kernel, seqs, head_dim ** (-0.5), experts),
        grid_spec=pltpu.PrefetchScalarGridSpec(
            num_scalar_prefetch=1,
            grid=(heads,),
            in_specs=[pl.BlockSpec((seqs, head_dim, block_len), lambda h, _: (0, h, 0))] * 4
            + group_specs * seqs
            + [
                pl.BlockSpec((3, head_dim, width), lambda h, _: (0, h, 0)),
                whole(*lookup.shape),
                whole(1, width),
                whole(1, width),
                whole(*router_rows.shape),
            ],
            out_specs=[out_spec] * 4 + [whole(*half_type.shape)] * 2,
            scratch_shapes=[
                pltpu.VMEM((head_dim, span), BF),
                pltpu.VMEM((LANES, 2 * span), F32),
                pltpu.VMEM((3, head_dim, span), BF),
                pltpu.VMEM((3, head_dim, width), F32),
                pltpu.VMEM((total, width), BF),
                pltpu.VMEM((1, width), F32),
                pltpu.VMEM((8, 2 * span), F32),
                pltpu.VMEM((LANES, span), BF),
                pltpu.VMEM((span, span), BF),
            ],
        ),
        out_shape=[out_type] * 4 + [half_type] * 2,
        compiler_params=pltpu.CompilerParams(vmem_limit_bytes=VMEM_BYTES),
        cost_estimate=pl.CostEstimate(
            flops=8 * seqs * heads * span * span * 256 * 2,
            bytes_accessed=seqs * heads * span * span * 2,
            transcendentals=0,
        ),
        name="attention_backward",
    )(
        info,
        *pieces,
        *[array for group in saved for array in group],
        own_weights,
        lookup,
        gain_one,
        gain_two_row,
        router_rows,
    )


def mix_kernel(info_ref, *refs):
    pieces, (other_ref, back_ref, sum_ref, here_ref, out_ref, rows_all) = refs[:-6], refs[-6:]
    rows = pieces[0].shape[0] // 2
    core, chip = info_ref[2], info_ref[3]
    for k, piece in enumerate(pieces):
        base = (chip ^ k) * 2
        own = piece[pl.ds(multi(core * rows, 16), rows), :]
        rows_all[pl.ds(multi((base + core) * rows, 16), rows), :] = own
        start = other_ref.shape[0] - (len(pieces) - k) * rows
        other = other_ref[start : start + rows, :]
        rows_all[pl.ds(multi((base + 1 - core) * rows, 16), rows), :] = other
    picked = matmul_f32(back_ref[...], rows_all[...])
    out_ref[...] = (here_ref[...] * (sum_ref[...] + picked)).astype(BF)


def mix_rows(info, pieces, other, placing_back, residual, present):
    rows, width = residual.shape
    return pl.pallas_call(
        mix_kernel,
        in_specs=[pl.BlockSpec(memory_space=pltpu.SMEM)]
        + [pl.BlockSpec(memory_space=pltpu.VMEM)] * (len(pieces) + 4),
        out_shape=jax.ShapeDtypeStruct((rows, width), BF),
        scratch_shapes=[pltpu.VMEM((len(pieces) * pieces[0].shape[0], width), BF)],
        compiler_params=pltpu.CompilerParams(vmem_limit_bytes=VMEM_BYTES),
        name="mix_rows",
    )(info, *pieces, other, placing_back, residual, present)


def gather_sum_kernel(info_ref, parts_ref, *refs):
    *pieces, kept_ref, sent_ref, total = refs
    total[...] = jnp.sum(parts_ref[...].astype(F32), axis=0)
    rows, core = kept_ref.shape[0], info_ref[2]
    kept_ref[...] = total[pl.ds(multi(core * rows, 8), rows), :].astype(BF)
    sent_ref[:rows, :] = total[pl.ds(multi((1 - core) * rows, 8), rows), :].astype(BF)
    for piece in pieces:
        count = piece.shape[0] // 2
        sent_ref[rows : rows + count, :] = piece[pl.ds(multi((1 - core) * count, 16), count), :]
        rows += count


def gather_sum(info, parts, pieces):
    _, rows, width = parts.shape
    more = sum(piece.shape[0] // 2 for piece in pieces)
    return pl.pallas_call(
        gather_sum_kernel,
        in_specs=[pl.BlockSpec(memory_space=pltpu.SMEM)]
        + [pl.BlockSpec(memory_space=pltpu.VMEM)] * (1 + len(pieces)),
        out_shape=(
            jax.ShapeDtypeStruct((rows // 2, width), BF),
            jax.ShapeDtypeStruct((rows // 2 + more, width), BF),
        ),
        scratch_shapes=[pltpu.VMEM((rows, width), F32)],
        compiler_params=pltpu.CompilerParams(vmem_limit_bytes=SMALL_BYTES),
        name="gather_sum",
    )(info, parts, *pieces)


def split_kernel(info_ref, kept_ref, other_ref, kept_more_ref, other_more_ref, *refs):
    *outs, half, more = refs
    chip = info_ref[3]
    half[...] = (kept_ref[...].astype(F32) + other_ref[...].astype(F32)).astype(BF)
    other_more = other_more_ref[: more.shape[0], :]
    more[...] = kept_more_ref[...].astype(F32) + other_more.astype(F32)
    rows, small = half.shape[0] // len(outs), more.shape[0] // len(outs)
    for k, out in enumerate(outs):
        out[:rows, :] = half[pl.ds(multi((chip ^ k) * rows, 16), rows), :]
        extra = more[pl.ds(multi((chip ^ k) * small, 8), small), :]
        spare = out.shape[0] - rows - small
        out[rows:, :] = jnp.pad(extra, ((0, spare), (0, 0))).astype(BF)


def split_sum(info, kept, other, kept_more, other_more, chips):
    rows, width = kept.shape
    small = kept_more.shape[0]
    out = jax.ShapeDtypeStruct((rows // chips + -(-small // chips // 16) * 16, width), BF)
    return pl.pallas_call(
        split_kernel,
        in_specs=[pl.BlockSpec(memory_space=pltpu.SMEM)]
        + [pl.BlockSpec(memory_space=pltpu.VMEM)] * 4,
        out_shape=(out,) * chips,
        scratch_shapes=[pltpu.VMEM((rows, width), BF), pltpu.VMEM((small, width), F32)],
        compiler_params=pltpu.CompilerParams(vmem_limit_bytes=SMALL_BYTES),
        name="split_sum",
    )(info, kept, other, kept_more, other_more)


def tail_kernel(heads, seqs, info_ref, *refs):
    pieces = refs[: 4 * len(heads)]
    *weights, token_ref, gain_ref, x_ref, out_ref, cols = refs[4 * len(heads) :]
    me = info_ref[0]
    _, width, rows = cols.shape
    block_len, group = rows // seqs, width // 4
    offset = 0
    for part, count in enumerate(heads):
        for step in range(4):
            piece = pieces[4 * part + step]
            start = multi((me ^ step) * group + offset, 64)
            for s in range(seqs):
                for kind in range(3):
                    cols[
                        kind, pl.ds(start, count), s * block_len : (s + 1) * block_len
                    ] = piece[s, kind]
        offset += count
    turned = sum(matmul_f32(weights[kind][...], cols[kind]) for kind in range(3))
    values = token_ref[...].astype(F32)
    root = lax.rsqrt(jnp.mean(values * values, axis=1, keepdims=True) + EPS)
    scaled = values * root
    grads = turned.T * gain_ref[...]
    inner = jnp.mean(grads * scaled, axis=1, keepdims=True)
    out_ref[...] = x_ref[...] + root * (grads - scaled * inner)


def tail_pass(info, pieces, heads, weights, tokens, gain, grad_x, seqs):
    rows, width = tokens.shape
    return pl.pallas_call(
        functools.partial(tail_kernel, heads, seqs),
        in_specs=[pl.BlockSpec(memory_space=pltpu.SMEM)]
        + [pl.BlockSpec(memory_space=pltpu.VMEM)] * (len(pieces) + 6),
        out_shape=jax.ShapeDtypeStruct((rows, width), F32),
        scratch_shapes=[pltpu.VMEM((3, width, rows), BF)],
        compiler_params=pltpu.CompilerParams(vmem_limit_bytes=VMEM_BYTES),
        name="tail_pass",
    )(info, *pieces, *weights, tokens, gain, grad_x)


def gelu_both(pre):
    square = pre * pre
    curve = jnp.tanh(pre * (0.7978845608028654 + 0.035677408136300125 * square))
    half = 0.5 + 0.5 * curve
    slope = half + pre * (0.5 - 0.5 * curve * curve) * (
        0.7978845608028654 + 0.10703222440890037 * square
    )
    return pre * half, slope


def router_prob(rows, router, experts):
    logits = matmul_f32(rows, router)
    lanes = lax.broadcasted_iota(jnp.int32, logits.shape, 1)
    logits = jnp.where(lanes < experts, logits, NEG)
    powers = jnp.exp(logits - jnp.max(logits, axis=1, keepdims=True))
    return powers / jnp.sum(powers, axis=1, keepdims=True), lanes


def expert_kernel(experts, parts, counts, mine_ref, *refs):
    row_refs, grad_refs = refs[:parts], refs[parts : 2 * parts]
    router_ref, first_ref, second_ref = refs[2 * parts : 2 * parts + 3]
    refs = refs[2 * parts + 3 :]
    back_ref, mixed_refs = refs[0], refs[1 : 1 + len(counts)]
    router_grad_ref, rows_all, grads_all, made_all, prob_all, out_sum, back_sum, mixed = refs[
        1 + len(counts) :
    ]
    step, steps = pl.program_id(0), pl.num_programs(0)

    @pl.when(step == 0)
    def _():
        start = 0
        for row_ref, grad_ref in zip(row_refs, grad_refs, strict=True):
            rows_all[start : start + row_ref.shape[0], :] = row_ref[...]
            grads_all[start : start + row_ref.shape[0], :] = grad_ref[...]
            start += row_ref.shape[0]
        prob, lanes = router_prob(rows_all[...], router_ref[...], experts)
        prob_all[...] = prob
        is_mine = lanes == mine_ref[1]
        gate = experts * jnp.sum(jnp.where(is_mine, prob, 0.0), axis=1, keepdims=True)
        made_all[...] = (gate * grads_all[...].astype(F32)).astype(BF)
        out_sum[...] = jnp.zeros_like(out_sum)
        back_sum[...] = jnp.zeros_like(back_sum)

    first, second = first_ref[...], second_ref[...]
    pre = matmul_f32(rows_all[...], first)
    grad_hidden = dot_dims(made_all[...], second, 1, 1)
    hidden, slope = gelu_both(pre)
    out_sum[...] += matmul_f32(hidden.astype(BF), second)
    back_sum[...] += dot_dims((grad_hidden * slope).astype(BF), first, 1, 1)

    @pl.when(step == steps - 1)
    def _():
        prob = prob_all[...]
        is_mine = lax.broadcasted_iota(jnp.int32, prob.shape, 1) == mine_ref[1]
        prob_mine = jnp.sum(jnp.where(is_mine, prob, 0.0), axis=1, keepdims=True)
        expert_out = out_sum[...].astype(BF).astype(F32)
        upper = experts * jnp.sum(grads_all[...].astype(F32) * expert_out, axis=1, keepdims=True)
        inner = prob_mine * upper
        grad_logits = (prob * (jnp.where(is_mine, upper, 0.0) - inner)).astype(BF)
        back = back_sum[...] + dot_dims(grad_logits, router_ref[...], 1, 1)
        back_ref[...] = back.astype(BF)
        mixed[...] = (experts * prob_mine * expert_out).astype(BF)
        if len(counts) == 1:
            mixed_refs[0][...] = mixed[...]
        else:
            for k, (count, ref) in enumerate(zip(counts, mixed_refs, strict=True)):
                start = multi((mine_ref[3] ^ k) * count, 16)
                ref[...] = mixed[pl.ds(start, count), :]
        router_grad_ref[...] = dot_dims(grad_logits, rows_all[...], 0, 0)


def expert_pass(mine, experts, row_parts, grad_parts, counts, router, first, second):
    width, hidden_width = first.shape
    total = sum(counts)
    tile = hidden_width // 3
    whole = lambda *shape: pl.BlockSpec(shape, lambda f, _: (0,) * len(shape))
    part_specs = [whole(*part.shape) for part in row_parts]
    piece_specs = [whole(count, width) for count in counts]
    piece_shapes = [jax.ShapeDtypeStruct((count, width), BF) for count in counts]
    return pl.pallas_call(
        functools.partial(expert_kernel, experts, len(row_parts), counts),
        grid_spec=pltpu.PrefetchScalarGridSpec(
            num_scalar_prefetch=1,
            grid=(hidden_width // tile,),
            in_specs=part_specs * 2
            + [
                whole(width, LANES),
                pl.BlockSpec((width, tile), lambda f, _: (0, f)),
                pl.BlockSpec((tile, width), lambda f, _: (f, 0)),
            ],
            out_specs=[whole(total, width)] + piece_specs + [whole(LANES, width)],
            scratch_shapes=[
                pltpu.VMEM((total, width), BF),
                pltpu.VMEM((total, width), BF),
                pltpu.VMEM((total, width), BF),
                pltpu.VMEM((total, LANES), F32),
                pltpu.VMEM((total, width), F32),
                pltpu.VMEM((total, width), F32),
                pltpu.VMEM((total, width), BF),
            ],
        ),
        out_shape=[jax.ShapeDtypeStruct((total, width), BF)]
        + piece_shapes
        + [jax.ShapeDtypeStruct((LANES, width), F32)],
        compiler_params=pltpu.CompilerParams(vmem_limit_bytes=VMEM_BYTES),
        cost_estimate=pl.CostEstimate(
            flops=8 * total * width * hidden_width,
            bytes_accessed=4 * width * hidden_width,
            transcendentals=total * hidden_width,
        ),
        name="expert_pass",
    )(mine, *row_parts, *grad_parts, router, first, second)


def grads_kernel(experts, parts, prior, info_ref, *refs):
    row_refs, grad_refs = refs[:parts], refs[parts : 2 * parts]
    router_ref, first_ref, second_ref = refs[2 * parts : 2 * parts + 3]
    refs = refs[2 * parts + 3 :]
    if prior:
        (prior_first, prior_second), refs = refs[:2], refs[2:]
    grad_first, grad_second, rows_all, rows_t, made_all, hidden_all, pre_all = refs
    count = row_refs[0].shape[0]

    @pl.when(pl.program_id(0) == 0)
    def _():
        for part in range(parts):
            spot = slice(part * count, (part + 1) * count)
            rows = row_refs[part][...]
            prob, lanes = router_prob(rows, router_ref[...], experts)
            gate = experts * jnp.sum(
                jnp.where(lanes == info_ref[1], prob, 0.0), axis=1, keepdims=True
            )
            made_all[spot, :] = (gate * grad_refs[part][...].astype(F32)).astype(BF)
            rows_all[spot, :] = rows
        rows_t[...] = rows_all[...].T

    first, second = first_ref[...], second_ref[...]
    for part in range(parts):
        spot = slice(part * count, (part + 1) * count)
        pre = matmul_f32(row_refs[part][...], first)
        grad_hidden = dot_dims(made_all[spot, :], second, 1, 1)
        hidden, slope = gelu_both(pre)
        hidden_all[spot, :] = hidden.astype(BF)
        pre_all[spot, :] = (grad_hidden * slope).astype(BF)
    own_first = matmul_f32(rows_t[...], pre_all[...])
    own_second = dot_dims(hidden_all[...], made_all[...], 0, 0)
    if prior:
        own_first = own_first + prior_first[...]
        own_second = own_second + prior_second[...]
    grad_first[...] = own_first
    grad_second[...] = own_second


def expert_grads(info, experts, row_parts, grad_parts, router, first, second, prior):
    width, hidden_width = first.shape
    own = hidden_width // 4
    tile = 256
    tiles = own // tile
    total = sum(part.shape[0] for part in row_parts)
    whole = lambda *shape: pl.BlockSpec(shape, lambda t, _: (0,) * len(shape))
    part_specs = [whole(*part.shape) for part in row_parts]
    out_specs = [
        pl.BlockSpec((width, tile), lambda t, _: (0, t)),
        pl.BlockSpec((tile, width), lambda t, _: (t, 0)),
    ]
    return pl.pallas_call(
        functools.partial(grads_kernel, experts, len(row_parts), len(prior) > 0),
        grid_spec=pltpu.PrefetchScalarGridSpec(
            num_scalar_prefetch=1,
            grid=(tiles,),
            in_specs=part_specs * 2
            + [
                whole(width, LANES),
                pl.BlockSpec((width, tile), lambda t, info: (0, info[0] * tiles + t)),
                pl.BlockSpec((tile, width), lambda t, info: (info[0] * tiles + t, 0)),
            ]
            + out_specs[: len(prior)],
            out_specs=out_specs,
            scratch_shapes=[
                pltpu.VMEM((total, width), BF),
                pltpu.VMEM((width, total), BF),
                pltpu.VMEM((total, width), BF),
                pltpu.VMEM((total, tile), BF),
                pltpu.VMEM((total, tile), BF),
            ],
        ),
        out_shape=(
            jax.ShapeDtypeStruct((width, own), F32),
            jax.ShapeDtypeStruct((own, width), F32),
        ),
        compiler_params=pltpu.CompilerParams(vmem_limit_bytes=VMEM_BYTES),
        cost_estimate=pl.CostEstimate(
            flops=total * width,
            bytes_accessed=total * width // 64,
            transcendentals=0,
        ),
        name="expert_grads",
    )(info, *row_parts, *grad_parts, router, first, second, *prior)


def final_kernel(rows, head_dim, info_ref, *refs):
    pieces = refs[:10]
    query_ref, key_ref, value_ref, output_ref, small_ref, rel_ref, whole = refs[10:]
    me, core, chip = info_ref[0], info_ref[2], info_ref[3]
    each = whole.shape[1] // 8
    step_rows = output_ref.shape[0] // 32
    chips = pieces[0].shape[0] // rows
    for other in range(2):
        for step, first, ref in zip(
            (0, 1, 2, 3, 3), (0, 0, 0, 0, chips // 2), pieces[5 * other : 5 * other + 5], strict=True
        ):
            for i in range(ref.shape[0] // rows):
                c, z = me ^ step, chip ^ (first + i)
                spot = ((core ^ other) * chips + z) * each
                whole[c, pl.ds(multi(spot, 16), each), :] = ref[i * rows : i * rows + each, :]
                tail = ref[i * rows + each : (i + 1) * rows, :].astype(F32)
                spot = ((c * 2 + (core ^ other)) * chips + z) * step_rows
                output_ref[pl.ds(multi(spot, 8), step_rows), :] = tail[:step_rows]
    heads = query_ref.shape[0] // (4 * head_dim)
    for kind, ref in enumerate((query_ref, key_ref, value_ref)):
        joined = [
            whole[c, (3 * h + kind) * head_dim : (3 * h + kind + 1) * head_dim, :]
            for c in range(4)
            for h in range(heads)
        ]
        ref[...] = jnp.concatenate(joined, axis=0).astype(F32).T
    small = whole[:, 3 * heads * head_dim :, :].astype(F32)
    small_ref[...] = jnp.sum(small, axis=0)
    rel_ref[...] = small[:, 2, :]


def final_pass(info, pieces, rows, head_dim, total, width):
    square = jax.ShapeDtypeStruct((width, width), F32)
    extra = total - 3 * (width // 4)
    return pl.pallas_call(
        functools.partial(final_kernel, rows, head_dim),
        in_specs=[pl.BlockSpec(memory_space=pltpu.SMEM)]
        + [pl.BlockSpec(memory_space=pltpu.VMEM)] * len(pieces),
        out_shape=(
            square,
            square,
            square,
            square,
            jax.ShapeDtypeStruct((extra, width), F32),
            jax.ShapeDtypeStruct((4, width), F32),
        ),
        scratch_shapes=[pltpu.VMEM((4, total, width), BF)],
        compiler_params=pltpu.CompilerParams(vmem_limit_bytes=SMALL_BYTES),
        name="final_pass",
    )(info, *pieces)


def on_device(
    tokens,
    lengths,
    routes,
    bucket_table,
    gain_one,
    w_query,
    w_key,
    w_value,
    w_output,
    rel_bias,
    gain_two,
    w_router,
    w_in,
    w_out,
    cotangent,
):
    seqs, block_len, width = tokens.shape
    buckets, heads = rel_bias.shape
    experts = w_router.shape[1]
    ways = lax.axis_size("seq")
    me = lax.axis_index("seq")
    mine = lax.axis_index("exp")
    span = block_len * ways
    group = width // ways
    heads_here = heads // ways
    total_rows = seqs * block_len
    capacity = (5 * total_rows + 4 * experts - 1) // (4 * experts)

    peers = lax.axis_size("exp")
    chips = peers // 2
    paired = peers == 8
    core, chip = mine % 2, mine // 2

    normed = norm_rows(tokens, gain_one[None, None])
    px, py = swap(normed, 1), swap(normed, 2)

    positions = me * block_len + jnp.arange(block_len, dtype=jnp.int32)
    present = (positions[None, :] < lengths[:, None]).astype(F32).reshape(total_rows)
    routed = routes.reshape(total_rows)
    chosen = (routed[:, None] == jnp.arange(experts, dtype=jnp.int32)[None, :]).astype(F32)
    live_hits = chosen * present[:, None]
    row_ids = jnp.arange(total_rows, dtype=jnp.int32)
    lower = (row_ids[:, None] >= row_ids[None, :]).astype(BF)
    running = matmul_f32(lower, live_hits.astype(BF))
    slot_index = jnp.sum(live_hits * (running - 1.0), axis=-1)
    kept = present * (slot_index < capacity).astype(F32)
    destin = routed.astype(F32) * capacity + slot_index
    slot_ids = jnp.arange(experts * capacity, dtype=jnp.int32).astype(F32)
    placing = ((destin[None, :] == slot_ids[:, None]) & (kept[None, :] > 0)).astype(BF)
    placing_back = placing.T
    cotangent_rows = cotangent.reshape(total_rows, width)

    def exchange(rows):
        sent = rows.reshape(experts, capacity, width)
        return lax.all_to_all(sent, "exp", split_axis=0, concat_axis=0, tiled=True).reshape(
            experts * capacity, width
        )


    wide = 2 * span
    padded = jnp.concatenate([bucket_table, jnp.full((1,), -1, jnp.int32)])
    turned = jnp.roll(jnp.flip(padded), -LANES)
    lookup = (jnp.arange(buckets, dtype=jnp.int32)[:, None] == turned[None, :]).astype(F32)
    own_bias = lax.dynamic_slice_in_dim(rel_bias, me * heads_here, heads_here, 1)
    bias_rows = jnp.dot(own_bias.T, lookup, precision=HIGH_PRECISION)
    info = jnp.concatenate([jnp.stack([me, mine, core, chip]), lengths])
    own_weights, base = prepare(info, (w_query, w_key, w_value), bias_rows[:, None, :], group)

    held, _ = lax.optimization_barrier((cotangent_rows, own_weights))
    px, py, own_weights, base = lax.optimization_barrier((px, py, own_weights, base))
    diagonals = (swap(px[:1], 2), swap(py[1:], 1))
    cot_rows = exchange(matmul_f32(placing, held).astype(BF))
    saved, attended = [], []
    for s in range(seqs):
        piece = diagonals[s].reshape(block_len, width)
        if s == 1:
            info, cot_rows = lax.optimization_barrier((info, cot_rows))
        *outs, probs, q, k, v, rows, sums, inverse = attention_forward(
            info, normed, px, py, piece, s, own_weights, base
        )
        saved.append((probs, q, k, v, rows, sums, inverse))
        attended += [outs[0]] + [swap(outs[step], step) for step in range(1, ways)]
    attended, cot_rows = lax.optimization_barrier((attended, cot_rows))
    cot_all = [swap(cot_rows, 1), swap(cot_rows, 2)]
    gain_row = gain_two[None]
    residual, sent, attended_cols = middle_forward(
        info, attended, tokens.reshape(total_rows, width), w_output, gain_row, placing
    )

    rows = exchange(sent)
    row_all = [swap(rows, 1), swap(rows, 2)]
    router = jnp.pad(w_router, ((0, 0), (0, LANES - experts)))
    counts = (2 * capacity,) * chips if paired else (experts * capacity,)
    grad_back, *weighted_out, router_rows = expert_pass(
        info, experts, [rows], [cot_rows], counts, router, w_in[0], w_out[0]
    )
    grad_back, row_all, cot_all = lax.optimization_barrier((grad_back, row_all, cot_all))
    cot_far, row_far = swap(cot_all[0], 2), swap(row_all[1], 1)
    grad_back = exchange(grad_back)
    grads_of = lambda row_parts, cot_parts, prior: expert_grads(
        info, experts, row_parts, cot_parts, router, w_in[0], w_out[0], prior
    )
    expert_sums = grads_of([rows, *row_all], [cot_rows, *cot_all], ())
    grad_back, cot_far, row_far, expert_sums = lax.optimization_barrier(
        (grad_back, cot_far, row_far, expert_sums)
    )

    grad_x_one, grad_output, gain_two_row, *grad_pieces = turn_back(
        info,
        [grad_back],
        (experts * capacity,),
        placing_back,
        residual,
        gain_row,
        cotangent_rows,
        present[:, None],
        w_output,
        attended_cols,
        seqs,
    )
    grad_pieces = [grad_pieces[0]] + [swap(grad_pieces[k], k) for k in range(1, ways)]
    add = lambda *terms: sum(term.astype(F32) for term in terms)
    grad_output = lax.all_to_all(
        grad_output.reshape(ways, group, width), "seq", split_axis=0, concat_axis=0, tiled=True
    )
    weighted_out, _ = lax.optimization_barrier((weighted_out, grad_x_one))
    if paired:
        returned = [weighted_out[0]] + [trade(weighted_out[k], 2 * k) for k in range(1, chips)]
    else:
        returned = exchange(weighted_out[0])

    head_dim = group // heads_here

    def tail(*pieces):
        return tail_pass(
            info,
            pieces,
            (group,),
            (w_query, w_key, w_value),
            tokens.reshape(total_rows, width),
            gain_one[None],
            grad_x_one,
            seqs,
        )

    *outs, kept_half, sent_half = attention_backward(
        info,
        grad_pieces,
        saved,
        own_weights,
        lookup,
        gain_one[None],
        gain_two_row,
        router_rows,
        experts,
    )
    kept_half, sent_half, returned, grad_output = lax.optimization_barrier(
        (kept_half, sent_half, returned, grad_output)
    )
    kept_more, sent_more = gather_sum(info, grad_output, returned if paired else [])
    sent_half, kept_more, sent_more = lax.optimization_barrier((sent_half, kept_more, sent_more))
    total = 2 * kept_half.shape[0]
    if paired:
        other = trade(sent_more, 1)
        spots = split_sum(info, kept_half, trade(sent_half, 1), kept_more, other, chips)
        spot = add(spots[0], *[trade(spots[k], 2 * k) for k in range(1, chips)]).astype(BF)
        row_far, out_x, out_y, *spots = lax.optimization_barrier(
            (row_far, outs[1], outs[2], *spots)
        )
        col_x, col_y = swap(out_x, 1), swap(out_y, 2)
        expert_sums = grads_of([row_far], [cot_far], expert_sums)
        spot, col_x, col_y, far_out, *expert_sums = lax.optimization_barrier(
            (spot, col_x, col_y, outs[3], *expert_sums)
        )
        col_far = swap(far_out, 3)
        near = jnp.concatenate([spot] + [trade(spot, 2 * k) for k in range(1, chips)], axis=0)
        near, col_far, other = lax.optimization_barrier((near, col_far, other))
        mixed = mix_rows(info, returned, other, placing_back, residual, present[:, None])
        grad_tokens = tail(outs[0], col_x, col_y, col_far)
        part = near.shape[0] // 2
        px, py = swap(near, 1), swap(near, 2)
        px, py, near, grad_tokens, mixed = lax.optimization_barrier(
            (px, py, near, grad_tokens, mixed)
        )
        pieces = [near, px, py, swap(px[:part], 2), swap(py[part:], 1)]
        pieces = pieces + [trade(piece, 1) for piece in pieces]
        *summed, grad_output, small, rel = final_pass(
            info, pieces, spot.shape[0], head_dim, total, width
        )
    else:
        picked = matmul_f32(placing_back, returned)
        mixed = (present[:, None] * (residual + picked)).astype(BF)
        expert_sums = grads_of([row_far], [cot_far], expert_sums)
        grad_tokens = tail(outs[0], *[swap(outs[k], k) for k in range(1, ways)])
        more = [jnp.where(core == side, kept_more, sent_more) for side in range(2)]
        more = lax.psum(jnp.concatenate(more, axis=0), "exp")
        grad_output = lax.all_gather(more, "seq", tiled=True).astype(F32)
        halves = [
            jnp.where(core == side, kept_half, sent_half) for side in range(2)
        ]
        packed = lax.psum(jnp.concatenate(halves, axis=0), "exp")
        packed = lax.all_gather(packed, "seq").astype(F32)
        small, rel = jnp.sum(packed[:, 3 * group :], axis=0), packed[:, 3 * group + 2]
        dense = packed[:, : 3 * group].reshape(ways, heads_here, 3, head_dim, width)
        summed = [dense[:, :, kind].reshape(width, width).T for kind in range(3)]
    grad_gain_one, grad_gain_two, grad_router = small[0], small[1], small[3 : 3 + experts].T
    grad_rel = rel[:, : heads_here * buckets].reshape(heads, buckets).T
    return (
        mixed.reshape(seqs, block_len, width),
        grad_tokens.reshape(seqs, block_len, width),
        grad_gain_one,
        summed[0],
        summed[1],
        summed[2],
        grad_output,
        grad_rel,
        grad_gain_two,
        grad_router,
        expert_sums[0][None],
        expert_sums[1][None],
    )


def solution(mesh):
    in_specs = (
        P("exp", "seq", None),
        P("exp"),
        P("exp", "seq", None),
        P(),
        P(),
        P(),
        P(),
        P(),
        P(),
        P(),
        P(),
        P(),
        P("exp", None, None),
        P("exp", None, None),
        P("exp", "seq", None),
    )
    out_specs = (
        P("exp", "seq", None),
        P("exp", "seq", None),
        P(),
        P(),
        P(),
        P(),
        P(),
        P(),
        P(),
        P(),
        P("exp", None, "seq"),
        P("exp", "seq", None),
    )
    return jax.shard_map(
        on_device, mesh=mesh, in_specs=in_specs, out_specs=out_specs, check_vma=False
    )
```

```python
import functools

import jax
import jax.numpy as jnp
from jax import lax
from jax.experimental import pallas as pl
from jax.experimental.pallas import tpu as pltpu
from jax.sharding import PartitionSpec as P

EPS = 1e-06
NEG = -1e30
HIGH_PRECISION = lax.Precision.HIGHEST
LANES = 128
VMEM_BYTES = 60 * 1024 * 1024
SMALL_BYTES = 24 * 1024 * 1024
BF = jnp.bfloat16
F32 = jnp.float32


def matmul_f32(left, right):
    return jnp.dot(left, right, preferred_element_type=F32)


def dot_dims(left, right, left_dim, right_dim):
    return lax.dot_general(
        left, right, (((left_dim,), (right_dim,)), ((), ())), preferred_element_type=F32
    )


def rms_norm(values_in, gain):
    return (
        values_in * lax.rsqrt(jnp.mean(values_in * values_in, axis=-1, keepdims=True) + EPS) * gain
    )


def swap(value, bit):
    ways = lax.axis_size("seq")
    return lax.ppermute(value, "seq", [(i, i ^ bit) for i in range(ways)])


def trade(value, bits):
    peers = lax.axis_size("exp")
    return lax.ppermute(value, "exp", [(i, i ^ bits) for i in range(peers)])


def multi(start, step):
    return pl.multiple_of(start, step)


def norm_kernel(token_ref, gain_ref, out_ref):
    out_ref[...] = rms_norm(token_ref[...].astype(F32), gain_ref[...]).astype(BF)


def norm_rows(tokens, gain):
    seqs, block_len, width = tokens.shape
    block = pl.BlockSpec((1, block_len, width), lambda s: (s, 0, 0))
    return pl.pallas_call(
        norm_kernel,
        grid=(seqs,),
        in_specs=[block, pl.BlockSpec((1, 1, width), lambda s: (0, 0, 0))],
        out_specs=block,
        out_shape=jax.ShapeDtypeStruct(tokens.shape, BF),
        compiler_params=pltpu.CompilerParams(vmem_limit_bytes=SMALL_BYTES),
        name="norm_rows",
    )(tokens, gain)


def prep_kernel(group, info_ref, *refs):
    windows, row_ref = refs[:6], refs[6]
    weight_ref, base_ref, turned = refs[7:]
    offset = (info_ref[0] * group) % LANES
    for kind in range(3):
        left, right = windows[2 * kind][...], windows[2 * kind + 1][...]
        turned[...] = jnp.concatenate([left, right], axis=1).T
        weight_ref[kind] = turned[pl.ds(multi(offset, LANES // 2), group), :]
    for head in range(base_ref.shape[0]):
        row = row_ref[head]
        wide = jnp.broadcast_to(row, (LANES, row.shape[1]))
        base_ref[head] = pltpu.roll(wide, 0, 1, stride=1, stride_axis=0)


def prepare(info, weights, bias_rows, group):
    heads_here, _, wide = bias_rows.shape
    width = weights[0].shape[0]
    whole = lambda *shape: pl.BlockSpec(shape, lambda i, _: (0,) * len(shape))
    window = lambda side: pl.BlockSpec(
        (width, LANES), lambda i, info: (0, info[0] * group // LANES + side)
    )
    return pl.pallas_call(
        functools.partial(prep_kernel, group),
        grid_spec=pltpu.PrefetchScalarGridSpec(
            num_scalar_prefetch=1,
            grid=(1,),
            in_specs=[window(0), window(1)] * 3 + [whole(heads_here, 1, wide)],
            out_specs=(whole(3, group, width), whole(heads_here, LANES, wide)),
            scratch_shapes=[pltpu.VMEM((2 * LANES, width), BF)],
        ),
        out_shape=(
            jax.ShapeDtypeStruct((3, group, width), BF),
            jax.ShapeDtypeStruct((heads_here, LANES, wide), F32),
        ),
        compiler_params=pltpu.CompilerParams(vmem_limit_bytes=VMEM_BYTES),
        name="prepare",
    )(info, *[weight for weight in weights for _ in range(2)], bias_rows)


def forward_kernel(heads_here, head_dim, scale, seq_id, info_ref, *refs):
    own_ref, px_ref, py_ref, pd_ref, weight_ref, base_ref = refs[:6]
    outs = refs[6:10]
    probs_ref, q_ref, k_ref, v_ref, rows_ref, sum_ref, inverse_ref = refs[10:17]
    key_rows, value_cols, query_cols, mask_col, out_cols = refs[17:]
    me, length = info_ref[0], info_ref[4 + seq_id]
    head = pl.program_id(0)
    span = rows_ref.shape[0]
    block_len = own_ref.shape[0]
    group = heads_here * head_dim
    tiles = span // LANES
    width = weight_ref.shape[2]

    @pl.when(head == 0)
    def _():
        for step, piece in enumerate((own_ref, px_ref, py_ref, pd_ref)):
            start = multi((me ^ step) * block_len, block_len)
            rows_ref[pl.ds(start, block_len), :] = piece[...]
        rows = rows_ref[...]
        weights = weight_ref[...].reshape(3 * group, width)
        cols = dot_dims(weights, rows, 1, 1).astype(BF)
        spare = jnp.zeros((key_rows.shape[1] - group, width), BF)
        key_rows[...] = dot_dims(
            rows, jnp.concatenate([weight_ref[1], spare], axis=0), 1, 1
        ).astype(BF)
        v_ref[...] = dot_dims(
            rows, jnp.concatenate([weight_ref[2], spare], axis=0), 1, 1
        ).astype(BF)
        places = lax.broadcasted_iota(jnp.int32, (span, LANES), 0)
        mask_col[...] = jnp.where(places < length, 0.0, NEG)
        ones = (lax.broadcasted_iota(jnp.int32, (16, span), 0) == 0).astype(BF)
        for h in range(heads_here):
            lo, hi = h * head_dim, (h + 1) * head_dim
            q_ref[h] = (cols[lo:hi].astype(F32) * scale).astype(BF)
            k_ref[h] = cols[group + lo : group + hi]
            value_cols[h, :head_dim] = cols[2 * group + lo : 2 * group + hi]
            value_cols[h, head_dim:] = ones

    share = LANES // head_dim
    keys = key_rows[:, pl.ds(multi(head // share * LANES, LANES), LANES)]
    values = value_cols[head]
    query_cols[...] = jnp.zeros_like(query_cols)
    query_cols[pl.ds(multi(head % share * head_dim, head_dim), head_dim), :] = q_ref[head]
    mask = jnp.concatenate([mask_col[...]] * (block_len // LANES), axis=1)
    for c in range(span // block_len):
        cols = slice(c * block_len, (c + 1) * block_len)
        first = c * block_len // LANES + tiles - 1
        bias = jnp.concatenate(
            [
                base_ref[0, :, (first - a) * LANES : (first - a) * LANES + block_len]
                for a in range(tiles)
            ],
            axis=0,
        )
        scores = dot_dims(keys, query_cols[:, cols], 1, 0) + bias + mask
        top = jnp.max(scores, axis=0, keepdims=True)
        probs_ref[0, :, cols] = jnp.exp(scores - top).astype(BF)
    result = dot_dims(values, probs_ref[0], 1, 0)
    inverse = 1.0 / result[head_dim : head_dim + 1]
    inverse_ref[0] = inverse
    result = result[:head_dim] * inverse
    sum_ref[0] = result
    out_cols[...] = result.astype(BF)
    for step, ref in enumerate(outs):
        ref[...] = out_cols[:, pl.ds(multi((me ^ step) * block_len, block_len), block_len)]


def attention_forward(info, own, px, py, diag, seq_id, weights, base):
    _, block_len, width = own.shape
    _, group, _ = weights.shape
    heads_here, _, wide = base.shape
    head_dim = group // heads_here
    span = 4 * block_len
    lanes = -(-group // LANES) * LANES
    piece = pl.BlockSpec((None, block_len, width), lambda h, _: (seq_id, 0, 0))
    full = lambda *shape: pl.BlockSpec(shape, lambda h, _: (0,) * len(shape))
    out_shape = (
        *[jax.ShapeDtypeStruct((group, block_len), BF)] * 4,
        jax.ShapeDtypeStruct((heads_here, span, span), BF),
        jax.ShapeDtypeStruct((heads_here, head_dim, span), BF),
        jax.ShapeDtypeStruct((heads_here, head_dim, span), BF),
        jax.ShapeDtypeStruct((span, lanes), BF),
        jax.ShapeDtypeStruct((span, width), BF),
        jax.ShapeDtypeStruct((heads_here, head_dim, span), F32),
        jax.ShapeDtypeStruct((heads_here, 1, span), F32),
    )
    return pl.pallas_call(
        functools.partial(forward_kernel, heads_here, head_dim, head_dim ** (-0.5), seq_id),
        grid_spec=pltpu.PrefetchScalarGridSpec(
            num_scalar_prefetch=1,
            grid=(heads_here,),
            in_specs=[
                piece,
                piece,
                piece,
                full(block_len, width),
                full(3, group, width),
                pl.BlockSpec((1, LANES, wide), lambda h, _: (h, 0, 0)),
            ],
            out_specs=(
                *[pl.BlockSpec((head_dim, block_len), lambda h, _: (h, 0))] * 4,
                pl.BlockSpec((1, span, span), lambda h, _: (h, 0, 0)),
                full(heads_here, head_dim, span),
                full(heads_here, head_dim, span),
                full(span, lanes),
                full(span, width),
                pl.BlockSpec((1, head_dim, span), lambda h, _: (h, 0, 0)),
                pl.BlockSpec((1, 1, span), lambda h, _: (h, 0, 0)),
            ),
            scratch_shapes=[
                pltpu.VMEM((span, lanes), BF),
                pltpu.VMEM((heads_here, head_dim + 16, span), BF),
                pltpu.VMEM((LANES, span), BF),
                pltpu.VMEM((span, LANES), F32),
                pltpu.VMEM((head_dim, span), BF),
            ],
        ),
        out_shape=out_shape,
        compiler_params=pltpu.CompilerParams(vmem_limit_bytes=VMEM_BYTES),
        cost_estimate=pl.CostEstimate(
            flops=6 * heads_here * span * span * 256 * 2,
            bytes_accessed=heads_here * span * span * 2,
            transcendentals=heads_here * span * span,
        ),
        name="attention_forward",
    )(info, own, px, py, diag, weights, base)


def middle_kernel(seqs, info_ref, *refs):
    pieces = refs[: 4 * seqs]
    token_ref, output_ref, gain_ref, place_ref = refs[4 * seqs : 4 * seqs + 4]
    sum_ref, sent_ref, cols_ref = refs[4 * seqs + 4 :]
    me = info_ref[0]
    group, block_len = pieces[0].shape
    for s in range(seqs):
        for step in range(4):
            start = multi((me ^ step) * group, 64)
            cols_ref[pl.ds(start, group), s * block_len : (s + 1) * block_len] = pieces[
                4 * s + step
            ][...]
    residual = token_ref[...].astype(F32) + dot_dims(cols_ref[...], output_ref[...], 0, 0)
    sum_ref[...] = residual
    routed = rms_norm(residual, gain_ref[...]).astype(BF)
    sent_ref[...] = matmul_f32(place_ref[...], routed).astype(BF)


def middle_forward(info, pieces, tokens, w_output, gain, placing):
    rows, width = tokens.shape
    slots = placing.shape[0]
    return pl.pallas_call(
        functools.partial(middle_kernel, len(pieces) // 4),
        in_specs=[pl.BlockSpec(memory_space=pltpu.SMEM)]
        + [pl.BlockSpec(memory_space=pltpu.VMEM)] * (len(pieces) + 4),
        out_shape=(
            jax.ShapeDtypeStruct((rows, width), F32),
            jax.ShapeDtypeStruct((slots, width), BF),
            jax.ShapeDtypeStruct((width, rows), BF),
        ),
        compiler_params=pltpu.CompilerParams(vmem_limit_bytes=VMEM_BYTES),
        name="middle_forward",
    )(info, *pieces, tokens, w_output, gain, placing)


def turn_kernel(counts, seqs, info_ref, *refs):
    pieces = refs[: len(counts)]
    back_ref, sum_ref, gain_ref, cot_ref, here_ref, output_ref, attended_ref = refs[
        len(counts) : len(counts) + 7
    ]
    x_ref, grad_out, gain_out, *outs = refs[len(counts) + 7 : len(counts) + 14]
    rows_all, cols = refs[len(counts) + 14 :]
    me = info_ref[0]
    start = 0
    for piece, count in zip(pieces, counts, strict=True):
        rows_all[start : start + count, :] = piece[:count, :]
        start += count
    grads = matmul_f32(back_ref[...], rows_all[...])
    values, gain = sum_ref[...], gain_ref[...]
    root = lax.rsqrt(jnp.mean(values * values, axis=1, keepdims=True) + EPS)
    scaled = values * root
    gain_out[...] = jnp.sum(grads * scaled, axis=0, keepdims=True)
    grads = grads * gain
    inner = jnp.mean(grads * scaled, axis=1, keepdims=True)
    grad_x = cot_ref[...].astype(F32) * here_ref[...] + root * (grads - scaled * inner)
    x_ref[...] = grad_x
    branch = grad_x.astype(BF)
    grad_out[...] = matmul_f32(attended_ref[...], branch).astype(BF)
    cols[...] = dot_dims(output_ref[...], branch, 1, 1).astype(BF)
    _, group, block_len = outs[0].shape
    for step, out in enumerate(outs):
        start = multi((me ^ step) * group, 64)
        for s in range(seqs):
            out[s] = cols[pl.ds(start, group), s * block_len : (s + 1) * block_len]


def turn_back(
    info, pieces, counts, placing_back, residual, gain, cotangent, present, w_output, attended, seqs
):
    rows, width = residual.shape
    out = jax.ShapeDtypeStruct((seqs, width // 4, rows // seqs), BF)
    return pl.pallas_call(
        functools.partial(turn_kernel, counts, seqs),
        in_specs=[pl.BlockSpec(memory_space=pltpu.SMEM)]
        + [pl.BlockSpec(memory_space=pltpu.VMEM)] * (len(pieces) + 7),
        out_shape=(
            jax.ShapeDtypeStruct((rows, width), F32),
            jax.ShapeDtypeStruct((width, width), BF),
            jax.ShapeDtypeStruct((1, width), F32),
            out,
            out,
            out,
            out,
        ),
        scratch_shapes=[
            pltpu.VMEM((sum(counts), width), BF),
            pltpu.VMEM((width, rows), BF),
        ],
        compiler_params=pltpu.CompilerParams(vmem_limit_bytes=VMEM_BYTES),
        name="turn_back",
    )(info, *pieces, placing_back, residual, gain, cotangent, present, w_output, attended)


def backward_kernel(seqs, scale, experts, info_ref, *refs):
    pieces = refs[:4]
    groups = refs[4 : 4 + 7 * seqs]
    own_ref, lookup_ref, gain_ref, gain_two_ref, router_ref = refs[4 + 7 * seqs : 9 + 7 * seqs]
    outs = refs[9 + 7 * seqs : 13 + 7 * seqs]
    kept_ref, sent_ref, grad_cols, rel_sum, out_cols, weight_sum, packed, gain_sum, folds = refs[
        13 + 7 * seqs : 22 + 7 * seqs
    ]
    wide_cols, scores_all = refs[22 + 7 * seqs :]
    head, heads = pl.program_id(0), pl.num_programs(0)
    me = info_ref[0]
    head_dim, span = grad_cols.shape
    block_len = span // 4
    tiles = span // LANES
    rel_sum[...] = jnp.zeros_like(rel_sum)
    share = LANES // head_dim
    half = multi(head % share * head_dim, head_dim)
    wide_cols[...] = jnp.zeros_like(wide_cols)
    for s in range(seqs):
        probs_ref, q_ref, k_ref, v_ref, rows_ref, sum_ref, inverse_ref = groups[7 * s : 7 * s + 7]
        for step, piece in enumerate(pieces):
            start = multi((me ^ step) * block_len, block_len)
            grad_cols[:, pl.ds(start, block_len)] = piece[s]
        grads = (grad_cols[...].astype(F32) * inverse_ref[0]).astype(BF)
        inner = jnp.sum(grads.astype(F32) * sum_ref[0], axis=0, keepdims=True)
        wide_cols[pl.ds(half, head_dim), :] = grads
        values = v_ref[...]
        for c in range(span // block_len):
            cols = slice(c * block_len, (c + 1) * block_len)
            first = c * block_len // LANES + tiles - 1
            grad_probs = dot_dims(values, wide_cols[:, cols], 1, 0)
            grad_scores = probs_ref[0, :, cols].astype(F32) * (grad_probs - inner[:, cols])
            for a in range(tiles):
                spot = slice((first - a) * LANES, (first - a) * LANES + block_len)
                rel_sum[:, spot] += grad_scores[a * LANES : (a + 1) * LANES]
            scores_all[:, cols] = grad_scores.astype(BF)
        low = scores_all[...]
        out_cols[0] = (dot_dims(k_ref[0], low, 1, 0) * scale).astype(BF)
        out_cols[1] = matmul_f32(low, q_ref[0].T).astype(BF).T
        out_cols[2] = matmul_f32(probs_ref[0], grads.T).astype(BF).T
        rows = rows_ref[...]
        for kind in range(3):
            product = matmul_f32(out_cols[kind], rows)
            if s == 0:
                weight_sum[kind] = product
            else:
                weight_sum[kind] += product
        for step, out in enumerate(outs):
            start = multi((me ^ step) * block_len, block_len)
            for kind in range(3):
                out[s, kind] = out_cols[kind, :, pl.ds(start, block_len)]
    fold = rel_sum[...]
    wide = fold.shape[1]
    half = LANES // 2
    while half >= 1:
        fold = fold[:half] + pltpu.roll(fold[half:], wide - half, 1)
        half //= 2
    sums = weight_sum[...]
    for kind in range(3):
        start = multi((3 * head + kind) * head_dim, head_dim)
        packed[pl.ds(start, head_dim), :] = sums[kind].astype(BF)

    @pl.when(head == 0)
    def _():
        gain_sum[...] = jnp.zeros_like(gain_sum)
        folds[...] = jnp.zeros_like(folds)

    gain_sum[...] += jnp.sum(own_ref[...].astype(F32) * sums, axis=(0, 1))[None]
    folds[pl.ds(head, 1), :] = fold

    @pl.when(head == heads - 1)
    def _():
        count = weight_sum.shape[2] // (4 * head_dim)
        buckets, width = lookup_ref.shape[0], packed.shape[1]
        rel = lax.dot_general(
            folds[...],
            lookup_ref[...],
            (((1,), (1,)), ((), ())),
            precision=HIGH_PRECISION,
            preferred_element_type=F32,
        )
        rel_row = jnp.concatenate([rel[h : h + 1] for h in range(count)], axis=1)
        rel_row = jnp.pad(rel_row, ((0, 0), (0, width - count * buckets)))
        small = [gain_sum[...] / gain_ref[...], gain_two_ref[...], rel_row, router_ref[:experts]]
        small = jnp.concatenate(small, axis=0)
        start = 3 * count * head_dim
        spare = packed.shape[0] - start - small.shape[0]
        packed[start:, :] = jnp.pad(small, ((0, spare), (0, 0))).astype(BF)
        half, core = packed.shape[0] // 2, info_ref[2]
        kept_ref[...] = packed[pl.ds(multi(core * half, 16), half), :]
        sent_ref[...] = packed[pl.ds(multi((1 - core) * half, 16), half), :]


def attention_backward(
    info, pieces, saved, own_weights, lookup, gain_one, gain_two_row, router_rows, experts
):
    seqs = len(saved)
    heads, head_dim, span = saved[0][1].shape
    width = saved[0][4].shape[1]
    block_len = span // 4
    total = 3 * heads * head_dim + -(-(3 + experts) // 64) * 64
    per_head = lambda *shape: pl.BlockSpec((1,) + shape, lambda h, _: (h,) + (0,) * len(shape))
    whole = lambda *shape: pl.BlockSpec(shape, lambda h, _: (0,) * len(shape))
    group_specs = [
        per_head(span, span),
        per_head(head_dim, span),
        per_head(head_dim, span),
        pl.BlockSpec((span, LANES), lambda h, _: (0, h // (LANES // head_dim))),
        whole(span, width),
        per_head(head_dim, span),
        per_head(1, span),
    ]
    out_spec = pl.BlockSpec((seqs, 3, head_dim, block_len), lambda h, _: (0, 0, h, 0))
    out_type = jax.ShapeDtypeStruct((seqs, 3, heads * head_dim, block_len), BF)
    half_type = jax.ShapeDtypeStruct((total // 2, width), BF)
    return pl.pallas_call(
        functools.partial(backward_kernel, seqs, head_dim ** (-0.5), experts),
        grid_spec=pltpu.PrefetchScalarGridSpec(
            num_scalar_prefetch=1,
            grid=(heads,),
            in_specs=[pl.BlockSpec((seqs, head_dim, block_len), lambda h, _: (0, h, 0))] * 4
            + group_specs * seqs
            + [
                pl.BlockSpec((3, head_dim, width), lambda h, _: (0, h, 0)),
                whole(*lookup.shape),
                whole(1, width),
                whole(1, width),
                whole(*router_rows.shape),
            ],
            out_specs=[out_spec] * 4 + [whole(*half_type.shape)] * 2,
            scratch_shapes=[
                pltpu.VMEM((head_dim, span), BF),
                pltpu.VMEM((LANES, 2 * span), F32),
                pltpu.VMEM((3, head_dim, span), BF),
                pltpu.VMEM((3, head_dim, width), F32),
                pltpu.VMEM((total, width), BF),
                pltpu.VMEM((1, width), F32),
                pltpu.VMEM((8, 2 * span), F32),
                pltpu.VMEM((LANES, span), BF),
                pltpu.VMEM((span, span), BF),
            ],
        ),
        out_shape=[out_type] * 4 + [half_type] * 2,
        compiler_params=pltpu.CompilerParams(vmem_limit_bytes=VMEM_BYTES),
        cost_estimate=pl.CostEstimate(
            flops=8 * seqs * heads * span * span * 256 * 2,
            bytes_accessed=seqs * heads * span * span * 2,
            transcendentals=0,
        ),
        name="attention_backward",
    )(
        info,
        *pieces,
        *[array for group in saved for array in group],
        own_weights,
        lookup,
        gain_one,
        gain_two_row,
        router_rows,
    )


def mix_kernel(info_ref, *refs):
    pieces, (other_ref, back_ref, sum_ref, here_ref, out_ref, rows_all) = refs[:-6], refs[-6:]
    rows = pieces[0].shape[0] // 2
    core, chip = info_ref[2], info_ref[3]
    for k, piece in enumerate(pieces):
        base = (chip ^ k) * 2
        own = piece[pl.ds(multi(core * rows, 16), rows), :]
        rows_all[pl.ds(multi((base + core) * rows, 16), rows), :] = own
        start = other_ref.shape[0] - (len(pieces) - k) * rows
        other = other_ref[start : start + rows, :]
        rows_all[pl.ds(multi((base + 1 - core) * rows, 16), rows), :] = other
    picked = matmul_f32(back_ref[...], rows_all[...])
    out_ref[...] = (here_ref[...] * (sum_ref[...] + picked)).astype(BF)


def mix_rows(info, pieces, other, placing_back, residual, present):
    rows, width = residual.shape
    return pl.pallas_call(
        mix_kernel,
        in_specs=[pl.BlockSpec(memory_space=pltpu.SMEM)]
        + [pl.BlockSpec(memory_space=pltpu.VMEM)] * (len(pieces) + 4),
        out_shape=jax.ShapeDtypeStruct((rows, width), BF),
        scratch_shapes=[pltpu.VMEM((len(pieces) * pieces[0].shape[0], width), BF)],
        compiler_params=pltpu.CompilerParams(vmem_limit_bytes=VMEM_BYTES),
        name="mix_rows",
    )(info, *pieces, other, placing_back, residual, present)


def gather_sum_kernel(info_ref, parts_ref, *refs):
    *pieces, kept_ref, sent_ref, total = refs
    total[...] = jnp.sum(parts_ref[...].astype(F32), axis=0)
    rows, core = kept_ref.shape[0], info_ref[2]
    kept_ref[...] = total[pl.ds(multi(core * rows, 8), rows), :].astype(BF)
    sent_ref[:rows, :] = total[pl.ds(multi((1 - core) * rows, 8), rows), :].astype(BF)
    for piece in pieces:
        count = piece.shape[0] // 2
        sent_ref[rows : rows + count, :] = piece[pl.ds(multi((1 - core) * count, 16), count), :]
        rows += count


def gather_sum(info, parts, pieces):
    _, rows, width = parts.shape
    more = sum(piece.shape[0] // 2 for piece in pieces)
    return pl.pallas_call(
        gather_sum_kernel,
        in_specs=[pl.BlockSpec(memory_space=pltpu.SMEM)]
        + [pl.BlockSpec(memory_space=pltpu.VMEM)] * (1 + len(pieces)),
        out_shape=(
            jax.ShapeDtypeStruct((rows // 2, width), BF),
            jax.ShapeDtypeStruct((rows // 2 + more, width), BF),
        ),
        scratch_shapes=[pltpu.VMEM((rows, width), F32)],
        compiler_params=pltpu.CompilerParams(vmem_limit_bytes=SMALL_BYTES),
        name="gather_sum",
    )(info, parts, *pieces)


def split_kernel(info_ref, kept_ref, other_ref, kept_more_ref, other_more_ref, *refs):
    *outs, half, more = refs
    chip = info_ref[3]
    half[...] = kept_ref[...].astype(F32) + other_ref[...].astype(F32)
    other_more = other_more_ref[: more.shape[0], :]
    more[...] = kept_more_ref[...].astype(F32) + other_more.astype(F32)
    rows, small = half.shape[0] // len(outs), more.shape[0] // len(outs)
    for k, out in enumerate(outs):
        parts = [
            half[pl.ds(multi((chip ^ k) * rows, 8), rows), :],
            more[pl.ds(multi((chip ^ k) * small, 8), small), :],
        ]
        out[...] = jnp.concatenate(parts, axis=0).astype(BF)


def split_sum(info, kept, other, kept_more, other_more, chips):
    rows, width = kept.shape
    small = kept_more.shape[0]
    out = jax.ShapeDtypeStruct(((rows + small) // chips, width), BF)
    return pl.pallas_call(
        split_kernel,
        in_specs=[pl.BlockSpec(memory_space=pltpu.SMEM)]
        + [pl.BlockSpec(memory_space=pltpu.VMEM)] * 4,
        out_shape=(out,) * chips,
        scratch_shapes=[pltpu.VMEM((rows, width), F32), pltpu.VMEM((small, width), F32)],
        compiler_params=pltpu.CompilerParams(vmem_limit_bytes=SMALL_BYTES),
        name="split_sum",
    )(info, kept, other, kept_more, other_more)


def tail_kernel(heads, seqs, info_ref, *refs):
    pieces = refs[: 4 * len(heads)]
    *weights, token_ref, gain_ref, x_ref, out_ref, cols = refs[4 * len(heads) :]
    me = info_ref[0]
    _, width, rows = cols.shape
    block_len, group = rows // seqs, width // 4
    offset = 0
    for part, count in enumerate(heads):
        for step in range(4):
            piece = pieces[4 * part + step]
            start = multi((me ^ step) * group + offset, 64)
            for s in range(seqs):
                for kind in range(3):
                    cols[
                        kind, pl.ds(start, count), s * block_len : (s + 1) * block_len
                    ] = piece[s, kind]
        offset += count
    turned = sum(matmul_f32(weights[kind][...], cols[kind]) for kind in range(3))
    values = token_ref[...].astype(F32)
    root = lax.rsqrt(jnp.mean(values * values, axis=1, keepdims=True) + EPS)
    scaled = values * root
    grads = turned.T * gain_ref[...]
    inner = jnp.mean(grads * scaled, axis=1, keepdims=True)
    out_ref[...] = x_ref[...] + root * (grads - scaled * inner)


def tail_pass(info, pieces, heads, weights, tokens, gain, grad_x, seqs):
    rows, width = tokens.shape
    return pl.pallas_call(
        functools.partial(tail_kernel, heads, seqs),
        in_specs=[pl.BlockSpec(memory_space=pltpu.SMEM)]
        + [pl.BlockSpec(memory_space=pltpu.VMEM)] * (len(pieces) + 6),
        out_shape=jax.ShapeDtypeStruct((rows, width), F32),
        scratch_shapes=[pltpu.VMEM((3, width, rows), BF)],
        compiler_params=pltpu.CompilerParams(vmem_limit_bytes=VMEM_BYTES),
        name="tail_pass",
    )(info, *pieces, *weights, tokens, gain, grad_x)


def gelu_both(pre):
    square = pre * pre
    curve = jnp.tanh(pre * (0.7978845608028654 + 0.035677408136300125 * square))
    half = 0.5 + 0.5 * curve
    slope = half + pre * (0.5 - 0.5 * curve * curve) * (
        0.7978845608028654 + 0.10703222440890037 * square
    )
    return pre * half, slope


def router_prob(rows, router, experts):
    logits = matmul_f32(rows, router)
    lanes = lax.broadcasted_iota(jnp.int32, logits.shape, 1)
    logits = jnp.where(lanes < experts, logits, NEG)
    powers = jnp.exp(logits - jnp.max(logits, axis=1, keepdims=True))
    return powers / jnp.sum(powers, axis=1, keepdims=True), lanes


def expert_kernel(experts, parts, counts, mine_ref, *refs):
    row_refs, grad_refs = refs[:parts], refs[parts : 2 * parts]
    router_ref, first_ref, second_ref = refs[2 * parts : 2 * parts + 3]
    refs = refs[2 * parts + 3 :]
    back_ref, mixed_refs = refs[0], refs[1 : 1 + len(counts)]
    router_grad_ref, rows_all, grads_all, made_all, prob_all, out_sum, back_sum, mixed = refs[
        1 + len(counts) :
    ]
    step, steps = pl.program_id(0), pl.num_programs(0)

    @pl.when(step == 0)
    def _():
        start = 0
        for row_ref, grad_ref in zip(row_refs, grad_refs, strict=True):
            rows_all[start : start + row_ref.shape[0], :] = row_ref[...]
            grads_all[start : start + row_ref.shape[0], :] = grad_ref[...]
            start += row_ref.shape[0]
        prob, lanes = router_prob(rows_all[...], router_ref[...], experts)
        prob_all[...] = prob
        is_mine = lanes == mine_ref[1]
        gate = experts * jnp.sum(jnp.where(is_mine, prob, 0.0), axis=1, keepdims=True)
        made_all[...] = (gate * grads_all[...].astype(F32)).astype(BF)
        out_sum[...] = jnp.zeros_like(out_sum)
        back_sum[...] = jnp.zeros_like(back_sum)

    first, second = first_ref[...], second_ref[...]
    pre = matmul_f32(rows_all[...], first)
    grad_hidden = dot_dims(made_all[...], second, 1, 1)
    hidden, slope = gelu_both(pre)
    out_sum[...] += matmul_f32(hidden.astype(BF), second)
    back_sum[...] += dot_dims((grad_hidden * slope).astype(BF), first, 1, 1)

    @pl.when(step == steps - 1)
    def _():
        prob = prob_all[...]
        is_mine = lax.broadcasted_iota(jnp.int32, prob.shape, 1) == mine_ref[1]
        prob_mine = jnp.sum(jnp.where(is_mine, prob, 0.0), axis=1, keepdims=True)
        expert_out = out_sum[...].astype(BF).astype(F32)
        upper = experts * jnp.sum(grads_all[...].astype(F32) * expert_out, axis=1, keepdims=True)
        inner = prob_mine * upper
        grad_logits = (prob * (jnp.where(is_mine, upper, 0.0) - inner)).astype(BF)
        back = back_sum[...] + dot_dims(grad_logits, router_ref[...], 1, 1)
        back_ref[...] = back.astype(BF)
        mixed[...] = (experts * prob_mine * expert_out).astype(BF)
        if len(counts) == 1:
            mixed_refs[0][...] = mixed[...]
        else:
            for k, (count, ref) in enumerate(zip(counts, mixed_refs, strict=True)):
                start = multi((mine_ref[3] ^ k) * count, 16)
                ref[...] = mixed[pl.ds(start, count), :]
        router_grad_ref[...] = dot_dims(grad_logits, rows_all[...], 0, 0)


def expert_pass(mine, experts, row_parts, grad_parts, counts, router, first, second):
    width, hidden_width = first.shape
    total = sum(counts)
    tile = hidden_width // 3
    whole = lambda *shape: pl.BlockSpec(shape, lambda f, _: (0,) * len(shape))
    part_specs = [whole(*part.shape) for part in row_parts]
    piece_specs = [whole(count, width) for count in counts]
    piece_shapes = [jax.ShapeDtypeStruct((count, width), BF) for count in counts]
    return pl.pallas_call(
        functools.partial(expert_kernel, experts, len(row_parts), counts),
        grid_spec=pltpu.PrefetchScalarGridSpec(
            num_scalar_prefetch=1,
            grid=(hidden_width // tile,),
            in_specs=part_specs * 2
            + [
                whole(width, LANES),
                pl.BlockSpec((width, tile), lambda f, _: (0, f)),
                pl.BlockSpec((tile, width), lambda f, _: (f, 0)),
            ],
            out_specs=[whole(total, width)] + piece_specs + [whole(LANES, width)],
            scratch_shapes=[
                pltpu.VMEM((total, width), BF),
                pltpu.VMEM((total, width), BF),
                pltpu.VMEM((total, width), BF),
                pltpu.VMEM((total, LANES), F32),
                pltpu.VMEM((total, width), F32),
                pltpu.VMEM((total, width), F32),
                pltpu.VMEM((total, width), BF),
            ],
        ),
        out_shape=[jax.ShapeDtypeStruct((total, width), BF)]
        + piece_shapes
        + [jax.ShapeDtypeStruct((LANES, width), F32)],
        compiler_params=pltpu.CompilerParams(vmem_limit_bytes=VMEM_BYTES),
        cost_estimate=pl.CostEstimate(
            flops=8 * total * width * hidden_width,
            bytes_accessed=4 * width * hidden_width,
            transcendentals=total * hidden_width,
        ),
        name="expert_pass",
    )(mine, *row_parts, *grad_parts, router, first, second)


def grads_kernel(experts, parts, prior, info_ref, *refs):
    row_refs, grad_refs = refs[:parts], refs[parts : 2 * parts]
    router_ref, first_ref, second_ref = refs[2 * parts : 2 * parts + 3]
    refs = refs[2 * parts + 3 :]
    if prior:
        (prior_first, prior_second), refs = refs[:2], refs[2:]
    grad_first, grad_second, rows_all, rows_t, made_all, hidden_all, pre_all = refs
    count = row_refs[0].shape[0]

    @pl.when(pl.program_id(0) == 0)
    def _():
        for part in range(parts):
            spot = slice(part * count, (part + 1) * count)
            rows = row_refs[part][...]
            prob, lanes = router_prob(rows, router_ref[...], experts)
            gate = experts * jnp.sum(
                jnp.where(lanes == info_ref[1], prob, 0.0), axis=1, keepdims=True
            )
            made_all[spot, :] = (gate * grad_refs[part][...].astype(F32)).astype(BF)
            rows_all[spot, :] = rows
        rows_t[...] = rows_all[...].T

    first, second = first_ref[...], second_ref[...]
    for part in range(parts):
        spot = slice(part * count, (part + 1) * count)
        pre = matmul_f32(row_refs[part][...], first)
        grad_hidden = dot_dims(made_all[spot, :], second, 1, 1)
        hidden, slope = gelu_both(pre)
        hidden_all[spot, :] = hidden.astype(BF)
        pre_all[spot, :] = (grad_hidden * slope).astype(BF)
    own_first = matmul_f32(rows_t[...], pre_all[...])
    own_second = dot_dims(hidden_all[...], made_all[...], 0, 0)
    if prior:
        own_first = own_first + prior_first[...]
        own_second = own_second + prior_second[...]
    grad_first[...] = own_first
    grad_second[...] = own_second


def expert_grads(info, experts, row_parts, grad_parts, router, first, second, prior):
    width, hidden_width = first.shape
    own = hidden_width // 4
    tile = 256
    tiles = own // tile
    total = sum(part.shape[0] for part in row_parts)
    whole = lambda *shape: pl.BlockSpec(shape, lambda t, _: (0,) * len(shape))
    part_specs = [whole(*part.shape) for part in row_parts]
    out_specs = [
        pl.BlockSpec((width, tile), lambda t, _: (0, t)),
        pl.BlockSpec((tile, width), lambda t, _: (t, 0)),
    ]
    return pl.pallas_call(
        functools.partial(grads_kernel, experts, len(row_parts), len(prior) > 0),
        grid_spec=pltpu.PrefetchScalarGridSpec(
            num_scalar_prefetch=1,
            grid=(tiles,),
            in_specs=part_specs * 2
            + [
                whole(width, LANES),
                pl.BlockSpec((width, tile), lambda t, info: (0, info[0] * tiles + t)),
                pl.BlockSpec((tile, width), lambda t, info: (info[0] * tiles + t, 0)),
            ]
            + out_specs[: len(prior)],
            out_specs=out_specs,
            scratch_shapes=[
                pltpu.VMEM((total, width), BF),
                pltpu.VMEM((width, total), BF),
                pltpu.VMEM((total, width), BF),
                pltpu.VMEM((total, tile), BF),
                pltpu.VMEM((total, tile), BF),
            ],
        ),
        out_shape=(
            jax.ShapeDtypeStruct((width, own), F32),
            jax.ShapeDtypeStruct((own, width), F32),
        ),
        compiler_params=pltpu.CompilerParams(vmem_limit_bytes=VMEM_BYTES),
        cost_estimate=pl.CostEstimate(
            flops=total * width,
            bytes_accessed=total * width // 64,
            transcendentals=0,
        ),
        name="expert_grads",
    )(info, *row_parts, *grad_parts, router, first, second, *prior)


def final_kernel(rows, head_dim, info_ref, *refs):
    pieces = refs[:10]
    query_ref, key_ref, value_ref, output_ref, small_ref, rel_ref, whole = refs[10:]
    me, core, chip = info_ref[0], info_ref[2], info_ref[3]
    each = whole.shape[1] // 8
    step_rows = output_ref.shape[0] // 32
    chips = pieces[0].shape[0] // rows
    for other in range(2):
        for step, first, ref in zip(
            (0, 1, 2, 3, 3), (0, 0, 0, 0, chips // 2), pieces[5 * other : 5 * other + 5], strict=True
        ):
            piece = ref[...].astype(F32)
            for i in range(ref.shape[0] // rows):
                c, z = me ^ step, chip ^ (first + i)
                spot = ((core ^ other) * chips + z) * each
                whole[c, pl.ds(multi(spot, 8), each), :] = piece[i * rows : i * rows + each]
                tail = piece[i * rows + each : (i + 1) * rows]
                spot = ((c * 2 + (core ^ other)) * chips + z) * step_rows
                output_ref[pl.ds(multi(spot, 8), step_rows), :] = tail
    heads = query_ref.shape[0] // (4 * head_dim)
    for kind, ref in enumerate((query_ref, key_ref, value_ref)):
        joined = [
            whole[c, (3 * h + kind) * head_dim : (3 * h + kind + 1) * head_dim, :]
            for c in range(4)
            for h in range(heads)
        ]
        ref[...] = jnp.concatenate(joined, axis=0).T
    small = whole[:, 3 * heads * head_dim :, :]
    small_ref[...] = jnp.sum(small, axis=0)
    rel_ref[...] = small[:, 2, :]


def final_pass(info, pieces, rows, head_dim, total, width):
    square = jax.ShapeDtypeStruct((width, width), F32)
    extra = total - 3 * (width // 4)
    return pl.pallas_call(
        functools.partial(final_kernel, rows, head_dim),
        in_specs=[pl.BlockSpec(memory_space=pltpu.SMEM)]
        + [pl.BlockSpec(memory_space=pltpu.VMEM)] * len(pieces),
        out_shape=(
            square,
            square,
            square,
            square,
            jax.ShapeDtypeStruct((extra, width), F32),
            jax.ShapeDtypeStruct((4, width), F32),
        ),
        scratch_shapes=[pltpu.VMEM((4, total, width), F32)],
        compiler_params=pltpu.CompilerParams(vmem_limit_bytes=2 * SMALL_BYTES),
        name="final_pass",
    )(info, *pieces)


def on_device(
    tokens,
    lengths,
    routes,
    bucket_table,
    gain_one,
    w_query,
    w_key,
    w_value,
    w_output,
    rel_bias,
    gain_two,
    w_router,
    w_in,
    w_out,
    cotangent,
):
    seqs, block_len, width = tokens.shape
    buckets, heads = rel_bias.shape
    experts = w_router.shape[1]
    ways = lax.axis_size("seq")
    me = lax.axis_index("seq")
    mine = lax.axis_index("exp")
    span = block_len * ways
    group = width // ways
    heads_here = heads // ways
    total_rows = seqs * block_len
    capacity = (5 * total_rows + 4 * experts - 1) // (4 * experts)

    peers = lax.axis_size("exp")
    chips = peers // 2
    paired = peers == 8
    core, chip = mine % 2, mine // 2

    normed = norm_rows(tokens, gain_one[None, None])
    px, py = swap(normed, 1), swap(normed, 2)

    positions = me * block_len + jnp.arange(block_len, dtype=jnp.int32)
    present = (positions[None, :] < lengths[:, None]).astype(F32).reshape(total_rows)
    routed = routes.reshape(total_rows)
    chosen = (routed[:, None] == jnp.arange(experts, dtype=jnp.int32)[None, :]).astype(F32)
    live_hits = chosen * present[:, None]
    row_ids = jnp.arange(total_rows, dtype=jnp.int32)
    lower = (row_ids[:, None] >= row_ids[None, :]).astype(BF)
    running = matmul_f32(lower, live_hits.astype(BF))
    slot_index = jnp.sum(live_hits * (running - 1.0), axis=-1)
    kept = present * (slot_index < capacity).astype(F32)
    destin = routed.astype(F32) * capacity + slot_index
    slot_ids = jnp.arange(experts * capacity, dtype=jnp.int32).astype(F32)
    placing = ((destin[None, :] == slot_ids[:, None]) & (kept[None, :] > 0)).astype(BF)
    placing_back = placing.T
    cotangent_rows = cotangent.reshape(total_rows, width)

    def exchange(rows):
        sent = rows.reshape(experts, capacity, width)
        return lax.all_to_all(sent, "exp", split_axis=0, concat_axis=0, tiled=True).reshape(
            experts * capacity, width
        )


    wide = 2 * span
    padded = jnp.concatenate([bucket_table, jnp.full((1,), -1, jnp.int32)])
    turned = jnp.roll(jnp.flip(padded), -LANES)
    lookup = (jnp.arange(buckets, dtype=jnp.int32)[:, None] == turned[None, :]).astype(F32)
    own_bias = lax.dynamic_slice_in_dim(rel_bias, me * heads_here, heads_here, 1)
    bias_rows = jnp.dot(own_bias.T, lookup, precision=HIGH_PRECISION)
    info = jnp.concatenate([jnp.stack([me, mine, core, chip]), lengths])
    own_weights, base = prepare(info, (w_query, w_key, w_value), bias_rows[:, None, :], group)

    held, _ = lax.optimization_barrier((cotangent_rows, own_weights))
    px, py, own_weights, base = lax.optimization_barrier((px, py, own_weights, base))
    diagonals = (swap(px[:1], 2), swap(py[1:], 1))
    cot_rows = exchange(matmul_f32(placing, held).astype(BF))
    saved, attended = [], []
    for s in range(seqs):
        piece = diagonals[s].reshape(block_len, width)
        if s == 1:
            info, cot_rows = lax.optimization_barrier((info, cot_rows))
        *outs, probs, q, k, v, rows, sums, inverse = attention_forward(
            info, normed, px, py, piece, s, own_weights, base
        )
        saved.append((probs, q, k, v, rows, sums, inverse))
        attended += [outs[0]] + [swap(outs[step], step) for step in range(1, ways)]
    attended, cot_rows = lax.optimization_barrier((attended, cot_rows))
    cot_all = [swap(cot_rows, 1), swap(cot_rows, 2)]
    gain_row = gain_two[None]
    residual, sent, attended_cols = middle_forward(
        info, attended, tokens.reshape(total_rows, width), w_output, gain_row, placing
    )

    rows = exchange(sent)
    row_all = [swap(rows, 1), swap(rows, 2)]
    router = jnp.pad(w_router, ((0, 0), (0, LANES - experts)))
    counts = (2 * capacity,) * chips if paired else (experts * capacity,)
    grad_back, *weighted_out, router_rows = expert_pass(
        info, experts, [rows], [cot_rows], counts, router, w_in[0], w_out[0]
    )
    grad_back, row_all, cot_all = lax.optimization_barrier((grad_back, row_all, cot_all))
    cot_far, row_far = swap(cot_all[0], 2), swap(row_all[1], 1)
    grad_back = exchange(grad_back)
    grads_of = lambda row_parts, cot_parts, prior: expert_grads(
        info, experts, row_parts, cot_parts, router, w_in[0], w_out[0], prior
    )
    expert_sums = grads_of([rows, *row_all], [cot_rows, *cot_all], ())
    grad_back, cot_far, row_far, expert_sums = lax.optimization_barrier(
        (grad_back, cot_far, row_far, expert_sums)
    )

    grad_x_one, grad_output, gain_two_row, *grad_pieces = turn_back(
        info,
        [grad_back],
        (experts * capacity,),
        placing_back,
        residual,
        gain_row,
        cotangent_rows,
        present[:, None],
        w_output,
        attended_cols,
        seqs,
    )
    grad_pieces = [grad_pieces[0]] + [swap(grad_pieces[k], k) for k in range(1, ways)]
    add = lambda *terms: sum(term.astype(F32) for term in terms)
    grad_output = lax.all_to_all(
        grad_output.reshape(ways, group, width), "seq", split_axis=0, concat_axis=0, tiled=True
    )
    weighted_out, _ = lax.optimization_barrier((weighted_out, grad_x_one))
    if paired:
        returned = [weighted_out[0]] + [trade(weighted_out[k], 2 * k) for k in range(1, chips)]
    else:
        returned = exchange(weighted_out[0])

    head_dim = group // heads_here

    def tail(*pieces):
        return tail_pass(
            info,
            pieces,
            (group,),
            (w_query, w_key, w_value),
            tokens.reshape(total_rows, width),
            gain_one[None],
            grad_x_one,
            seqs,
        )

    *outs, kept_half, sent_half = attention_backward(
        info,
        grad_pieces,
        saved,
        own_weights,
        lookup,
        gain_one[None],
        gain_two_row,
        router_rows,
        experts,
    )
    kept_half, sent_half, returned, grad_output = lax.optimization_barrier(
        (kept_half, sent_half, returned, grad_output)
    )
    kept_more, sent_more = gather_sum(info, grad_output, returned if paired else [])
    sent_half, kept_more, sent_more = lax.optimization_barrier((sent_half, kept_more, sent_more))
    total = 2 * kept_half.shape[0]
    if paired:
        other = trade(sent_more, 1)
        spots = split_sum(info, kept_half, trade(sent_half, 1), kept_more, other, chips)
        spot = add(spots[0], *[trade(spots[k], 2 * k) for k in range(1, chips)]).astype(BF)
        row_far, out_x, out_y, *spots = lax.optimization_barrier(
            (row_far, outs[1], outs[2], *spots)
        )
        col_x, col_y = swap(out_x, 1), swap(out_y, 2)
        expert_sums = grads_of([row_far], [cot_far], expert_sums)
        spot, col_x, col_y, far_out, *expert_sums = lax.optimization_barrier(
            (spot, col_x, col_y, outs[3], *expert_sums)
        )
        col_far = swap(far_out, 3)
        near = jnp.concatenate([spot] + [trade(spot, 2 * k) for k in range(1, chips)], axis=0)
        near, col_far, other = lax.optimization_barrier((near, col_far, other))
        mixed = mix_rows(info, returned, other, placing_back, residual, present[:, None])
        grad_tokens = tail(outs[0], col_x, col_y, col_far)
        part = near.shape[0] // 2
        px, py = swap(near, 1), swap(near, 2)
        px, py, near, grad_tokens, mixed = lax.optimization_barrier(
            (px, py, near, grad_tokens, mixed)
        )
        pieces = [near, px, py, swap(px[:part], 2), swap(py[part:], 1)]
        pieces = pieces + [trade(piece, 1) for piece in pieces]
        *summed, grad_output, small, rel = final_pass(
            info, pieces, spot.shape[0], head_dim, total, width
        )
    else:
        picked = matmul_f32(placing_back, returned)
        mixed = (present[:, None] * (residual + picked)).astype(BF)
        expert_sums = grads_of([row_far], [cot_far], expert_sums)
        grad_tokens = tail(outs[0], *[swap(outs[k], k) for k in range(1, ways)])
        more = [jnp.where(core == side, kept_more, sent_more) for side in range(2)]
        more = lax.psum(jnp.concatenate(more, axis=0), "exp")
        grad_output = lax.all_gather(more, "seq", tiled=True).astype(F32)
        halves = [
            jnp.where(core == side, kept_half, sent_half) for side in range(2)
        ]
        packed = lax.psum(jnp.concatenate(halves, axis=0), "exp")
        packed = lax.all_gather(packed, "seq").astype(F32)
        small, rel = jnp.sum(packed[:, 3 * group :], axis=0), packed[:, 3 * group + 2]
        dense = packed[:, : 3 * group].reshape(ways, heads_here, 3, head_dim, width)
        summed = [dense[:, :, kind].reshape(width, width).T for kind in range(3)]
    grad_gain_one, grad_gain_two, grad_router = small[0], small[1], small[3 : 3 + experts].T
    grad_rel = rel[:, : heads_here * buckets].reshape(heads, buckets).T
    return (
        mixed.reshape(seqs, block_len, width),
        grad_tokens.reshape(seqs, block_len, width),
        grad_gain_one,
        summed[0],
        summed[1],
        summed[2],
        grad_output,
        grad_rel,
        grad_gain_two,
        grad_router,
        expert_sums[0][None],
        expert_sums[1][None],
    )


def solution(mesh):
    in_specs = (
        P("exp", "seq", None),
        P("exp"),
        P("exp", "seq", None),
        P(),
        P(),
        P(),
        P(),
        P(),
        P(),
        P(),
        P(),
        P(),
        P("exp", None, None),
        P("exp", None, None),
        P("exp", "seq", None),
    )
    out_specs = (
        P("exp", "seq", None),
        P("exp", "seq", None),
        P(),
        P(),
        P(),
        P(),
        P(),
        P(),
        P(),
        P(),
        P("exp", None, "seq"),
        P("exp", "seq", None),
    )
    return jax.shard_map(
        on_device, mesh=mesh, in_specs=in_specs, out_specs=out_specs, check_vma=False
    )
```

```python
import functools

import jax
import jax.numpy as jnp
from jax import lax
from jax.experimental import pallas as pl
from jax.experimental.pallas import tpu as pltpu
from jax.sharding import PartitionSpec as P

EPS = 1e-06
NEG = -1e30
HIGH_PRECISION = lax.Precision.HIGHEST
LANES = 128
VMEM_BYTES = 60 * 1024 * 1024
SMALL_BYTES = 24 * 1024 * 1024
BF = jnp.bfloat16
F32 = jnp.float32


def matmul_f32(left, right):
    return jnp.dot(left, right, preferred_element_type=F32)


def dot_dims(left, right, left_dim, right_dim):
    return lax.dot_general(
        left, right, (((left_dim,), (right_dim,)), ((), ())), preferred_element_type=F32
    )


def rms_norm(values_in, gain):
    return (
        values_in * lax.rsqrt(jnp.mean(values_in * values_in, axis=-1, keepdims=True) + EPS) * gain
    )


def swap(value, bit):
    ways = lax.axis_size("seq")
    return lax.ppermute(value, "seq", [(i, i ^ bit) for i in range(ways)])


def trade(value, bits):
    peers = lax.axis_size("exp")
    return lax.ppermute(value, "exp", [(i, i ^ bits) for i in range(peers)])


def multi(start, step):
    return pl.multiple_of(start, step)


def norm_kernel(token_ref, gain_ref, out_ref):
    out_ref[...] = rms_norm(token_ref[...].astype(F32), gain_ref[...]).astype(BF)


def norm_rows(tokens, gain):
    seqs, block_len, width = tokens.shape
    block = pl.BlockSpec((1, block_len, width), lambda s: (s, 0, 0))
    return pl.pallas_call(
        norm_kernel,
        grid=(seqs,),
        in_specs=[block, pl.BlockSpec((1, 1, width), lambda s: (0, 0, 0))],
        out_specs=block,
        out_shape=jax.ShapeDtypeStruct(tokens.shape, BF),
        compiler_params=pltpu.CompilerParams(vmem_limit_bytes=SMALL_BYTES),
        name="norm_rows",
    )(tokens, gain)


def prep_kernel(group, info_ref, *refs):
    windows, row_ref = refs[:6], refs[6]
    weight_ref, base_ref, turned = refs[7:]
    offset = (info_ref[0] * group) % LANES
    for kind in range(3):
        left, right = windows[2 * kind][...], windows[2 * kind + 1][...]
        turned[...] = jnp.concatenate([left, right], axis=1).T
        weight_ref[kind] = turned[pl.ds(multi(offset, LANES // 2), group), :]
    for head in range(base_ref.shape[0]):
        row = row_ref[head]
        wide = jnp.broadcast_to(row, (LANES, row.shape[1]))
        base_ref[head] = pltpu.roll(wide, 0, 1, stride=1, stride_axis=0)


def prepare(info, weights, bias_rows, group):
    heads_here, _, wide = bias_rows.shape
    width = weights[0].shape[0]
    whole = lambda *shape: pl.BlockSpec(shape, lambda i, _: (0,) * len(shape))
    window = lambda side: pl.BlockSpec(
        (width, LANES), lambda i, info: (0, info[0] * group // LANES + side)
    )
    return pl.pallas_call(
        functools.partial(prep_kernel, group),
        grid_spec=pltpu.PrefetchScalarGridSpec(
            num_scalar_prefetch=1,
            grid=(1,),
            in_specs=[window(0), window(1)] * 3 + [whole(heads_here, 1, wide)],
            out_specs=(whole(3, group, width), whole(heads_here, LANES, wide)),
            scratch_shapes=[pltpu.VMEM((2 * LANES, width), BF)],
        ),
        out_shape=(
            jax.ShapeDtypeStruct((3, group, width), BF),
            jax.ShapeDtypeStruct((heads_here, LANES, wide), F32),
        ),
        compiler_params=pltpu.CompilerParams(vmem_limit_bytes=VMEM_BYTES),
        name="prepare",
    )(info, *[weight for weight in weights for _ in range(2)], bias_rows)


def forward_kernel(heads_here, head_dim, scale, seq_id, info_ref, *refs):
    own_ref, px_ref, py_ref, pd_ref, weight_ref, base_ref = refs[:6]
    outs = refs[6:10]
    probs_ref, q_ref, k_ref, v_ref, rows_ref, sum_ref, inverse_ref = refs[10:17]
    key_rows, value_cols, query_cols, mask_col, out_cols = refs[17:]
    me, length = info_ref[0], info_ref[4 + seq_id]
    head = pl.program_id(0)
    span = rows_ref.shape[0]
    block_len = own_ref.shape[0]
    group = heads_here * head_dim
    tiles = span // LANES
    width = weight_ref.shape[2]

    @pl.when(head == 0)
    def _():
        for step, piece in enumerate((own_ref, px_ref, py_ref, pd_ref)):
            start = multi((me ^ step) * block_len, block_len)
            rows_ref[pl.ds(start, block_len), :] = piece[...]
        rows = rows_ref[...]
        weights = weight_ref[...].reshape(3 * group, width)
        cols = dot_dims(weights, rows, 1, 1).astype(BF)
        spare = jnp.zeros((key_rows.shape[1] - group, width), BF)
        key_rows[...] = dot_dims(
            rows, jnp.concatenate([weight_ref[1], spare], axis=0), 1, 1
        ).astype(BF)
        v_ref[...] = dot_dims(
            rows, jnp.concatenate([weight_ref[2], spare], axis=0), 1, 1
        ).astype(BF)
        places = lax.broadcasted_iota(jnp.int32, (span, LANES), 0)
        mask_col[...] = jnp.where(places < length, 0.0, NEG)
        ones = (lax.broadcasted_iota(jnp.int32, (16, span), 0) == 0).astype(BF)
        for h in range(heads_here):
            lo, hi = h * head_dim, (h + 1) * head_dim
            q_ref[h] = (cols[lo:hi].astype(F32) * scale).astype(BF)
            k_ref[h] = cols[group + lo : group + hi]
            value_cols[h, :head_dim] = cols[2 * group + lo : 2 * group + hi]
            value_cols[h, head_dim:] = ones

    share = LANES // head_dim
    keys = key_rows[:, pl.ds(multi(head // share * LANES, LANES), LANES)]
    values = value_cols[head]
    query_cols[...] = jnp.zeros_like(query_cols)
    query_cols[pl.ds(multi(head % share * head_dim, head_dim), head_dim), :] = q_ref[head]
    mask = jnp.concatenate([mask_col[...]] * (block_len // LANES), axis=1)
    for c in range(span // block_len):
        cols = slice(c * block_len, (c + 1) * block_len)
        first = c * block_len // LANES + tiles - 1
        bias = jnp.concatenate(
            [
                base_ref[0, :, (first - a) * LANES : (first - a) * LANES + block_len]
                for a in range(tiles)
            ],
            axis=0,
        )
        scores = dot_dims(keys, query_cols[:, cols], 1, 0) + bias + mask
        top = jnp.max(scores, axis=0, keepdims=True)
        probs_ref[0, :, cols] = jnp.exp(scores - top).astype(BF)
    result = dot_dims(values, probs_ref[0], 1, 0)
    inverse = 1.0 / result[head_dim : head_dim + 1]
    inverse_ref[0] = inverse
    result = result[:head_dim] * inverse
    sum_ref[0] = result
    out_cols[...] = result.astype(BF)
    for step, ref in enumerate(outs):
        ref[...] = out_cols[:, pl.ds(multi((me ^ step) * block_len, block_len), block_len)]


def attention_forward(info, own, px, py, diag, seq_id, weights, base):
    _, block_len, width = own.shape
    _, group, _ = weights.shape
    heads_here, _, wide = base.shape
    head_dim = group // heads_here
    span = 4 * block_len
    lanes = -(-group // LANES) * LANES
    piece = pl.BlockSpec((None, block_len, width), lambda h, _: (seq_id, 0, 0))
    full = lambda *shape: pl.BlockSpec(shape, lambda h, _: (0,) * len(shape))
    out_shape = (
        *[jax.ShapeDtypeStruct((group, block_len), BF)] * 4,
        jax.ShapeDtypeStruct((heads_here, span, span), BF),
        jax.ShapeDtypeStruct((heads_here, head_dim, span), BF),
        jax.ShapeDtypeStruct((heads_here, head_dim, span), BF),
        jax.ShapeDtypeStruct((span, lanes), BF),
        jax.ShapeDtypeStruct((span, width), BF),
        jax.ShapeDtypeStruct((heads_here, head_dim, span), F32),
        jax.ShapeDtypeStruct((heads_here, 1, span), F32),
    )
    return pl.pallas_call(
        functools.partial(forward_kernel, heads_here, head_dim, head_dim ** (-0.5), seq_id),
        grid_spec=pltpu.PrefetchScalarGridSpec(
            num_scalar_prefetch=1,
            grid=(heads_here,),
            in_specs=[
                piece,
                piece,
                piece,
                full(block_len, width),
                full(3, group, width),
                pl.BlockSpec((1, LANES, wide), lambda h, _: (h, 0, 0)),
            ],
            out_specs=(
                *[pl.BlockSpec((head_dim, block_len), lambda h, _: (h, 0))] * 4,
                pl.BlockSpec((1, span, span), lambda h, _: (h, 0, 0)),
                full(heads_here, head_dim, span),
                full(heads_here, head_dim, span),
                full(span, lanes),
                full(span, width),
                pl.BlockSpec((1, head_dim, span), lambda h, _: (h, 0, 0)),
                pl.BlockSpec((1, 1, span), lambda h, _: (h, 0, 0)),
            ),
            scratch_shapes=[
                pltpu.VMEM((span, lanes), BF),
                pltpu.VMEM((heads_here, head_dim + 16, span), BF),
                pltpu.VMEM((LANES, span), BF),
                pltpu.VMEM((span, LANES), F32),
                pltpu.VMEM((head_dim, span), BF),
            ],
        ),
        out_shape=out_shape,
        compiler_params=pltpu.CompilerParams(vmem_limit_bytes=VMEM_BYTES),
        cost_estimate=pl.CostEstimate(
            flops=6 * heads_here * span * span * 256 * 2,
            bytes_accessed=heads_here * span * span * 2,
            transcendentals=heads_here * span * span,
        ),
        name="attention_forward",
    )(info, own, px, py, diag, weights, base)


def middle_kernel(seqs, info_ref, *refs):
    pieces = refs[: 4 * seqs]
    token_ref, output_ref, gain_ref, place_ref = refs[4 * seqs : 4 * seqs + 4]
    sum_ref, sent_ref, cols_ref = refs[4 * seqs + 4 :]
    me = info_ref[0]
    group, block_len = pieces[0].shape
    for s in range(seqs):
        for step in range(4):
            start = multi((me ^ step) * group, 64)
            cols_ref[pl.ds(start, group), s * block_len : (s + 1) * block_len] = pieces[
                4 * s + step
            ][...]
    residual = token_ref[...].astype(F32) + dot_dims(cols_ref[...], output_ref[...], 0, 0)
    sum_ref[...] = residual
    routed = rms_norm(residual, gain_ref[...]).astype(BF)
    sent_ref[...] = matmul_f32(place_ref[...], routed).astype(BF)


def middle_forward(info, pieces, tokens, w_output, gain, placing):
    rows, width = tokens.shape
    slots = placing.shape[0]
    return pl.pallas_call(
        functools.partial(middle_kernel, len(pieces) // 4),
        in_specs=[pl.BlockSpec(memory_space=pltpu.SMEM)]
        + [pl.BlockSpec(memory_space=pltpu.VMEM)] * (len(pieces) + 4),
        out_shape=(
            jax.ShapeDtypeStruct((rows, width), F32),
            jax.ShapeDtypeStruct((slots, width), BF),
            jax.ShapeDtypeStruct((width, rows), BF),
        ),
        compiler_params=pltpu.CompilerParams(vmem_limit_bytes=VMEM_BYTES),
        name="middle_forward",
    )(info, *pieces, tokens, w_output, gain, placing)


def turn_kernel(counts, seqs, info_ref, *refs):
    pieces = refs[: len(counts)]
    back_ref, sum_ref, gain_ref, cot_ref, here_ref, output_ref, attended_ref = refs[
        len(counts) : len(counts) + 7
    ]
    x_ref, grad_out, gain_out, *outs = refs[len(counts) + 7 : len(counts) + 14]
    rows_all, cols = refs[len(counts) + 14 :]
    me = info_ref[0]
    start = 0
    for piece, count in zip(pieces, counts, strict=True):
        rows_all[start : start + count, :] = piece[:count, :]
        start += count
    grads = matmul_f32(back_ref[...], rows_all[...])
    values, gain = sum_ref[...], gain_ref[...]
    root = lax.rsqrt(jnp.mean(values * values, axis=1, keepdims=True) + EPS)
    scaled = values * root
    gain_out[...] = jnp.sum(grads * scaled, axis=0, keepdims=True)
    grads = grads * gain
    inner = jnp.mean(grads * scaled, axis=1, keepdims=True)
    grad_x = cot_ref[...].astype(F32) * here_ref[...] + root * (grads - scaled * inner)
    x_ref[...] = grad_x
    branch = grad_x.astype(BF)
    grad_out[...] = matmul_f32(attended_ref[...], branch).astype(BF)
    cols[...] = dot_dims(output_ref[...], branch, 1, 1).astype(BF)
    _, group, block_len = outs[0].shape
    for step, out in enumerate(outs):
        start = multi((me ^ step) * group, 64)
        for s in range(seqs):
            out[s] = cols[pl.ds(start, group), s * block_len : (s + 1) * block_len]


def turn_back(
    info, pieces, counts, placing_back, residual, gain, cotangent, present, w_output, attended, seqs
):
    rows, width = residual.shape
    out = jax.ShapeDtypeStruct((seqs, width // 4, rows // seqs), BF)
    return pl.pallas_call(
        functools.partial(turn_kernel, counts, seqs),
        in_specs=[pl.BlockSpec(memory_space=pltpu.SMEM)]
        + [pl.BlockSpec(memory_space=pltpu.VMEM)] * (len(pieces) + 7),
        out_shape=(
            jax.ShapeDtypeStruct((rows, width), F32),
            jax.ShapeDtypeStruct((width, width), BF),
            jax.ShapeDtypeStruct((1, width), F32),
            out,
            out,
            out,
            out,
        ),
        scratch_shapes=[
            pltpu.VMEM((sum(counts), width), BF),
            pltpu.VMEM((width, rows), BF),
        ],
        compiler_params=pltpu.CompilerParams(vmem_limit_bytes=VMEM_BYTES),
        name="turn_back",
    )(info, *pieces, placing_back, residual, gain, cotangent, present, w_output, attended)


def backward_kernel(seqs, scale, experts, info_ref, *refs):
    pieces = refs[:4]
    groups = refs[4 : 4 + 7 * seqs]
    own_ref, lookup_ref, gain_ref, gain_two_ref, router_ref = refs[4 + 7 * seqs : 9 + 7 * seqs]
    outs = refs[9 + 7 * seqs : 13 + 7 * seqs]
    kept_ref, sent_ref, grad_cols, rel_sum, out_cols, weight_sum, packed, gain_sum, folds = refs[
        13 + 7 * seqs : 22 + 7 * seqs
    ]
    wide_cols, scores_all = refs[22 + 7 * seqs :]
    head, heads = pl.program_id(0), pl.num_programs(0)
    me = info_ref[0]
    head_dim, span = grad_cols.shape
    block_len = span // 4
    tiles = span // LANES
    rel_sum[...] = jnp.zeros_like(rel_sum)
    share = LANES // head_dim
    half = multi(head % share * head_dim, head_dim)
    wide_cols[...] = jnp.zeros_like(wide_cols)
    for s in range(seqs):
        probs_ref, q_ref, k_ref, v_ref, rows_ref, sum_ref, inverse_ref = groups[7 * s : 7 * s + 7]
        for step, piece in enumerate(pieces):
            start = multi((me ^ step) * block_len, block_len)
            grad_cols[:, pl.ds(start, block_len)] = piece[s]
        grads = (grad_cols[...].astype(F32) * inverse_ref[0]).astype(BF)
        inner = jnp.sum(grads.astype(F32) * sum_ref[0], axis=0, keepdims=True)
        wide_cols[pl.ds(half, head_dim), :] = grads
        values = v_ref[...]
        for c in range(span // block_len):
            cols = slice(c * block_len, (c + 1) * block_len)
            first = c * block_len // LANES + tiles - 1
            grad_probs = dot_dims(values, wide_cols[:, cols], 1, 0)
            grad_scores = probs_ref[0, :, cols].astype(F32) * (grad_probs - inner[:, cols])
            for a in range(tiles):
                spot = slice((first - a) * LANES, (first - a) * LANES + block_len)
                rel_sum[:, spot] += grad_scores[a * LANES : (a + 1) * LANES]
            scores_all[:, cols] = grad_scores.astype(BF)
        low = scores_all[...]
        out_cols[0] = (dot_dims(k_ref[0], low, 1, 0) * scale).astype(BF)
        out_cols[1] = matmul_f32(low, q_ref[0].T).astype(BF).T
        out_cols[2] = matmul_f32(probs_ref[0], grads.T).astype(BF).T
        rows = rows_ref[...]
        for kind in range(3):
            product = matmul_f32(out_cols[kind], rows)
            if s == 0:
                weight_sum[kind] = product
            else:
                weight_sum[kind] += product
        for step, out in enumerate(outs):
            start = multi((me ^ step) * block_len, block_len)
            for kind in range(3):
                out[s, kind] = out_cols[kind, :, pl.ds(start, block_len)]
    fold = rel_sum[...]
    wide = fold.shape[1]
    half = LANES // 2
    while half >= 1:
        fold = fold[:half] + pltpu.roll(fold[half:], wide - half, 1)
        half //= 2
    sums = weight_sum[...]
    for kind in range(3):
        start = multi((3 * head + kind) * head_dim, head_dim)
        packed[pl.ds(start, head_dim), :] = sums[kind].astype(BF)

    @pl.when(head == 0)
    def _():
        gain_sum[...] = jnp.zeros_like(gain_sum)
        folds[...] = jnp.zeros_like(folds)

    gain_sum[...] += jnp.sum(own_ref[...].astype(F32) * sums, axis=(0, 1))[None]
    folds[pl.ds(head, 1), :] = fold

    @pl.when(head == heads - 1)
    def _():
        count = weight_sum.shape[2] // (4 * head_dim)
        buckets, width = lookup_ref.shape[0], packed.shape[1]
        rel = lax.dot_general(
            folds[...],
            lookup_ref[...],
            (((1,), (1,)), ((), ())),
            precision=HIGH_PRECISION,
            preferred_element_type=F32,
        )
        rel_row = jnp.concatenate([rel[h : h + 1] for h in range(count)], axis=1)
        rel_row = jnp.pad(rel_row, ((0, 0), (0, width - count * buckets)))
        small = [gain_sum[...] / gain_ref[...], gain_two_ref[...], rel_row, router_ref[:experts]]
        small = jnp.concatenate(small, axis=0)
        start = 3 * count * head_dim
        spare = packed.shape[0] - start - small.shape[0]
        packed[start:, :] = jnp.pad(small, ((0, spare), (0, 0))).astype(BF)
        half, core = packed.shape[0] // 2, info_ref[2]
        kept_ref[...] = packed[pl.ds(multi(core * half, 16), half), :]
        sent_ref[...] = packed[pl.ds(multi((1 - core) * half, 16), half), :]


def attention_backward(
    info, pieces, saved, own_weights, lookup, gain_one, gain_two_row, router_rows, experts
):
    seqs = len(saved)
    heads, head_dim, span = saved[0][1].shape
    width = saved[0][4].shape[1]
    block_len = span // 4
    total = 3 * heads * head_dim + -(-(3 + experts) // 64) * 64
    per_head = lambda *shape: pl.BlockSpec((1,) + shape, lambda h, _: (h,) + (0,) * len(shape))
    whole = lambda *shape: pl.BlockSpec(shape, lambda h, _: (0,) * len(shape))
    group_specs = [
        per_head(span, span),
        per_head(head_dim, span),
        per_head(head_dim, span),
        pl.BlockSpec((span, LANES), lambda h, _: (0, h // (LANES // head_dim))),
        whole(span, width),
        per_head(head_dim, span),
        per_head(1, span),
    ]
    out_spec = pl.BlockSpec((seqs, 3, head_dim, block_len), lambda h, _: (0, 0, h, 0))
    out_type = jax.ShapeDtypeStruct((seqs, 3, heads * head_dim, block_len), BF)
    half_type = jax.ShapeDtypeStruct((total // 2, width), BF)
    return pl.pallas_call(
        functools.partial(backward_kernel, seqs, head_dim ** (-0.5), experts),
        grid_spec=pltpu.PrefetchScalarGridSpec(
            num_scalar_prefetch=1,
            grid=(heads,),
            in_specs=[pl.BlockSpec((seqs, head_dim, block_len), lambda h, _: (0, h, 0))] * 4
            + group_specs * seqs
            + [
                pl.BlockSpec((3, head_dim, width), lambda h, _: (0, h, 0)),
                whole(*lookup.shape),
                whole(1, width),
                whole(1, width),
                whole(*router_rows.shape),
            ],
            out_specs=[out_spec] * 4 + [whole(*half_type.shape)] * 2,
            scratch_shapes=[
                pltpu.VMEM((head_dim, span), BF),
                pltpu.VMEM((LANES, 2 * span), F32),
                pltpu.VMEM((3, head_dim, span), BF),
                pltpu.VMEM((3, head_dim, width), F32),
                pltpu.VMEM((total, width), BF),
                pltpu.VMEM((1, width), F32),
                pltpu.VMEM((8, 2 * span), F32),
                pltpu.VMEM((LANES, span), BF),
                pltpu.VMEM((span, span), BF),
            ],
        ),
        out_shape=[out_type] * 4 + [half_type] * 2,
        compiler_params=pltpu.CompilerParams(vmem_limit_bytes=VMEM_BYTES),
        cost_estimate=pl.CostEstimate(
            flops=8 * seqs * heads * span * span * 256 * 2,
            bytes_accessed=seqs * heads * span * span * 2,
            transcendentals=0,
        ),
        name="attention_backward",
    )(
        info,
        *pieces,
        *[array for group in saved for array in group],
        own_weights,
        lookup,
        gain_one,
        gain_two_row,
        router_rows,
    )


def mix_kernel(info_ref, *refs):
    pieces, (other_ref, back_ref, sum_ref, here_ref, out_ref, rows_all) = refs[:-6], refs[-6:]
    rows = pieces[0].shape[0] // 2
    core, chip = info_ref[2], info_ref[3]
    for k, piece in enumerate(pieces):
        base = (chip ^ k) * 2
        own = piece[pl.ds(multi(core * rows, 16), rows), :]
        rows_all[pl.ds(multi((base + core) * rows, 16), rows), :] = own
        start = other_ref.shape[0] - (len(pieces) - k) * rows
        other = other_ref[start : start + rows, :]
        rows_all[pl.ds(multi((base + 1 - core) * rows, 16), rows), :] = other
    picked = matmul_f32(back_ref[...], rows_all[...])
    out_ref[...] = (here_ref[...] * (sum_ref[...] + picked)).astype(BF)


def mix_rows(info, pieces, other, placing_back, residual, present):
    rows, width = residual.shape
    return pl.pallas_call(
        mix_kernel,
        in_specs=[pl.BlockSpec(memory_space=pltpu.SMEM)]
        + [pl.BlockSpec(memory_space=pltpu.VMEM)] * (len(pieces) + 4),
        out_shape=jax.ShapeDtypeStruct((rows, width), BF),
        scratch_shapes=[pltpu.VMEM((len(pieces) * pieces[0].shape[0], width), BF)],
        compiler_params=pltpu.CompilerParams(vmem_limit_bytes=VMEM_BYTES),
        name="mix_rows",
    )(info, *pieces, other, placing_back, residual, present)


def gather_sum_kernel(info_ref, parts_ref, *refs):
    *pieces, kept_ref, sent_ref, total = refs
    total[...] = jnp.sum(parts_ref[...].astype(F32), axis=0)
    rows, core = kept_ref.shape[0], info_ref[2]
    kept_ref[...] = total[pl.ds(multi(core * rows, 8), rows), :].astype(BF)
    sent_ref[:rows, :] = total[pl.ds(multi((1 - core) * rows, 8), rows), :].astype(BF)
    for piece in pieces:
        count = piece.shape[0] // 2
        sent_ref[rows : rows + count, :] = piece[pl.ds(multi((1 - core) * count, 16), count), :]
        rows += count


def gather_sum(info, parts, pieces):
    _, rows, width = parts.shape
    more = sum(piece.shape[0] // 2 for piece in pieces)
    return pl.pallas_call(
        gather_sum_kernel,
        in_specs=[pl.BlockSpec(memory_space=pltpu.SMEM)]
        + [pl.BlockSpec(memory_space=pltpu.VMEM)] * (1 + len(pieces)),
        out_shape=(
            jax.ShapeDtypeStruct((rows // 2, width), BF),
            jax.ShapeDtypeStruct((rows // 2 + more, width), BF),
        ),
        scratch_shapes=[pltpu.VMEM((rows, width), F32)],
        compiler_params=pltpu.CompilerParams(vmem_limit_bytes=SMALL_BYTES),
        name="gather_sum",
    )(info, parts, *pieces)


def split_kernel(info_ref, kept_ref, other_ref, kept_more_ref, other_more_ref, *refs):
    *outs, half, more = refs
    chip = info_ref[3]
    half[...] = kept_ref[...].astype(F32) + other_ref[...].astype(F32)
    other_more = other_more_ref[: more.shape[0], :]
    more[...] = kept_more_ref[...].astype(F32) + other_more.astype(F32)
    rows, small = half.shape[0] // len(outs), more.shape[0] // len(outs)
    for k, out in enumerate(outs):
        parts = [
            half[pl.ds(multi((chip ^ k) * rows, 8), rows), :],
            more[pl.ds(multi((chip ^ k) * small, 8), small), :],
        ]
        out[...] = jnp.concatenate(parts, axis=0).astype(BF)


def split_sum(info, kept, other, kept_more, other_more, chips):
    rows, width = kept.shape
    small = kept_more.shape[0]
    out = jax.ShapeDtypeStruct(((rows + small) // chips, width), BF)
    return pl.pallas_call(
        split_kernel,
        in_specs=[pl.BlockSpec(memory_space=pltpu.SMEM)]
        + [pl.BlockSpec(memory_space=pltpu.VMEM)] * 4,
        out_shape=(out,) * chips,
        scratch_shapes=[pltpu.VMEM((rows, width), F32), pltpu.VMEM((small, width), F32)],
        compiler_params=pltpu.CompilerParams(vmem_limit_bytes=SMALL_BYTES),
        name="split_sum",
    )(info, kept, other, kept_more, other_more)


def tail_kernel(heads, seqs, info_ref, *refs):
    pieces = refs[: 4 * len(heads)]
    *weights, token_ref, gain_ref, x_ref, out_ref, cols = refs[4 * len(heads) :]
    me = info_ref[0]
    _, width, rows = cols.shape
    block_len, group = rows // seqs, width // 4
    offset = 0
    for part, count in enumerate(heads):
        for step in range(4):
            piece = pieces[4 * part + step]
            start = multi((me ^ step) * group + offset, 64)
            for s in range(seqs):
                for kind in range(3):
                    cols[
                        kind, pl.ds(start, count), s * block_len : (s + 1) * block_len
                    ] = piece[s, kind]
        offset += count
    turned = sum(matmul_f32(weights[kind][...], cols[kind]) for kind in range(3))
    values = token_ref[...].astype(F32)
    root = lax.rsqrt(jnp.mean(values * values, axis=1, keepdims=True) + EPS)
    scaled = values * root
    grads = turned.T * gain_ref[...]
    inner = jnp.mean(grads * scaled, axis=1, keepdims=True)
    out_ref[...] = x_ref[...] + root * (grads - scaled * inner)


def tail_pass(info, pieces, heads, weights, tokens, gain, grad_x, seqs):
    rows, width = tokens.shape
    return pl.pallas_call(
        functools.partial(tail_kernel, heads, seqs),
        in_specs=[pl.BlockSpec(memory_space=pltpu.SMEM)]
        + [pl.BlockSpec(memory_space=pltpu.VMEM)] * (len(pieces) + 6),
        out_shape=jax.ShapeDtypeStruct((rows, width), F32),
        scratch_shapes=[pltpu.VMEM((3, width, rows), BF)],
        compiler_params=pltpu.CompilerParams(vmem_limit_bytes=VMEM_BYTES),
        name="tail_pass",
    )(info, *pieces, *weights, tokens, gain, grad_x)


def gelu_both(pre):
    square = pre * pre
    curve = jnp.tanh(pre * (0.7978845608028654 + 0.035677408136300125 * square))
    half = 0.5 + 0.5 * curve
    slope = half + pre * (0.5 - 0.5 * curve * curve) * (
        0.7978845608028654 + 0.10703222440890037 * square
    )
    return pre * half, slope


def router_prob(rows, router, experts):
    logits = matmul_f32(rows, router)
    lanes = lax.broadcasted_iota(jnp.int32, logits.shape, 1)
    logits = jnp.where(lanes < experts, logits, NEG)
    powers = jnp.exp(logits - jnp.max(logits, axis=1, keepdims=True))
    return powers / jnp.sum(powers, axis=1, keepdims=True), lanes


def expert_kernel(experts, parts, counts, mine_ref, *refs):
    row_refs, grad_refs = refs[:parts], refs[parts : 2 * parts]
    router_ref, first_ref, second_ref = refs[2 * parts : 2 * parts + 3]
    refs = refs[2 * parts + 3 :]
    back_ref, mixed_refs = refs[0], refs[1 : 1 + len(counts)]
    router_grad_ref, rows_all, grads_all, made_all, prob_all, out_sum, back_sum, mixed = refs[
        1 + len(counts) :
    ]
    step, steps = pl.program_id(0), pl.num_programs(0)

    @pl.when(step == 0)
    def _():
        start = 0
        for row_ref, grad_ref in zip(row_refs, grad_refs, strict=True):
            rows_all[start : start + row_ref.shape[0], :] = row_ref[...]
            grads_all[start : start + row_ref.shape[0], :] = grad_ref[...]
            start += row_ref.shape[0]
        prob, lanes = router_prob(rows_all[...], router_ref[...], experts)
        prob_all[...] = prob
        is_mine = lanes == mine_ref[1]
        gate = experts * jnp.sum(jnp.where(is_mine, prob, 0.0), axis=1, keepdims=True)
        made_all[...] = (gate * grads_all[...].astype(F32)).astype(BF)
        out_sum[...] = jnp.zeros_like(out_sum)
        back_sum[...] = jnp.zeros_like(back_sum)

    first, second = first_ref[...], second_ref[...]
    pre = matmul_f32(rows_all[...], first)
    grad_hidden = dot_dims(made_all[...], second, 1, 1)
    hidden, slope = gelu_both(pre)
    out_sum[...] += matmul_f32(hidden.astype(BF), second)
    back_sum[...] += dot_dims((grad_hidden * slope).astype(BF), first, 1, 1)

    @pl.when(step == steps - 1)
    def _():
        prob = prob_all[...]
        is_mine = lax.broadcasted_iota(jnp.int32, prob.shape, 1) == mine_ref[1]
        prob_mine = jnp.sum(jnp.where(is_mine, prob, 0.0), axis=1, keepdims=True)
        expert_out = out_sum[...].astype(BF).astype(F32)
        upper = experts * jnp.sum(grads_all[...].astype(F32) * expert_out, axis=1, keepdims=True)
        inner = prob_mine * upper
        grad_logits = (prob * (jnp.where(is_mine, upper, 0.0) - inner)).astype(BF)
        back = back_sum[...] + dot_dims(grad_logits, router_ref[...], 1, 1)
        back_ref[...] = back.astype(BF)
        mixed[...] = (experts * prob_mine * expert_out).astype(BF)
        if len(counts) == 1:
            mixed_refs[0][...] = mixed[...]
        else:
            for k, (count, ref) in enumerate(zip(counts, mixed_refs, strict=True)):
                start = multi((mine_ref[3] ^ k) * count, 16)
                ref[...] = mixed[pl.ds(start, count), :]
        router_grad_ref[...] = dot_dims(grad_logits, rows_all[...], 0, 0)


def expert_pass(mine, experts, row_parts, grad_parts, counts, router, first, second):
    width, hidden_width = first.shape
    total = sum(counts)
    tile = hidden_width // 3
    whole = lambda *shape: pl.BlockSpec(shape, lambda f, _: (0,) * len(shape))
    part_specs = [whole(*part.shape) for part in row_parts]
    piece_specs = [whole(count, width) for count in counts]
    piece_shapes = [jax.ShapeDtypeStruct((count, width), BF) for count in counts]
    return pl.pallas_call(
        functools.partial(expert_kernel, experts, len(row_parts), counts),
        grid_spec=pltpu.PrefetchScalarGridSpec(
            num_scalar_prefetch=1,
            grid=(hidden_width // tile,),
            in_specs=part_specs * 2
            + [
                whole(width, LANES),
                pl.BlockSpec((width, tile), lambda f, _: (0, f)),
                pl.BlockSpec((tile, width), lambda f, _: (f, 0)),
            ],
            out_specs=[whole(total, width)] + piece_specs + [whole(LANES, width)],
            scratch_shapes=[
                pltpu.VMEM((total, width), BF),
                pltpu.VMEM((total, width), BF),
                pltpu.VMEM((total, width), BF),
                pltpu.VMEM((total, LANES), F32),
                pltpu.VMEM((total, width), F32),
                pltpu.VMEM((total, width), F32),
                pltpu.VMEM((total, width), BF),
            ],
        ),
        out_shape=[jax.ShapeDtypeStruct((total, width), BF)]
        + piece_shapes
        + [jax.ShapeDtypeStruct((LANES, width), F32)],
        compiler_params=pltpu.CompilerParams(vmem_limit_bytes=VMEM_BYTES),
        cost_estimate=pl.CostEstimate(
            flops=8 * total * width * hidden_width,
            bytes_accessed=4 * width * hidden_width,
            transcendentals=total * hidden_width,
        ),
        name="expert_pass",
    )(mine, *row_parts, *grad_parts, router, first, second)


def grads_kernel(experts, parts, prior, info_ref, *refs):
    row_refs, grad_refs = refs[:parts], refs[parts : 2 * parts]
    router_ref, first_ref, second_ref = refs[2 * parts : 2 * parts + 3]
    refs = refs[2 * parts + 3 :]
    if prior:
        (prior_first, prior_second), refs = refs[:2], refs[2:]
    grad_first, grad_second, rows_all, rows_t, made_all, hidden_all, pre_all = refs
    count = row_refs[0].shape[0]

    @pl.when(pl.program_id(0) == 0)
    def _():
        for part in range(parts):
            spot = slice(part * count, (part + 1) * count)
            rows = row_refs[part][...]
            prob, lanes = router_prob(rows, router_ref[...], experts)
            gate = experts * jnp.sum(
                jnp.where(lanes == info_ref[1], prob, 0.0), axis=1, keepdims=True
            )
            made_all[spot, :] = (gate * grad_refs[part][...].astype(F32)).astype(BF)
            rows_all[spot, :] = rows
        rows_t[...] = rows_all[...].T

    first, second = first_ref[...], second_ref[...]
    for part in range(parts):
        spot = slice(part * count, (part + 1) * count)
        pre = matmul_f32(row_refs[part][...], first)
        grad_hidden = dot_dims(made_all[spot, :], second, 1, 1)
        hidden, slope = gelu_both(pre)
        hidden_all[spot, :] = hidden.astype(BF)
        pre_all[spot, :] = (grad_hidden * slope).astype(BF)
    own_first = matmul_f32(rows_t[...], pre_all[...])
    own_second = dot_dims(hidden_all[...], made_all[...], 0, 0)
    if prior:
        own_first = own_first + prior_first[...]
        own_second = own_second + prior_second[...]
    grad_first[...] = own_first
    grad_second[...] = own_second


def expert_grads(info, experts, row_parts, grad_parts, router, first, second, prior):
    width, hidden_width = first.shape
    own = hidden_width // 4
    tile = 256
    tiles = own // tile
    total = sum(part.shape[0] for part in row_parts)
    whole = lambda *shape: pl.BlockSpec(shape, lambda t, _: (0,) * len(shape))
    part_specs = [whole(*part.shape) for part in row_parts]
    out_specs = [
        pl.BlockSpec((width, tile), lambda t, _: (0, t)),
        pl.BlockSpec((tile, width), lambda t, _: (t, 0)),
    ]
    return pl.pallas_call(
        functools.partial(grads_kernel, experts, len(row_parts), len(prior) > 0),
        grid_spec=pltpu.PrefetchScalarGridSpec(
            num_scalar_prefetch=1,
            grid=(tiles,),
            in_specs=part_specs * 2
            + [
                whole(width, LANES),
                pl.BlockSpec((width, tile), lambda t, info: (0, info[0] * tiles + t)),
                pl.BlockSpec((tile, width), lambda t, info: (info[0] * tiles + t, 0)),
            ]
            + out_specs[: len(prior)],
            out_specs=out_specs,
            scratch_shapes=[
                pltpu.VMEM((total, width), BF),
                pltpu.VMEM((width, total), BF),
                pltpu.VMEM((total, width), BF),
                pltpu.VMEM((total, tile), BF),
                pltpu.VMEM((total, tile), BF),
            ],
        ),
        out_shape=(
            jax.ShapeDtypeStruct((width, own), F32),
            jax.ShapeDtypeStruct((own, width), F32),
        ),
        compiler_params=pltpu.CompilerParams(vmem_limit_bytes=VMEM_BYTES),
        cost_estimate=pl.CostEstimate(
            flops=total * width,
            bytes_accessed=total * width // 64,
            transcendentals=0,
        ),
        name="expert_grads",
    )(info, *row_parts, *grad_parts, router, first, second, *prior)


def final_kernel(rows, head_dim, info_ref, *refs):
    pieces = refs[:10]
    query_ref, key_ref, value_ref, output_ref, small_ref, rel_ref, whole = refs[10:]
    me, core, chip = info_ref[0], info_ref[2], info_ref[3]
    each = whole.shape[1] // 8
    step_rows = output_ref.shape[0] // 32
    chips = pieces[0].shape[0] // rows
    for other in range(2):
        for step, first, ref in zip(
            (0, 1, 2, 3, 3), (0, 0, 0, 0, chips // 2), pieces[5 * other : 5 * other + 5], strict=True
        ):
            piece = ref[...].astype(F32)
            for i in range(ref.shape[0] // rows):
                c, z = me ^ step, chip ^ (first + i)
                spot = ((core ^ other) * chips + z) * each
                whole[c, pl.ds(multi(spot, 8), each), :] = piece[i * rows : i * rows + each]
                tail = piece[i * rows + each : (i + 1) * rows]
                spot = ((c * 2 + (core ^ other)) * chips + z) * step_rows
                output_ref[pl.ds(multi(spot, 8), step_rows), :] = tail
    heads = query_ref.shape[0] // (4 * head_dim)
    for kind, ref in enumerate((query_ref, key_ref, value_ref)):
        joined = [
            whole[c, (3 * h + kind) * head_dim : (3 * h + kind + 1) * head_dim, :]
            for c in range(4)
            for h in range(heads)
        ]
        ref[...] = jnp.concatenate(joined, axis=0).T
    small = whole[:, 3 * heads * head_dim :, :]
    small_ref[...] = jnp.sum(small, axis=0)
    rel_ref[...] = small[:, 2, :]


def final_pass(info, pieces, rows, head_dim, total, width):
    square = jax.ShapeDtypeStruct((width, width), F32)
    extra = total - 3 * (width // 4)
    return pl.pallas_call(
        functools.partial(final_kernel, rows, head_dim),
        in_specs=[pl.BlockSpec(memory_space=pltpu.SMEM)]
        + [pl.BlockSpec(memory_space=pltpu.VMEM)] * len(pieces),
        out_shape=(
            square,
            square,
            square,
            square,
            jax.ShapeDtypeStruct((extra, width), F32),
            jax.ShapeDtypeStruct((4, width), F32),
        ),
        scratch_shapes=[pltpu.VMEM((4, total, width), F32)],
        compiler_params=pltpu.CompilerParams(vmem_limit_bytes=2 * SMALL_BYTES),
        name="final_pass",
    )(info, *pieces)


def on_device(
    tokens,
    lengths,
    routes,
    bucket_table,
    gain_one,
    w_query,
    w_key,
    w_value,
    w_output,
    rel_bias,
    gain_two,
    w_router,
    w_in,
    w_out,
    cotangent,
):
    seqs, block_len, width = tokens.shape
    buckets, heads = rel_bias.shape
    experts = w_router.shape[1]
    ways = lax.axis_size("seq")
    me = lax.axis_index("seq")
    mine = lax.axis_index("exp")
    span = block_len * ways
    group = width // ways
    heads_here = heads // ways
    total_rows = seqs * block_len
    capacity = (5 * total_rows + 4 * experts - 1) // (4 * experts)

    peers = lax.axis_size("exp")
    chips = peers // 2
    paired = peers == 8
    core, chip = mine % 2, mine // 2

    normed = norm_rows(tokens, gain_one[None, None])
    px, py = swap(normed, 1), swap(normed, 2)

    positions = me * block_len + jnp.arange(block_len, dtype=jnp.int32)
    present = (positions[None, :] < lengths[:, None]).astype(F32).reshape(total_rows)
    routed = routes.reshape(total_rows)
    chosen = (routed[:, None] == jnp.arange(experts, dtype=jnp.int32)[None, :]).astype(F32)
    live_hits = chosen * present[:, None]
    row_ids = jnp.arange(total_rows, dtype=jnp.int32)
    lower = (row_ids[:, None] >= row_ids[None, :]).astype(BF)
    running = matmul_f32(lower, live_hits.astype(BF))
    slot_index = jnp.sum(live_hits * (running - 1.0), axis=-1)
    kept = present * (slot_index < capacity).astype(F32)
    destin = routed.astype(F32) * capacity + slot_index
    slot_ids = jnp.arange(experts * capacity, dtype=jnp.int32).astype(F32)
    placing = ((destin[None, :] == slot_ids[:, None]) & (kept[None, :] > 0)).astype(BF)
    placing_back = placing.T
    cotangent_rows = cotangent.reshape(total_rows, width)

    def exchange(rows):
        sent = rows.reshape(experts, capacity, width)
        return lax.all_to_all(sent, "exp", split_axis=0, concat_axis=0, tiled=True).reshape(
            experts * capacity, width
        )


    wide = 2 * span
    padded = jnp.concatenate([bucket_table, jnp.full((1,), -1, jnp.int32)])
    turned = jnp.roll(jnp.flip(padded), -LANES)
    lookup = (jnp.arange(buckets, dtype=jnp.int32)[:, None] == turned[None, :]).astype(F32)
    own_bias = lax.dynamic_slice_in_dim(rel_bias, me * heads_here, heads_here, 1)
    bias_rows = jnp.dot(own_bias.T, lookup, precision=HIGH_PRECISION)
    info = jnp.concatenate([jnp.stack([me, mine, core, chip]), lengths])
    own_weights, base = prepare(info, (w_query, w_key, w_value), bias_rows[:, None, :], group)

    held, _ = lax.optimization_barrier((cotangent_rows, own_weights))
    px, py, own_weights, base = lax.optimization_barrier((px, py, own_weights, base))
    diagonals = (swap(px[:1], 2), swap(py[1:], 1))
    cot_rows = exchange(matmul_f32(placing, held).astype(BF))
    saved, attended = [], []
    for s in range(seqs):
        piece = diagonals[s].reshape(block_len, width)
        if s == 1:
            info, cot_rows = lax.optimization_barrier((info, cot_rows))
        *outs, probs, q, k, v, rows, sums, inverse = attention_forward(
            info, normed, px, py, piece, s, own_weights, base
        )
        saved.append((probs, q, k, v, rows, sums, inverse))
        attended += [outs[0]] + [swap(outs[step], step) for step in range(1, ways)]
    attended, cot_rows = lax.optimization_barrier((attended, cot_rows))
    cot_all = [swap(cot_rows, 1), swap(cot_rows, 2)]
    gain_row = gain_two[None]
    residual, sent, attended_cols = middle_forward(
        info, attended, tokens.reshape(total_rows, width), w_output, gain_row, placing
    )

    rows = exchange(sent)
    row_all = [swap(rows, 1), swap(rows, 2)]
    router = jnp.pad(w_router, ((0, 0), (0, LANES - experts)))
    counts = (2 * capacity,) * chips if paired else (experts * capacity,)
    grad_back, *weighted_out, router_rows = expert_pass(
        info, experts, [rows], [cot_rows], counts, router, w_in[0], w_out[0]
    )
    row_all, cot_all = lax.optimization_barrier((row_all, cot_all))
    cot_far, row_far = swap(cot_all[0], 2), swap(row_all[1], 1)
    grad_back = exchange(grad_back)
    grads_of = lambda row_parts, cot_parts, prior: expert_grads(
        info, experts, row_parts, cot_parts, router, w_in[0], w_out[0], prior
    )
    expert_sums = grads_of([rows, *row_all], [cot_rows, *cot_all], ())
    grad_back, cot_far, row_far, expert_sums = lax.optimization_barrier(
        (grad_back, cot_far, row_far, expert_sums)
    )

    grad_x_one, grad_output, gain_two_row, *grad_pieces = turn_back(
        info,
        [grad_back],
        (experts * capacity,),
        placing_back,
        residual,
        gain_row,
        cotangent_rows,
        present[:, None],
        w_output,
        attended_cols,
        seqs,
    )
    grad_pieces = [grad_pieces[0]] + [swap(grad_pieces[k], k) for k in range(1, ways)]
    add = lambda *terms: sum(term.astype(F32) for term in terms)
    grad_output = lax.all_to_all(
        grad_output.reshape(ways, group, width), "seq", split_axis=0, concat_axis=0, tiled=True
    )
    weighted_out, _ = lax.optimization_barrier((weighted_out, grad_x_one))
    if paired:
        returned = [weighted_out[0]] + [trade(weighted_out[k], 2 * k) for k in range(1, chips)]
    else:
        returned = exchange(weighted_out[0])

    head_dim = group // heads_here

    def tail(*pieces):
        return tail_pass(
            info,
            pieces,
            (group,),
            (w_query, w_key, w_value),
            tokens.reshape(total_rows, width),
            gain_one[None],
            grad_x_one,
            seqs,
        )

    *outs, kept_half, sent_half = attention_backward(
        info,
        grad_pieces,
        saved,
        own_weights,
        lookup,
        gain_one[None],
        gain_two_row,
        router_rows,
        experts,
    )
    kept_half, sent_half, returned, grad_output = lax.optimization_barrier(
        (kept_half, sent_half, returned, grad_output)
    )
    kept_more, sent_more = gather_sum(info, grad_output, returned if paired else [])
    sent_half, kept_more, sent_more = lax.optimization_barrier((sent_half, kept_more, sent_more))
    total = 2 * kept_half.shape[0]
    if paired:
        other = trade(sent_more, 1)
        spots = split_sum(info, kept_half, trade(sent_half, 1), kept_more, other, chips)
        spot = add(spots[0], *[trade(spots[k], 2 * k) for k in range(1, chips)]).astype(BF)
        row_far, out_x, out_y, *spots = lax.optimization_barrier(
            (row_far, outs[1], outs[2], *spots)
        )
        col_x, col_y = swap(out_x, 1), swap(out_y, 2)
        expert_sums = grads_of([row_far], [cot_far], expert_sums)
        spot, col_x, col_y, far_out, *expert_sums = lax.optimization_barrier(
            (spot, col_x, col_y, outs[3], *expert_sums)
        )
        col_far = swap(far_out, 3)
        near = jnp.concatenate([spot] + [trade(spot, 2 * k) for k in range(1, chips)], axis=0)
        near, col_far, other = lax.optimization_barrier((near, col_far, other))
        mixed = mix_rows(info, returned, other, placing_back, residual, present[:, None])
        grad_tokens = tail(outs[0], col_x, col_y, col_far)
        part = near.shape[0] // 2
        px, py = swap(near, 1), swap(near, 2)
        px, py, near, grad_tokens, mixed = lax.optimization_barrier(
            (px, py, near, grad_tokens, mixed)
        )
        pieces = [near, px, py, swap(px[:part], 2), swap(py[part:], 1)]
        pieces = pieces + [trade(piece, 1) for piece in pieces]
        *summed, grad_output, small, rel = final_pass(
            info, pieces, spot.shape[0], head_dim, total, width
        )
    else:
        picked = matmul_f32(placing_back, returned)
        mixed = (present[:, None] * (residual + picked)).astype(BF)
        expert_sums = grads_of([row_far], [cot_far], expert_sums)
        grad_tokens = tail(outs[0], *[swap(outs[k], k) for k in range(1, ways)])
        more = [jnp.where(core == side, kept_more, sent_more) for side in range(2)]
        more = lax.psum(jnp.concatenate(more, axis=0), "exp")
        grad_output = lax.all_gather(more, "seq", tiled=True).astype(F32)
        halves = [
            jnp.where(core == side, kept_half, sent_half) for side in range(2)
        ]
        packed = lax.psum(jnp.concatenate(halves, axis=0), "exp")
        packed = lax.all_gather(packed, "seq").astype(F32)
        small, rel = jnp.sum(packed[:, 3 * group :], axis=0), packed[:, 3 * group + 2]
        dense = packed[:, : 3 * group].reshape(ways, heads_here, 3, head_dim, width)
        summed = [dense[:, :, kind].reshape(width, width).T for kind in range(3)]
    grad_gain_one, grad_gain_two, grad_router = small[0], small[1], small[3 : 3 + experts].T
    grad_rel = rel[:, : heads_here * buckets].reshape(heads, buckets).T
    return (
        mixed.reshape(seqs, block_len, width),
        grad_tokens.reshape(seqs, block_len, width),
        grad_gain_one,
        summed[0],
        summed[1],
        summed[2],
        grad_output,
        grad_rel,
        grad_gain_two,
        grad_router,
        expert_sums[0][None],
        expert_sums[1][None],
    )


def solution(mesh):
    in_specs = (
        P("exp", "seq", None),
        P("exp"),
        P("exp", "seq", None),
        P(),
        P(),
        P(),
        P(),
        P(),
        P(),
        P(),
        P(),
        P(),
        P("exp", None, None),
        P("exp", None, None),
        P("exp", "seq", None),
    )
    out_specs = (
        P("exp", "seq", None),
        P("exp", "seq", None),
        P(),
        P(),
        P(),
        P(),
        P(),
        P(),
        P(),
        P(),
        P("exp", None, "seq"),
        P("exp", "seq", None),
    )
    return jax.shard_map(
        on_device, mesh=mesh, in_specs=in_specs, out_specs=out_specs, check_vma=False
    )
```
